32 devices in a mesh: dp: 4 (over y, x), rows: 2 (over core), cols: 4 (over z).
Axes of the slice: x: 2, y: 2, z: 4, core: 2. Of those that a mesh axis runs over, the one named last changes fastest.
Arguments:
- block_input: bfloat16 [1024, 8, 1536], P('cols', 'dp', 'rows'), may hold values from -6 to 6
- block_cotangent: bfloat16 [1024, 8, 1536], P('cols', 'dp', 'rows'), may hold values from -6 to 6
- w_query: bfloat16 [2, 1536, 1536], P(None, 'rows', 'cols'), may hold values from -0.15625 to 0.15625
- w_key: bfloat16 [2, 1536, 768], P(None, 'rows', 'cols'), may hold values from -0.15625 to 0.15625
- w_value: bfloat16 [2, 1536, 768], P(None, 'rows', 'cols'), may hold values from -0.15625 to 0.15625
- w_out: bfloat16 [2, 1536, 1536], P(None, 'cols', 'rows'), may hold values from -1.25 to 1.25
- w_gate: bfloat16 [2, 1536, 4096], P(None, 'rows', 'cols'), may hold values from -0.15625 to 0.15625
- w_up: bfloat16 [2, 1536, 4096], P(None, 'rows', 'cols'), may hold values from -0.15625 to 0.15625
- w_down: bfloat16 [2, 4096, 1536], P(None, 'cols', 'rows'), may hold values from -0.09375 to 0.09375
- norm_gains: float32 [2, 2, 1536], P(None, None, 'rows'), may hold values from 0.5 to 1.5
Outputs:
- activations: float32 [1024, 8, 1536], P('cols', 'dp', 'rows')
- input_grad: float32 [1024, 8, 1536], P('cols', 'dp', 'rows')
- grad_query: float32 [2, 1536, 1536], P(None, 'rows', 'cols')
- grad_key: float32 [2, 1536, 768], P(None, 'rows', 'cols')
- grad_value: float32 [2, 1536, 768], P(None, 'rows', 'cols')
- grad_out: float32 [2, 1536, 1536], P(None, 'cols', 'rows')
- grad_gate: float32 [2, 1536, 4096], P(None, 'rows', 'cols')
- grad_up: float32 [2, 1536, 4096], P(None, 'rows', 'cols')
- grad_down: float32 [2, 4096, 1536], P(None, 'cols', 'rows')
- grad_gains: float32 [2, 2, 1536], P(None, None, 'rows')
The draws below stay inside these ranges and needn't reach their ends.
All inputs are finite; a program needn't handle non-finite values.
Results may differ from the reference program's by a relative error of at most 0.02.
Values may be sent and summed in bfloat16 or wider, within the bound.
No kernel may reach another device: no remote copies, remote signals or barrier semaphores. Data moves between devices by JAX's collectives and lax.ppermute only.
A program may use at most 256 MiB of HBM per device.

```python
import jax
import jax.numpy as jnp
from jax import lax

D = 1536
HEADS = 16
KV = 8
HEAD = 96
FF = 4096
LEN = 1024
LAYERS = 2
SEQ_DEV = 2
SEQS = 8


def block_levels(rng, shape, pieces, least, high):
    factor_of, own = 1.0, jax.random.fold_in(rng, 6)
    for dim, blocks in pieces:
        steps = jnp.exp(jax.random.uniform(jax.random.fold_in(own, dim), (blocks,), jnp.float32, least / len(pieces), high / len(pieces)))
        factor_of = factor_of * jnp.repeat(steps, shape[dim] // blocks).reshape([-1 if axis == dim else 1 for axis in range(len(shape))])
    return factor_of


def normal_values(stream_key, shape, width, limit, pieces=(), kind=jnp.bfloat16):
    values = width * jax.random.normal(stream_key, shape, jnp.float32)
    if pieces:
        values = values * block_levels(stream_key, shape, pieces, -0.22, 0.18)
    return jnp.clip(values, -limit, limit).astype(kind)


def setup_inputs(seed: int = 0) -> dict:
    arg_keys = jax.random.split(jax.random.key(seed), 11)
    return {
        "block_input": normal_values(arg_keys[0], (LEN, SEQS, D), 1.0, 6.0, ((0, 4), (1, 4), (2, 2))),
        "block_cotangent": normal_values(arg_keys[1], (LEN, SEQS, D), 1.0, 6.0, ((0, 4), (1, 4), (2, 2))),
        "w_query": normal_values(arg_keys[2], (LAYERS, D, HEADS * HEAD), D ** -0.5, 0.15625, ((1, 2), (2, 4))),
        "w_key": normal_values(arg_keys[3], (LAYERS, D, KV * HEAD), D ** -0.5, 0.15625, ((1, 2), (2, 4))),
        "w_value": normal_values(arg_keys[4], (LAYERS, D, KV * HEAD), D ** -0.5, 0.15625, ((1, 2), (2, 4))),
        "w_out": normal_values(arg_keys[5], (LAYERS, HEADS * HEAD, D), (max(HEADS * HEAD * 16 // LEN, 1)) ** -0.5, 1.25, ((1, 4), (2, 2))),
        "w_gate": normal_values(arg_keys[6], (LAYERS, D, FF), D ** -0.5, 0.15625, ((1, 2), (2, 4))),
        "w_up": normal_values(arg_keys[7], (LAYERS, D, FF), D ** -0.5, 0.15625, ((1, 2), (2, 4))),
        "w_down": normal_values(arg_keys[8], (LAYERS, FF, D), FF ** -0.5, 0.09375, ((1, 4), (2, 2))),
        "norm_gains": jnp.clip(1.0 + 0.1 * jax.random.normal(arg_keys[9], (LAYERS, 2, D), jnp.float32), 0.5, 1.5),
    }


EPSILON = 1e-05
ROPE_BASE = 100000.0
NEGATIVE = -1e+30
HIGHEST = lax.Precision.HIGHEST

@jax.custom_vjp
def low(v):
    return lax.optimization_barrier(v.astype(jnp.bfloat16)).astype(jnp.float32)

@jax.custom_vjp
def low_back(v):
    return v

def low_keep(v):
    return (low(v), None)

def low_pass(kept, grad):
    return (grad,)

def back_keep(v):
    return (v, None)

def back_low(kept, grad):
    return (low(grad),)
low.defvjp(low_keep, low_pass)
low_back.defvjp(back_keep, back_low)

def product(left_side, right_side, pattern):
    return jnp.einsum(pattern, left_side, right_side, precision=HIGHEST)

def rms_norm(hidden_state, gain_row):
    return hidden_state * lax.rsqrt(lax.optimization_barrier(jnp.mean(hidden_state * hidden_state, axis=-1, keepdims=True)) + EPSILON) * gain_row

def rope_tables(positions, head_width):
    indices = jnp.arange(head_width // 2, dtype=jnp.float32)
    inverse = ROPE_BASE ** (-2.0 * indices / head_width)
    angles = positions.astype(jnp.float32)[:, None] * inverse[None, :]
    return (jnp.cos(angles)[:, None, None, :], jnp.sin(angles)[:, None, None, :])

def rotate(vectors, cosine, sine):
    half_width = vectors.shape[-1] // 2
    first_half = vectors[..., :half_width]
    second_half = vectors[..., half_width:]
    return jnp.concatenate([first_half * cosine - second_half * sine, second_half * cosine + first_half * sine], axis=-1)

def attend_block(query_block, key_all, value_all, first_row):
    factor = query_block.shape[-1] ** (-0.5)
    scores = low_back(jnp.einsum('qgcre,kgce->gcrqk', query_block, key_all, precision=HIGHEST) * factor)
    row_pos = first_row + jnp.arange(query_block.shape[0], dtype=jnp.int32)
    key_pos = jnp.arange(key_all.shape[0], dtype=jnp.int32)
    scores = jnp.where(row_pos[:, None] >= key_pos[None, :], scores, NEGATIVE)
    highest = lax.optimization_barrier(jnp.max(scores, axis=-1, keepdims=True))
    exponent = jnp.exp(scores - highest)
    probs = exponent / lax.optimization_barrier(jnp.sum(exponent, axis=-1, keepdims=True))
    return jnp.einsum('gcrqk,kgce->qgcre', low(probs), value_all, precision=HIGHEST)

def layer_forward(hidden_state, wq_layer, wk_layer, wv_layer, wo_layer, wg_layer, wu_layer, wd_layer, gains_pair):
    length, group = (hidden_state.shape[0], hidden_state.shape[1])
    normed_a = low(rms_norm(hidden_state, gains_pair[0]))
    proj_q = low_back(product(normed_a, wq_layer, 'lgd,df->lgf')).reshape(length, group, HEADS, HEAD)
    proj_k = low_back(product(normed_a, wk_layer, 'lgd,df->lgf')).reshape(length, group, KV, HEAD)
    proj_v = low_back(product(normed_a, wv_layer, 'lgd,df->lgf')).reshape(length, group, KV, HEAD)
    cosine, sine = rope_tables(jnp.arange(length, dtype=jnp.int32), HEAD)
    query = low(rotate(proj_q, cosine, sine)).reshape(length, group, KV, HEADS // KV, HEAD)
    key_rot = low(rotate(proj_k, cosine, sine))
    value_low = low(proj_v)
    block_rows = min(512, length)
    block_count = length // block_rows
    query_blocks = query.reshape(block_count, block_rows, group, KV, HEADS // KV, HEAD)
    starts = jnp.arange(block_count, dtype=jnp.int32) * block_rows
    checked = jax.checkpoint(attend_block)
    attended = lax.map(lambda paired: checked(paired[0], key_rot, value_low, paired[1]), (query_blocks, starts))
    attended = low_back(low(attended.reshape(length, group, HEADS * HEAD)))
    mixed_output = hidden_state + low_back(product(attended, wo_layer, 'lgf,fd->lgd'))
    normed_b = low(rms_norm(mixed_output, gains_pair[1]))
    gate = low_back(product(normed_b, wg_layer, 'lgd,df->lgf'))
    up_act = low_back(product(normed_b, wu_layer, 'lgd,df->lgf'))
    inner = low(jax.nn.silu(gate) * up_act)
    return mixed_output + low_back(product(inner, wd_layer, 'lgf,fd->lgd'))

def forward_all(hidden_state, w_query, w_key, w_value, w_out, w_gate, w_up, w_down, norm_gains):
    for layer_idx in range(LAYERS):
        hidden_state = layer_forward(hidden_state, w_query[layer_idx], w_key[layer_idx], w_value[layer_idx], w_out[layer_idx], w_gate[layer_idx], w_up[layer_idx], w_down[layer_idx], norm_gains[layer_idx])
    return hidden_state

def reference(block_input, block_cotangent, w_query, w_key, w_value, w_out, w_gate, w_up, w_down, norm_gains):
    params = tuple((weight_arr.astype(jnp.float32) for weight_arr in (w_query, w_key, w_value, w_out, w_gate, w_up, w_down, norm_gains)))
    group_count = SEQS // SEQ_DEV

    def regroup(stacked_array):
        return jnp.transpose(stacked_array.reshape(LEN, group_count, SEQ_DEV, D), (1, 0, 2, 3))

    def ungroup(stacked_array):
        return jnp.transpose(stacked_array, (1, 0, 2, 3)).reshape(LEN, SEQS, D)

    def one_group(running, group_pair):
        x_group, cot_group = group_pair
        layer_result, pullback = jax.vjp(forward_all, x_group.astype(jnp.float32), *params)
        grads = pullback(cot_group.astype(jnp.float32))
        running = tuple((held_sum + fresh_grad for held_sum, fresh_grad in zip(running, grads[1:])))
        return (running, (layer_result, grads[0]))
    initial = tuple((jnp.zeros_like(weight_arr) for weight_arr in params))
    totals, (outs_grouped, grads_grouped) = lax.scan(one_group, initial, (regroup(block_input), regroup(block_cotangent)))
    return (ungroup(outs_grouped), ungroup(grads_grouped), totals[0], totals[1], totals[2], totals[3], totals[4], totals[5], totals[6], totals[7])
```

```python
import functools

import jax
import jax.numpy as jnp
from jax import lax
from jax.experimental import pallas as pl
from jax.experimental.pallas import tpu as pltpu
from jax.sharding import PartitionSpec as P

HEAD = 96
LAYERS = 2
CHUNKS = 2
EPSILON = 1e-05
ROPE_BASE = 100000.0
NEGATIVE = -1e30
LOW = jnp.bfloat16
FULL = jnp.float32
NT = (((1,), (1,)), ((), ()))
TN = (((0,), (0,)), ((), ()))
ROOM = 56 * 2**20
SCALE = 30


def hop(value, axis, distance):
    size = lax.axis_size(axis)
    return lax.ppermute(value, axis, [(i, i ^ distance) for i in range(size)])


def flip_hi(value):
    return hop(value, "cols", lax.axis_size("cols") // 2)


def flip_core(value):
    return hop(value, "rows", 1)


def low_bits():
    bits, bit = [], 1
    while bit < lax.axis_size("cols") // 2:
        bits.append(bit)
        bit *= 2
    return bits


def group_pair(part):
    bits = low_bits()
    for bit in bits[:-1]:
        part = add_low(part, hop(part, "cols", bit))
    return (part, hop(part, "cols", bits[-1]))


class Order:
    def __init__(self):
        self.last = ()

    def after(self, values):
        return lax.optimization_barrier((values, self.last))[0] if self.last else values

    def mark(self, value):
        self.last = (value,)
        return value

    def join(self, *values):
        self.last = (*self.last, values)


def add_low(left, right):
    return (left.astype(FULL) + right.astype(FULL)).astype(LOW)


def low_dot(left, right):
    return jnp.dot(left, right, preferred_element_type=FULL)


def dot_nt(left, right):
    return lax.dot_general(left, right, NT, preferred_element_type=FULL)


def dot_tn(left, right):
    return lax.dot_general(left, right, TN, preferred_element_type=FULL)


def whole(shape):
    return pl.BlockSpec(shape, lambda *_: (0,) * len(shape))


def far():
    return pl.BlockSpec(memory_space=pl.ANY)


def cost(flops, size, exps=0):
    return pl.CostEstimate(
        flops=int(flops * SCALE), bytes_accessed=int(size * SCALE), transcendentals=0
    )


def limits():
    return pltpu.CompilerParams(vmem_limit_bytes=ROOM)


class Part:
    def __init__(self, array, layer=None, row=0, rows=None, column=0, columns=None):
        self.array, self.layer, self.row, self.column = array, layer, row, column
        self.shape = (rows or array.shape[-2], columns or array.shape[-1])

    def view(self, ref):
        ref = ref if self.layer is None else ref.at[self.layer]
        return ref.at[pl.ds(self.row, self.shape[0]), pl.ds(self.column, self.shape[1])]

    def scratch(self):
        return pltpu.VMEM(self.shape, LOW)


def copies_of(parts, refs, held, sems):
    return [
        pltpu.make_async_copy(part.view(ref), to, sems.at[i])
        for i, (part, ref, to) in enumerate(zip(parts, refs, held))
    ]


def half_dots(left, first, second):
    half = left.shape[1] // 2
    return low_dot(left[:, :half], first) + low_dot(left[:, half:], second)


def turn(value, cosine, sine):
    width = value.shape[1]
    q_width = cosine.shape[1]
    ahead = pltpu.roll(value, width - HEAD // 2, 1)
    behind = pltpu.roll(value, HEAD // 2, 1)
    column = lax.broadcasted_iota(jnp.int32, value.shape, 1)
    other = jnp.where(lax.rem(column, HEAD) < HEAD // 2, ahead, behind)
    is_key = lax.broadcasted_iota(jnp.int32, cosine.shape, 1) < q_width // 2
    query = value[:, :q_width] * cosine + other[:, :q_width] * sine
    rest = value[:, q_width:] * jnp.where(is_key, cosine, 1.0)
    rest = rest + other[:, q_width:] * jnp.where(is_key, sine, 0.0)
    return (query, rest)


def put_norm(refs, outs):
    hidden_ref, left_ref, right_ref, gain_ref = refs
    sum_ref, factor_ref, normed_ref = outs
    hidden = hidden_ref[...].astype(FULL)
    if left_ref is not None:
        hidden = hidden + left_ref[...].astype(FULL) + right_ref[...].astype(FULL)
    factor = lax.rsqrt(jnp.mean(hidden * hidden, axis=-1, keepdims=True) + EPSILON)
    sum_ref[...] = hidden
    factor_ref[...] = factor
    normed_ref[...] = (hidden * factor * gain_ref[...]).astype(LOW)


def put_norm_back(refs, outs):
    grad_ref, left_ref, right_ref, hidden_ref, factor_ref, gain_ref = refs
    sum_ref, low_ref, gain_out_ref = outs
    grad_normed = left_ref[...].astype(FULL) + right_ref[...].astype(FULL)
    factor = factor_ref[...]
    unit = hidden_ref[...] * factor
    grad_unit = grad_normed * gain_ref[...]
    inner = jnp.mean(grad_unit * unit, axis=-1, keepdims=True)
    grad = grad_ref[...] + factor * (grad_unit - unit * inner)
    sum_ref[...] = grad
    low_ref[...] = grad.astype(LOW)
    gain_out_ref[...] = jnp.sum(grad_normed * unit, axis=0, keepdims=True)


def norm_shapes(rows, wide):
    return [((rows, wide), FULL), ((rows, 1), FULL), ((rows, wide), LOW)]


def norm_back_shapes(rows, wide):
    return [((rows, wide), FULL), ((rows, wide), LOW), ((1, wide), FULL)]


def call(kernel, name, operands, parts, outs, scratch, flops, exps=0, scalars=()):
    size = sum(2 * p.shape[0] * p.shape[1] for p in parts) + sum(
        s[0] * s[1] * (4 if k == FULL else 2) for s, k in outs
    )
    return pl.pallas_call(
        kernel,
        grid_spec=pltpu.PrefetchScalarGridSpec(
            num_scalar_prefetch=len(scalars),
            grid=(1,),
            in_specs=[whole(v.shape) for v in operands] + [far()] * len(parts),
            out_specs=[whole(s) for s, _ in outs],
            scratch_shapes=list(scratch)
            + [p.scratch() for p in parts]
            + [pltpu.SemaphoreType.DMA((max(len(parts), 1),))],
        ),
        out_shape=[jax.ShapeDtypeStruct(s, k) for s, k in outs],
        compiler_params=limits(),
        cost_estimate=cost(flops, size, exps),
        name=name,
    )(*scalars, *operands, *[p.array for p in parts])


def take(refs, *counts):
    out, at = [], 0
    for count in counts:
        out.append(refs[at : at + count])
        at += count
    return out + [refs[at:]]


def project_kernel(parts, first, *refs):
    ins, refs = take(refs, 2 if first else 4)
    (cos_ref, sin_ref), hbm, outs, (q_ref, kv_ref), held, (sems,) = take(
        refs, 2, len(parts), 3, 2, len(parts)
    )
    copies = copies_of(parts, hbm, held, sems)
    for copy in copies:
        copy.start()
    put_norm([ins[0], None, None, ins[1]] if first else ins, outs)
    normed_ref = outs[2]
    q_width = cos_ref.shape[1]
    for side in range(2):
        copies[2 * side].wait()
        copies[2 * side + 1].wait()
        projected = half_dots(normed_ref[...], held[2 * side][...], held[2 * side + 1][...])
        query, rest = turn(projected, cos_ref[...], sin_ref[...])
        here = slice(side * q_width, (side + 1) * q_width)
        q_ref[:, here] = query.astype(LOW)
        kv_ref[:, here] = rest.astype(LOW)


def project(hidden, pair, gain, parts, cosine, sine):
    rows, wide = hidden.shape
    both = 2 * cosine.shape[1]
    return call(
        functools.partial(project_kernel, parts, pair is None),
        "project",
        [hidden, *(pair or ()), gain, cosine, sine],
        parts,
        norm_shapes(rows, wide) + [((rows, both), LOW)] * 2,
        [],
        4 * rows * wide * both,
    )


def score(key, query, kind, core):
    raw = dot_nt(key, query) * HEAD ** (-0.5)
    if kind == "own":
        key_pos = lax.broadcasted_iota(jnp.int32, raw.shape, 0)
        query_pos = lax.broadcasted_iota(jnp.int32, raw.shape, 1)
        raw = jnp.where(query_pos >= key_pos, raw, NEGATIVE)
    if kind == "sib":
        raw = jnp.where(core == 1, raw, NEGATIVE)
    return raw


def kinds_of(chunks):
    return ["all"] * (2 * chunks - 2) + ["own", "sib"]


def attend_kernel(chunks, parts, core_ref, q_ref, *refs):
    kv_refs, refs = refs[: 2 * chunks], refs[2 * chunks :]
    count = len(parts)
    hbm, (att_ref, lse_ref, part_ref) = refs[:count], refs[count : count + 3]
    held, sems = refs[count + 3 : -1], refs[-1]
    copies = copies_of(parts, hbm, held, sems)
    for copy in copies:
        copy.start()
    core = core_ref[0]
    q_width = q_ref.shape[1] // 2
    kv_width = q_width // 2
    heads = q_width // HEAD
    for h in range(2 * heads):
        group = (h // heads) * q_width + (h % heads) // 2 * HEAD
        mine = slice(h * HEAD, (h + 1) * HEAD)
        query = q_ref[:, mine]
        scores = [
            score(ref[:, group : group + HEAD], query, kind, core)
            for ref, kind in zip(kv_refs, kinds_of(chunks))
        ]
        highest = functools.reduce(
            jnp.maximum, [jnp.max(s, axis=0, keepdims=True) for s in scores]
        )
        exps = [jnp.exp(s - highest) for s in scores]
        total = sum(jnp.sum(e, axis=0, keepdims=True) for e in exps)
        share = 1.0 / total
        lse_ref[h : h + 1, :] = highest + jnp.log(total)
        spot = slice(group + kv_width, group + kv_width + HEAD)
        att = sum(dot_tn((e * share).astype(LOW), ref[:, spot]) for e, ref in zip(exps, kv_refs))
        att_ref[:, mine] = att.astype(LOW)
    for copy in copies:
        copy.wait()
    wide = part_ref.shape[1]
    for side in range(2):
        columns = slice(side * wide // 2, (side + 1) * wide // 2)
        total = low_dot(att_ref[:, :q_width], held[side][...])
        total = total + low_dot(att_ref[:, q_width:], held[2 + side][...])
        part_ref[:, columns] = total.astype(LOW)


def attend(core, query, kvs, parts):
    rows, both = query.shape
    heads = both // HEAD
    wide = 2 * parts[0].shape[1]
    chunks = len(kvs) // 2
    shapes = [(rows, both), (heads, rows), (rows, wide)]
    operands = [query] + list(kvs)
    return pl.pallas_call(
        functools.partial(attend_kernel, chunks, parts),
        grid_spec=pltpu.PrefetchScalarGridSpec(
            num_scalar_prefetch=1,
            grid=(1,),
            in_specs=[whole(v.shape) for v in operands] + [far()] * len(parts),
            out_specs=[whole(s) for s in shapes],
            scratch_shapes=[p.scratch() for p in parts] + [pltpu.SemaphoreType.DMA((len(parts),))],
        ),
        out_shape=[
            jax.ShapeDtypeStruct(s, FULL if i == 1 else LOW) for i, s in enumerate(shapes)
        ],
        compiler_params=limits(),
        cost_estimate=cost(
            8 * heads * rows * rows * len(kvs) * 128 + 2 * rows * both * wide,
            2 * both * wide + 4 * rows * wide,
            heads * rows * rows * len(kvs),
        ),
        name="attend",
    )(core, *operands, *[p.array for p in parts])


def attend_back_kernel(chunks, has_held, parts, core_ref, *refs):
    ins, (q_ref, lse_ref), refs = take(refs, 6, 2)
    kv_refs, refs = refs[: 2 * chunks], refs[2 * chunks :]
    held_refs, refs = (refs[:2], refs[2:]) if has_held else (None, refs)
    count = len(parts)
    hbm, outs, (dq_ref,), out_refs, (grad_ref,), held, (sems,) = take(
        refs, count, 3, 1, 2 * chunks, 1, count
    )
    copies = copies_of(parts, hbm, held, sems)
    for copy in copies:
        copy.start()
    put_norm_back(ins, outs)
    g_ref = outs[1]
    core = core_ref[0]
    q_width = q_ref.shape[1] // 2
    kv_width = q_width // 2
    heads = q_width // HEAD
    half = g_ref.shape[1] // 2
    scale = HEAD ** (-0.5)
    for copy in copies:
        copy.wait()
    for side in range(2):
        grad = dot_nt(g_ref[:, :half], held[2 * side][...])
        grad = grad + dot_nt(g_ref[:, half:], held[2 * side + 1][...])
        grad_ref[:, side * q_width : (side + 1) * q_width] = grad.astype(LOW)
    for first in range(0, 2 * heads, 2):
        group = (first // heads) * q_width + (first % heads) // 2 * HEAD
        key_spot = slice(group, group + HEAD)
        value_spot = slice(group + kv_width, group + kv_width + HEAD)
        key_sums, value_sums = [0.0] * len(kv_refs), [0.0] * len(kv_refs)
        for h in (first, first + 1):
            mine = slice(h * HEAD, (h + 1) * HEAD)
            query, grad, lse = q_ref[:, mine], grad_ref[:, mine], lse_ref[h : h + 1, :]
            probs = [
                jnp.exp(score(ref[:, key_spot], query, kind, core) - lse)
                for ref, kind in zip(kv_refs, kinds_of(chunks))
            ]
            prob_grads = [dot_nt(ref[:, value_spot], grad) for ref in kv_refs]
            delta = sum(
                jnp.sum(p * d, axis=0, keepdims=True) for p, d in zip(probs, prob_grads)
            )
            query_grad = 0.0
            for i, (p, d, ref) in enumerate(zip(probs, prob_grads, kv_refs)):
                score_grad = (p * (d - delta)).astype(LOW)
                query_grad = query_grad + dot_tn(score_grad, ref[:, key_spot])
                key_sums[i] = key_sums[i] + low_dot(score_grad, query)
                value_sums[i] = value_sums[i] + low_dot(p.astype(LOW), grad)
            dq_ref[:, mine] = query_grad * scale
        for i, out_ref in enumerate(out_refs):
            for spot, value in ((key_spot, key_sums[i] * scale), (value_spot, value_sums[i])):
                if has_held and i >= 2 * chunks - 2:
                    value = value + held_refs[i - 2 * chunks + 2][:, spot]
                out_ref[:, spot] = value.astype(out_ref.dtype)


def attend_back(core, norm_ins, query, lse, kvs, held, parts):
    rows, both = query.shape
    heads = both // HEAD
    wide = norm_ins[0].shape[1]
    chunks = len(kvs) // 2
    return call(
        functools.partial(attend_back_kernel, chunks, held is not None, parts),
        "attend_back",
        [*norm_ins, query, lse, *kvs, *(held or ())],
        parts,
        norm_back_shapes(rows, wide) + [((rows, both), FULL)] * (2 * chunks + 1),
        [pltpu.VMEM((rows, both), LOW)],
        20 * heads * rows * rows * len(kvs) * 128 + 2 * rows * both * wide,
        heads * rows * rows * len(kvs),
        (core,),
    )


def project_back_kernel(parts, dq_ref, own_ref, came_ref, cos_ref, sin_ref, *refs):
    count = len(parts)
    hbm, (proj_ref, part_ref), held, sems = refs[:count], refs[count : count + 2], refs[count + 2 : -1], refs[-1]
    copies = copies_of(parts, hbm, held, sems)
    for copy in copies:
        copy.start()
    q_width = cos_ref.shape[1]
    half = part_ref.shape[1] // 2
    for side in range(2):
        here = slice(side * q_width, (side + 1) * q_width)
        rest = own_ref[:, here] + came_ref[:, here].astype(FULL)
        flat = jnp.concatenate([dq_ref[:, here], rest], axis=1)
        query, rest = turn(flat, cos_ref[...], -sin_ref[...])
        start = 2 * side * q_width
        proj_ref[:, start : start + q_width] = query.astype(LOW)
        proj_ref[:, start + q_width : start + 2 * q_width] = rest.astype(LOW)
    for copy in copies:
        copy.wait()
    for side in range(2):
        total = dot_nt(proj_ref[:, : 2 * q_width], held[side][...])
        total = total + dot_nt(proj_ref[:, 2 * q_width :], held[2 + side][...])
        part_ref[:, side * half : (side + 1) * half] = total.astype(LOW)


def project_back(dq, own, came, cosine, sine, parts):
    rows, both = dq.shape
    wide = 2 * parts[0].shape[0]
    operands = [dq, own, came, cosine, sine]
    shapes = [(rows, 2 * both), (rows, wide)]
    return pl.pallas_call(
        functools.partial(project_back_kernel, parts),
        in_specs=[whole(v.shape) for v in operands] + [far()] * len(parts),
        out_specs=[whole(s) for s in shapes],
        out_shape=[jax.ShapeDtypeStruct(s, LOW) for s in shapes],
        grid=(1,),
        scratch_shapes=[p.scratch() for p in parts] + [pltpu.SemaphoreType.DMA((len(parts),))],
        compiler_params=limits(),
        cost_estimate=cost(4 * rows * wide * both, 4 * wide * both + 12 * rows * both),
        name="project_back",
    )(*operands, *[p.array for p in parts])


def ff_kernel(parts, *refs):
    ins, hbm, outs, (gate_ref, up_ref, inner_ref, part_ref), held, (sems,) = take(
        refs, 4, len(parts), 3, 4, len(parts)
    )
    copies = copies_of(parts, hbm, held, sems)
    for copy in copies:
        copy.start()
    put_norm(ins, outs)
    tokens = outs[2][...]
    ff = gate_ref.shape[1] // 2
    half = part_ref.shape[1] // 2
    for side in range(2):
        for copy in copies[4 * side : 4 * side + 4]:
            copy.wait()
        g1_ref, g2_ref, u1_ref, u2_ref = held[4 * side : 4 * side + 4]
        here = slice(side * ff, (side + 1) * ff)
        gate = half_dots(tokens, g1_ref[...], g2_ref[...])
        up = half_dots(tokens, u1_ref[...], u2_ref[...])
        gate_ref[:, here] = gate.astype(LOW)
        up_ref[:, here] = up.astype(LOW)
        inner_ref[:, here] = (gate * jax.nn.sigmoid(gate) * up).astype(LOW)
    for copy in copies[8:]:
        copy.wait()
    for side in range(2):
        total = low_dot(inner_ref[:, :ff], held[8 + side][...])
        total = total + dot_nt(inner_ref[:, ff:], held[10 + side][...])
        part_ref[:, side * half : (side + 1) * half] = total.astype(LOW)


def feed_forward(hidden, pair, gain, pair_parts, down_parts):
    rows, wide = hidden.shape
    ff = down_parts[0].shape[0]
    parts = pair_parts + down_parts
    return call(
        functools.partial(ff_kernel, parts),
        "feed_forward",
        [hidden, *pair, gain],
        parts,
        norm_shapes(rows, wide) + [((rows, 2 * ff), LOW)] * 3 + [((rows, wide), LOW)],
        [],
        12 * rows * wide * ff,
        2 * rows * ff,
    )


def ff_back_kernel(parts, first, *refs):
    ins, (gate_ref, up_ref), hbm, refs = take(refs, 1 if first else 6, 2, len(parts))
    outs, (grad_ref, part_ref), held, (sems,) = take(refs, 0 if first else 3, 2, len(parts))
    copies = copies_of(parts, hbm, held, sems)
    for copy in copies:
        copy.start()
    if first:
        x_ref = ins[0]
    else:
        put_norm_back(ins, outs)
        x_ref = outs[1]
    half = x_ref.shape[1] // 2
    ff = gate_ref.shape[1] // 2
    for side in range(2):
        for copy in copies[2 * side : 2 * side + 2]:
            copy.wait()
        here = slice(side * ff, (side + 1) * ff)
        times = low_dot if side else dot_nt
        inner_grad = times(x_ref[:, :half], held[2 * side][...])
        inner_grad = inner_grad + times(x_ref[:, half:], held[2 * side + 1][...])
        gate, up = gate_ref[:, here].astype(FULL), up_ref[:, here].astype(FULL)
        sigma = jax.nn.sigmoid(gate)
        start = 2 * side * ff
        grad_ref[:, start : start + ff] = (
            inner_grad * up * sigma * (1.0 + gate * (1.0 - sigma))
        ).astype(LOW)
        grad_ref[:, start + ff : start + 2 * ff] = (inner_grad * gate * sigma).astype(LOW)
    for copy in copies[4:]:
        copy.wait()
    for side in range(2):
        total = 0.0
        for i in range(4):
            grad = grad_ref[:, i * ff : (i + 1) * ff]
            total = total + dot_nt(grad, held[4 + 2 * i + side][...])
        part_ref[:, side * half : (side + 1) * half] = total.astype(LOW)


def feed_back(norm_ins, gate, up, pair_parts, down_parts):
    rows, wide = norm_ins[0].shape
    ff = down_parts[0].shape[0]
    g, u = (0, 1, 4, 5), (2, 3, 6, 7)
    order = [g[0], g[1], u[0], u[1], g[2], g[3], u[2], u[3]]
    parts = down_parts + [pair_parts[i] for i in order]
    first = len(norm_ins) == 1
    return call(
        functools.partial(ff_back_kernel, parts, first),
        "feed_back",
        [*norm_ins, gate, up],
        parts,
        ([] if first else norm_back_shapes(rows, wide))
        + [((rows, 4 * ff), LOW), ((rows, wide), LOW)],
        [],
        12 * rows * wide * ff,
        2 * rows * ff,
    )


def ff_weights_kernel(chunks, split, *refs):
    xb_refs, bb_refs, dg_refs, in_refs = [refs[i * chunks : (i + 1) * chunks] for i in range(4)]
    first_ref, second_ref, turned_ref = refs[4 * chunks :]
    j = pl.program_id(0)
    rows = xb_refs[0].shape[0]
    half = first_ref.shape[0]

    def take(x_refs):
        for i, ref in enumerate(x_refs):
            turned_ref[:, i * rows : (i + 1) * rows] = ref[...].T

    def work(y_refs):
        grads = jnp.concatenate([ref[...] for ref in y_refs], axis=0)
        second_ref[...] = low_dot(turned_ref[half:, :], grads).astype(LOW)
        first_ref[...] = low_dot(turned_ref[:half, :], grads).astype(LOW)

    @pl.when(j == 0)
    def _():
        take(xb_refs)

    @pl.when(j == split)
    def _():
        take(bb_refs)

    @pl.when(j < split)
    def _():
        work(dg_refs)

    @pl.when(j >= split)
    def _():
        work(in_refs)


def ff_weights(all_b, branch_b, grads, inner):
    chunks = len(all_b)
    rows, wide = all_b[0].shape
    ff = inner[0].shape[1] // 2
    step = min(512, ff)
    n = ff // step
    split = 4 * n
    full = whole((rows, wide))
    grad = pl.BlockSpec((rows, step), lambda j: (0, jnp.minimum(j, split - 1)))
    last = pl.BlockSpec((rows, step), lambda j: (0, jnp.maximum(j - split, 0)))

    def place(j):
        k = j - split
        early = jnp.where(j < 2 * n, j, j + n)
        late = jnp.where(k < n, 2 * n + k, 4 * n + k)
        return (0, jnp.where(j < split, early, late))

    out = pl.BlockSpec((wide // 2, step), place)
    shape = jax.ShapeDtypeStruct((wide // 2, 6 * ff), LOW)
    return pl.pallas_call(
        functools.partial(ff_weights_kernel, chunks, split),
        grid=(6 * n,),
        in_specs=[full] * (2 * chunks) + [grad] * chunks + [last] * chunks,
        out_specs=[out, out],
        scratch_shapes=[pltpu.VMEM((wide, rows * chunks), LOW)],
        out_shape=[shape, shape],
        compiler_params=limits(),
        cost_estimate=cost(12 * chunks * rows * wide * ff, 12 * wide * ff + 8 * chunks * rows * wide),
        name="ff_weights",
    )(*all_b, *branch_b, *grads, *inner)


def in_weights_kernel(chunks, *refs):
    xa_refs, ba_refs, dp_refs, at_refs = [refs[i * chunks : (i + 1) * chunks] for i in range(4)]
    first_ref, second_ref = refs[4 * chunks :]
    width = dp_refs[0].shape[1] // 2
    q_width = at_refs[0].shape[1] // 2
    half = first_ref.shape[0]
    for x_refs, y_refs, size, base in (
        (xa_refs, dp_refs, width, 0),
        (ba_refs, at_refs, q_width, width),
    ):
        turned = jnp.concatenate([ref[...].T for ref in x_refs], axis=1)
        for side in range(2):
            grads = jnp.concatenate(
                [ref[:, side * size : (side + 1) * size] for ref in y_refs], axis=0
            )
            start = side * (width + q_width) + base
            second_ref[:, start : start + size] = low_dot(turned[half:], grads).astype(LOW)
            first_ref[:, start : start + size] = low_dot(turned[:half], grads).astype(LOW)


def in_weights(all_a, branch_a, grads, attended):
    chunks = len(all_a)
    rows, wide = all_a[0].shape
    width = grads[0].shape[1] + attended[0].shape[1]
    operands = list(all_a) + list(branch_a) + list(grads) + list(attended)
    shape = (wide // 2, width)
    return pl.pallas_call(
        functools.partial(in_weights_kernel, chunks),
        grid=(1,),
        in_specs=[whole(v.shape) for v in operands],
        out_specs=[whole(shape)] * 2,
        out_shape=[jax.ShapeDtypeStruct(shape, LOW)] * 2,
        compiler_params=limits(),
        cost_estimate=cost(
            2 * chunks * rows * wide * width, 2 * wide * width + 4 * chunks * rows * wide
        ),
        name="in_weights",
    )(*operands)


def role_sum_kernel(row_ref, side_ref, left_ref, right_ref, *outs):
    step = pl.program_id(0)
    total = (left_ref[...].astype(FULL) + right_ref[...].astype(FULL)).astype(LOW)
    for i, out_ref in enumerate(outs):

        @pl.when(step // 2 == i)
        def _(out_ref=out_ref):
            out_ref[...] = total


def role_sums(place, left, right):
    rows, both = left.shape[0] // 4, left.shape[1]
    width = both // 2
    picks = [pick for role in ROLES for pick in role]
    row = place ^ jnp.array([m for m, _ in picks], jnp.int32)
    side = jnp.array([s for _, s in picks], jnp.int32)
    block = pl.BlockSpec((rows, width), lambda i, r, s: (r[i], s[i]))

    def out(k):
        return pl.BlockSpec((rows, width), lambda i, r, s: (jnp.where(i > 2 * k, 1, 0), 0))

    return pl.pallas_call(
        role_sum_kernel,
        grid_spec=pltpu.PrefetchScalarGridSpec(
            num_scalar_prefetch=2,
            grid=(8,),
            in_specs=[block, block],
            out_specs=[out(k) for k in range(4)],
        ),
        out_shape=[jax.ShapeDtypeStruct((2 * rows, width), LOW)] * 4,
        compiler_params=limits(),
        cost_estimate=cost(0, 12 * rows * both),
        name="role_sums",
    )(row, side, left, right)


def cut_kernel(place_ref, gate_ref, up_ref, down_ref, *refs):
    outs, turned_ref = refs[:3], refs[3]
    turned_ref[...] = down_ref[...].T
    outs[0][...] = gate_ref[...]
    outs[1][...] = up_ref[...]
    rows = outs[2].shape[0]
    start = pl.multiple_of(place_ref[0] * rows, rows)
    outs[2][...] = turned_ref[pl.ds(start, rows), :]


def cut_ff(place, layer, gate, up, down):
    wide, ff = gate.shape[1:]
    rows = wide // lax.axis_size("dp")
    block = pl.BlockSpec((None, rows, ff), lambda i, p: (layer, p[0], 0))
    return pl.pallas_call(
        cut_kernel,
        grid_spec=pltpu.PrefetchScalarGridSpec(
            num_scalar_prefetch=1,
            grid=(1,),
            in_specs=[block, block, pl.BlockSpec((None, ff, wide), lambda i, p: (layer, 0, 0))],
            out_specs=[whole((rows, ff))] * 3,
            scratch_shapes=[pltpu.VMEM((wide, ff), LOW)],
        ),
        out_shape=[jax.ShapeDtypeStruct((rows, ff), LOW)] * 3,
        compiler_params=limits(),
        cost_estimate=cost(0, 4 * wide * ff),
        name="cut_ff",
    )(place, gate, up, down)


def pick_kernel(hi_ref, block_ref, mine_ref, other_ref):
    first, second = block_ref[:, 0, :], block_ref[:, 1, :]
    mine_ref[...] = jnp.where(hi_ref[0] == 0, first, second)
    other_ref[...] = jnp.where(hi_ref[0] == 0, second, first)


def pick(hi, block):
    rows, _, width = block.shape
    return pl.pallas_call(
        pick_kernel,
        grid_spec=pltpu.PrefetchScalarGridSpec(
            num_scalar_prefetch=1,
            grid=(1,),
            in_specs=[whole(block.shape)],
            out_specs=[whole((rows, width))] * 2,
        ),
        out_shape=[jax.ShapeDtypeStruct((rows, width), LOW)] * 2,
        compiler_params=limits(),
        cost_estimate=cost(0, 8 * rows * width),
        name="pick",
    )(hi.astype(jnp.int32).reshape(1), block)


def spread_ff_kernel(spots, place_ref, *refs):
    count = len(spots)
    gate_refs, up_refs, down_refs = [refs[i * count : (i + 1) * count] for i in range(3)]
    outs, held_ref = refs[-4:-1], refs[-1]
    put_parts(place_ref, gate_refs, spots, outs[0].at[0])
    put_parts(place_ref, up_refs, spots, outs[1].at[0])
    put_parts(place_ref, down_refs, spots, held_ref)
    outs[2][0] = held_ref[...].T


def flatten(pieces):
    parts, spots = [], []
    for m, piece in enumerate(pieces):
        piece = piece if isinstance(piece, tuple) else (piece,)
        for i, part in enumerate(piece):
            if not isinstance(part, tuple):
                part = (part, 0, part.shape[0])
            parts.append((part[0], part[1] // part[2], part[2]))
            spots.append((m, i, len(piece)))
    return (parts, spots)


def put_parts(place_ref, refs, spots, out_ref):
    for ref, (m, i, count) in zip(refs, spots):
        rows = ref.shape[0]
        start = pl.multiple_of((place_ref[0] ^ m) * (rows * count) + i * rows, rows)
        out_ref[pl.ds(start, rows), :] = ref[...].astype(FULL)


def spread_ff(place, pieces, layer, earlier):
    pieces, spots = flatten(pieces)
    count = len(pieces)
    rows, wide = pieces[0][2], pieces[0][0].shape[1]
    ff = wide // 3
    step = min(256, ff)
    steps = ff // step
    tall = rows * count

    def block(k, at):
        return pl.BlockSpec((rows, step), lambda j, p: (at, j + k * steps))

    in_specs = [block(k, at) for k in range(3) for _, at, _ in pieces]
    operands = [array for array, _, _ in pieces] * 3
    aliases = {}
    if earlier is not None:
        aliases = {1 + len(operands) + i: i for i in range(3)}
        in_specs += [pl.BlockSpec(memory_space=pl.ANY)] * 3
        operands += list(earlier)

    def kernel(place_ref, *refs):
        refs = refs[: 3 * count] + refs[len(operands) :]
        spread_ff_kernel(spots, place_ref, *refs)

    tall_out = pl.BlockSpec((1, tall, step), lambda j, p: (layer, 0, j))
    flat_out = pl.BlockSpec((1, step, tall), lambda j, p: (layer, j, 0))
    return pl.pallas_call(
        kernel,
        grid_spec=pltpu.PrefetchScalarGridSpec(
            num_scalar_prefetch=1,
            grid=(steps,),
            in_specs=in_specs,
            out_specs=[tall_out, tall_out, flat_out],
            scratch_shapes=[pltpu.VMEM((tall, step), FULL)],
        ),
        out_shape=[
            jax.ShapeDtypeStruct((LAYERS, tall, ff), FULL),
            jax.ShapeDtypeStruct((LAYERS, tall, ff), FULL),
            jax.ShapeDtypeStruct((LAYERS, ff, tall), FULL),
        ],
        input_output_aliases=aliases,
        compiler_params=limits(),
        cost_estimate=cost(0, 18 * tall * ff),
        name="spread_ff",
    )(place, *operands)


def spread_in(place, pieces, layer, earlier, q_width):
    pieces, spots = flatten(pieces)
    count = len(pieces)
    rows, width = pieces[0][2], pieces[0][0].shape[1]
    tall = rows * count
    kv_width = q_width // 2
    operands = [array for array, _, _ in pieces]
    in_specs = [pl.BlockSpec((rows, width), lambda j, p, at=at: (at, 0)) for _, at, _ in pieces]
    aliases = {}
    if earlier is not None:
        aliases = {1 + count + i: i for i in range(4)}
        in_specs = in_specs + [pl.BlockSpec(memory_space=pl.ANY)] * 4
        operands += list(earlier)

    def kernel(place_ref, *refs):
        piece_refs, (q_ref, k_ref, v_ref, o_ref, held_ref) = refs[:count], refs[len(operands) :]
        put_parts(place_ref, piece_refs, spots, held_ref)
        at = 0
        for out_ref, size in ((q_ref, q_width), (k_ref, kv_width), (v_ref, kv_width)):
            out_ref[0] = held_ref[:, at : at + size]
            at += size
        o_ref[0] = held_ref[:, at:].T

    sizes = [(tall, q_width), (tall, kv_width), (tall, kv_width), (q_width, tall)]
    return pl.pallas_call(
        kernel,
        grid_spec=pltpu.PrefetchScalarGridSpec(
            num_scalar_prefetch=1,
            grid=(1,),
            in_specs=in_specs,
            out_specs=[pl.BlockSpec((1,) + s, lambda j, p: (layer, 0, 0)) for s in sizes],
            scratch_shapes=[pltpu.VMEM((tall, width), FULL)],
        ),
        out_shape=[jax.ShapeDtypeStruct((LAYERS,) + s, FULL) for s in sizes],
        input_output_aliases=aliases,
        compiler_params=limits(),
        cost_estimate=cost(0, 6 * tall * width),
        name="spread_in",
    )(place, *operands)


def gather_kernel(count, tops, place_ref, *refs):
    piece_refs, out_ref = refs[:count], refs[count]
    for m, ref in enumerate(piece_refs):
        row, part_row = 0, 0
        for size in tops:
            part = size // count
            start = pl.multiple_of(row + (place_ref[0] ^ m) * part, part)
            out_ref[pl.ds(start, part), :] = ref[part_row : part_row + part, :]
            row += size
            part_row += part


def gather_pieces(place, pieces, tops):
    count = len(pieces)
    shape = (sum(tops), pieces[0].shape[1])
    return pl.pallas_call(
        functools.partial(gather_kernel, count, tops),
        grid_spec=pltpu.PrefetchScalarGridSpec(
            num_scalar_prefetch=1,
            grid=(1,),
            in_specs=[whole(p.shape) for p in pieces],
            out_specs=whole(shape),
        ),
        out_shape=jax.ShapeDtypeStruct(shape, LOW),
        compiler_params=limits(),
        cost_estimate=cost(0, 4 * shape[0] * shape[1]),
        name="gather_pieces",
    )(place, *pieces)


def cut(weight, layer, place):
    rows = weight.shape[1] // lax.axis_size("dp")
    start = (jnp.int32(layer), place * rows, jnp.int32(0))
    return lax.dynamic_slice(weight, start, (1, rows, weight.shape[2]))[0]


class Group:
    def __init__(self, piece, tops, place):
        self.piece, self.tops, self.place = piece, tops, place
        self.count = lax.axis_size("dp")
        self.even = all(size // self.count % 16 == 0 for size in tops)

    def fetch(self, order):
        self.piece = flip_hi(order.after(self.piece))

    def gather(self, order):
        order.join(self.piece)
        piece = order.after(self.piece)
        if len(self.tops) == 1:
            self.first = lax.all_gather(piece, "dp", axis=0, tiled=True)
            return
        pieces = lax.all_gather(piece, "dp", axis=0)
        at, rows = 0, []
        for size in self.tops:
            part = size // self.count
            rows.append(pieces[:, at : at + part].reshape(size, -1))
            at += part
        self.first = jnp.concatenate(rows, axis=0)

    def cross(self, order):
        self.halves = (self.first, flip_core(self.first))

    def spread(self, order):
        order.join(self.piece)
        if self.even:
            piece = order.after(self.piece)
            self.pieces = [piece] + [hop(piece, "dp", m) for m in (1, 2)]
        else:
            self.gather(order)

    def spread_on(self, order):
        if self.even:
            order.join(*self.pieces[1:])
            piece = order.after(self.pieces[0])
            self.pieces += [hop(piece, "dp", m) for m in range(len(self.pieces), self.count)]

    def collect(self, order):
        if self.even:
            spot = self.place.astype(jnp.int32).reshape(1)
            order.join(*self.pieces[1:])
            pieces = [order.after(self.pieces[0])] + self.pieces[1:]
            self.first = gather_pieces(spot, pieces, self.tops)
        order.mark(self.first)
        self.cross(order)

    def done(self, order):
        order.join(self.halves[1])


def in_groups(layer, w_in, w_out, place, packed):
    in_piece, out_piece = cut(w_in, layer, place), cut(w_out, layer, place)
    wide, q_width = w_in.shape[1], w_out.shape[1]
    if packed and w_in.shape[2] == w_out.shape[2]:
        piece = jnp.concatenate([in_piece, out_piece], axis=0)
        return [Group(piece, (wide, q_width), place)]
    return [Group(in_piece, (wide,), place), Group(out_piece, (q_width,), place)]


ROLES = (((1, 0), (3, 0)), ((2, 1), (3, 1)), ((2, 0), (1, 1)), ((0, 0), (0, 1)))


class Sum:
    def __init__(self, parts, place):
        self.first, self.last = parts
        self.place = place
        self.even = lax.axis_size("dp") == 4

    def flip(self, order):
        self.came = flip_core(order.after(self.last))

    def start(self, order):
        if not self.even:
            total = add_low(self.first, self.came)
            width = total.shape[1] // 2
            self.own = lax.psum_scatter(total[:, :width], "dp", scatter_dimension=0, tiled=True)
            self.other = lax.psum_scatter(total[:, width:], "dp", scatter_dimension=0, tiled=True)
            return
        order.join(self.came)
        spot = self.place.astype(jnp.int32).reshape(1)
        roles = role_sums(spot, order.after(self.first), self.came)
        to_x, to_y, self.on, self.keep = order.mark(roles)
        self.from_x, self.from_y = hop(to_x, "dp", 1), hop(to_y, "dp", 2)

    def arrived(self, order):
        if self.even:
            order.join(self.from_x, self.from_y)

    def second(self, order):
        if not self.even:
            return
        rows = self.on.shape[0] // 2
        on, keep, from_x, from_y = order.after((self.on, self.keep, self.from_x, self.from_y))
        to_y = add_low(on[:rows], from_x[rows:])
        to_x = add_low(on[rows:], from_y[rows:])
        self.own = add_low(keep[:rows], from_x[:rows])
        self.other = add_low(keep[rows:], from_y[:rows])
        order.mark((to_x, to_y))
        self.to_own, self.to_other = hop(to_y, "dp", 2), hop(to_x, "dp", 1)

    def third(self, order):
        if self.even:
            order.join(self.to_own)
            other, came = order.after((self.other, self.to_other))
            self.other = order.mark(add_low(other, came))

    def across(self, order):
        self.far = flip_hi(order.after(self.other))

    def fourth(self, order):
        if self.even:
            own, came, far = order.after((self.own, self.to_own, self.far))
            total = (own.astype(FULL) + came.astype(FULL) + far.astype(FULL)).astype(LOW)
        else:
            total = add_low(self.own, self.far)
        self.total = order.mark(total)

    def near(self, order):
        count = lax.axis_size("dp")
        total = order.after(self.total)
        if not self.even:
            self.pieces = [total] + [hop(total, "dp", m) for m in range(1, count)]
            return
        rows = total.shape[0] // 2
        self.mine = (total[:rows], total[rows:])
        self.beside = [hop(self.mine[0], "dp", 1), hop(self.mine[1], "dp", 2)]

    def fifth(self, order):
        if not self.even:
            return
        top, bottom = self.mine
        order.join(*self.beside)
        near_x, near_y = order.after(tuple(self.beside))
        tops = order.mark(jnp.concatenate([top, near_x], axis=0))
        bottoms = order.mark(jnp.concatenate([bottom, near_y], axis=0))
        tops, bottoms = hop(tops, "dp", 2), hop(bottoms, "dp", 1)
        rows = top.shape[0]
        self.pieces = [
            (top, bottom),
            (near_x, (bottoms, 0, rows)),
            ((tops, 0, rows), near_y),
            ((tops, rows, rows), (bottoms, rows, rows)),
        ]

    def done(self, order):
        order.join(*(part for piece in self.pieces if isinstance(piece, tuple) for part in piece))


def rope_tables(positions, width):
    indices = jnp.arange(HEAD // 2, dtype=FULL)
    inverse = ROPE_BASE ** (-2.0 * indices / HEAD)
    angles = positions.astype(FULL)[:, None] * inverse[None, :]
    cosine, sine = jnp.cos(angles), jnp.sin(angles)
    heads = width // HEAD
    return (
        jnp.concatenate([cosine, cosine] * heads, axis=1),
        jnp.concatenate([-sine, sine] * heads, axis=1),
    )


def finish_back(grad, left, right, hidden, factor, gain):
    unit = hidden * factor
    grad_normed = left.astype(FULL) + right.astype(FULL)
    grad_unit = grad_normed * gain
    inner = jnp.mean(grad_unit * unit, axis=-1, keepdims=True)
    return (
        grad + factor * (grad_unit - unit * inner),
        jnp.sum(grad_normed * unit, axis=0, keepdims=True),
    )


class Arrival:
    def __init__(self, block, hi, lo, core):
        self.block, self.hi, self.lo, self.core = block, hi, lo, core

    def pick(self, order):
        self.mine, self.other = order.mark(pick(self.hi, order.after(self.block)))

    def fetch_on(self, order):
        self.far = flip_hi(order.after(self.other))

    def fetch(self, order):
        self.pick(order)
        self.fetch_on(order)

    def share(self, order):
        order.join(self.far)
        mine, far = order.after((self.mine, self.far))
        self.parts = [jnp.where(self.hi == j, mine, far) for j in range(CHUNKS)]
        order.mark(tuple(self.parts))
        self.halves = [None] * CHUNKS
        self.near = [None] * CHUNKS

    def send(self, order, j):
        self.near[j] = hop(order.after(self.parts[j]), "cols", 1)

    def cross(self, order, j):
        lo, core = self.lo, self.core
        order.join(self.near[j])
        part, near = order.after((self.parts[j], self.near[j]))
        if len(low_bits()) == 1:
            at_home = lo == core
            first = jnp.where(at_home, part, near)
            second = jnp.where(at_home, near, part)
        else:
            for bit in low_bits():
                far = near if bit == 1 else hop(part, "cols", bit)
                part = jnp.where(
                    (lo & bit) == 0,
                    jnp.concatenate([part, far], axis=0),
                    jnp.concatenate([far, part], axis=0),
                )
            half = part.shape[0] // 2
            first = lax.dynamic_slice_in_dim(part, core * half, half, 0)
            second = lax.dynamic_slice_in_dim(part, (1 - core) * half, half, 0)
        first, second = order.mark((first, second))
        self.halves[j] = (first, flip_core(second))

    def chunk(self, order, j):
        order.join(self.halves[j][1])
        return order.mark(jnp.concatenate(order.after(self.halves[j]), axis=-1))


def leave(chunks, hi, lo, core, rows):
    parts = []
    for value in chunks:
        width = value.shape[-1] // 2
        first = value[:, :width]
        second = flip_core(value[:, width:].astype(LOW)).astype(FULL)
        both = jnp.where(
            core == 0,
            jnp.concatenate([first, second], axis=0),
            jnp.concatenate([second, first], axis=0),
        )
        parts.append(lax.dynamic_slice_in_dim(both, lo * rows, rows, 0))
    mine = jnp.where(hi == 0, parts[0], parts[1])
    other = flip_hi(jnp.where(hi == 0, parts[1], parts[0]).astype(LOW)).astype(FULL)
    return jnp.where(
        hi == 0, jnp.stack([mine, other], axis=1), jnp.stack([other, mine], axis=1)
    )


def shards(
    block_input, block_cotangent, w_query, w_key, w_value, w_out, w_gate, w_up, w_down, norm_gains
):
    low_count = lax.axis_size("cols") // 2
    core, col, place = lax.axis_index("rows"), lax.axis_index("cols"), lax.axis_index("dp")
    hi, lo = col // low_count, col % low_count
    core_ref = core.astype(jnp.int32).reshape(1)
    block_rows = block_input.shape[0]
    rows = block_rows * low_count
    q_width = w_query.shape[2]
    half = rows // 2
    tables = [
        rope_tables(jnp.arange(half, dtype=jnp.int32) + j * rows + core * half, q_width)
        for j in range(CHUNKS)
    ]
    spot = place.astype(jnp.int32).reshape(1)
    order = Order()
    w_in = jnp.concatenate([w_query, w_key, w_value], axis=2)
    wide = w_in.shape[1]
    ff = w_gate.shape[2]
    a_groups = [in_groups(0, w_in, w_out, place, True), None]
    order.mark([group.piece for group in a_groups[0]])
    for group in a_groups[0]:
        group.fetch(order)
    arrival = Arrival(block_input, hi, lo, core)
    arrival.fetch(order)
    in_own, out_own, gates, ups, own_downs = [
        (v, flip_core(v)) for v in (w_in, w_out, w_gate, w_up, w_down)
    ]
    gains = jnp.concatenate([norm_gains, flip_core(norm_gains)], axis=-1)
    f_groups = []
    for l in range(LAYERS):
        pieces = order.mark(cut_ff(spot, l, order.after(w_gate), w_up, w_down))
        f_groups.append([Group(piece, (wide,), place) for piece in pieces])
        order.join(*((in_own[1], gains) if not l else (out_own[1],)))
    a_groups[1] = in_groups(1, order.after(w_in), w_out, place, True)
    order.mark([group.piece for group in a_groups[1]])
    order.join(gates[1], ups[1])
    for group in a_groups[0]:
        group.spread(order)
    arrival.share(order)
    arrival.send(order, 0)
    f_groups[0][0].fetch(order)
    for group in a_groups[0]:
        group.spread_on(order)
    arrival.cross(order, 0)
    f_groups[0][0].gather(order)
    f_groups[0][1].fetch(order)
    for group in a_groups[0]:
        group.collect(order)
    hidden = [arrival.chunk(order, 0)]
    order.join(own_downs[1])
    arrival.send(order, 1)
    f_groups[0][1].gather(order)
    for group in a_groups[0]:
        group.done(order)

    cotangent = Arrival(block_cotangent, hi, lo, core)
    stash = [[None] * CHUNKS for _ in range(LAYERS)]
    weights = [None] * LAYERS
    pairs = [None] * CHUNKS

    def front(l, j):
        block, factor_a, normed_a, query, mine = order.mark(
            project(order.after(hidden[j]), pairs[j], gains[l, 0:1], ins, *tables[j])
        )
        kvs.extend([mine, flip_core(mine)])
        return (block, factor_a, normed_a, query)

    def middle(l, j, kept):
        order.join(kvs[2 * j + 1])
        attended, lse, part = order.mark(
            attend(core_ref, order.after(kept[3]), kvs[: 2 * j + 2], outs)
        )
        pairs[j] = group_pair(part)
        return (*kept, kvs[: 2 * j + 2], lse, attended)

    def rear(l, j, kept):
        order.join(pairs[j])
        mixed, factor_b, normed_b, gate, up, inner, part = order.mark(
            feed_forward(order.after(kept[0]), pairs[j], gains[l, 1:2], pair_parts, down_parts)
        )
        hidden[j] = mixed
        pairs[j] = group_pair(part) if l + 1 < LAYERS else part
        stash[l][j] = kept + (mixed, factor_b, normed_b, gate, up, inner)

    for l in range(LAYERS):
        more = l + 1 < LAYERS
        halves = [group.halves for group in a_groups[l]]
        if len(halves) == 1:
            ins = [Part(v, None, 0, wide) for v in halves[0]]
            outs = [Part(v, None, wide, w_out.shape[1]) for v in halves[0]]
        else:
            ins, outs = [[Part(v) for v in pair] for pair in halves]
        ins = [Part(v, l) for v in in_own] + ins
        outs = [Part(v, l) for v in out_own] + outs
        kvs, kept = [], [None] * CHUNKS
        first, second, third = f_groups[l]
        if not l:
            kept[0] = front(l, 0)
            third.fetch(order)
            arrival.cross(order, 1)
            kept[0] = middle(l, 0, kept[0])
            third.gather(order)
            hidden.append(arrival.chunk(order, 1))
            kept[1] = front(l, 1)
            first.cross(order)
            for group in a_groups[1]:
                group.fetch(order)
            order.join(pairs[0])
            kept[1] = middle(l, 1, kept[1])
            first.done(order)
            for group in a_groups[1]:
                group.gather(order)
            f_groups[1][0].fetch(order)
            second.cross(order)
            third.cross(order)
        else:
            order.join(pairs[0])
            kept[0] = front(l, 0)
            second.gather(order)
            third.fetch(order)
            order.join(pairs[1])
            kept[1] = front(l, 1)
            kept[0] = middle(l, 0, kept[0])
            third.gather(order)
            cotangent.fetch_on(order)
            first.cross(order)
            kept[1] = middle(l, 1, kept[1])
            first.done(order)
            cotangent.share(order)
            cotangent.send(order, 1)
            second.cross(order)
            third.cross(order)
        second.done(order)
        third.done(order)
        packs = [group.halves for group in f_groups[l]]
        pair_parts = [Part(v, l) for v in (*gates, *ups)] + [
            Part(v) for pack in packs[:2] for v in pack
        ]
        down_parts = [Part(v, l) for v in own_downs] + [Part(v) for v in packs[2]]
        weights[l] = (ins, outs, pair_parts, down_parts)
        rear(l, 0, kept[0])
        if more:
            order.join(pairs[1])
            f_groups[1][0].gather(order)
            f_groups[1][1].fetch(order)
        else:
            cotangent.cross(order, 1)
            cotangent.send(order, 0)
        rear(l, 1, kept[1])
        if more:
            cotangent.pick(order)
            for group in a_groups[1]:
                group.cross(order)
                group.done(order)
    grads = [None] * CHUNKS
    grads[1] = (cotangent.chunk(order, 1),)

    gain_a, gain_b = [0.0] * LAYERS, [0.0] * LAYERS
    sums = {}

    def ff_step(l, j):
        pair_parts, down_parts = weights[l][2:]
        gate, up, inner = stash[l][j][-3:]
        if len(grads[j]) == 1:
            branch_b = order.after(grads[j][0])
            grad_hidden = branch_b.astype(FULL)
            pair_grad, part = order.mark(feed_back((branch_b,), gate, up, pair_parts, down_parts))
        else:
            order.join(*grads[j][1:3])
            grad_hidden, branch_b, gain_part, pair_grad, part = order.mark(
                feed_back(
                    (order.after(grads[j][0]), *grads[j][1:]), gate, up, pair_parts, down_parts
                )
            )
            gain_a[l + 1] = gain_a[l + 1] + gain_part
        mixed, factor_b, normed_b = stash[l][j][7:10]
        grads[j] = (grad_hidden, *group_pair(part), mixed, factor_b, gains[l, 1:2])
        return (normed_b, branch_b, pair_grad, inner)

    def ff_grad(l, kept):
        columns = list(zip(*kept))
        columns[0] = order.after(columns[0])
        sums["ff", l] = Sum(order.mark(ff_weights(*columns)), place)

    def attend_step(l, j, held):
        block, factor_a, normed_a, query, kvs, lse, attended = stash[l][j][:7]
        order.join(*grads[j][1:3])
        grad_mixed, branch_a, gain_part, dq, *dkvs = order.mark(
            attend_back(
                core_ref,
                (order.after(grads[j][0]), *grads[j][1:]),
                query,
                lse,
                kvs,
                held,
                weights[l][1],
            )
        )
        gain_b[l] = gain_b[l] + gain_part
        grads[j] = (grad_mixed, None, None, block, factor_a, gains[l, 0:1])
        send = order.mark(order.after(dkvs[-1]).astype(LOW))
        middle = (dq, dkvs[-2], flip_core(send))
        return (dkvs[:2], middle, (normed_a, branch_a, None, attended))

    def project_step(l, j, middle, kept):
        dq, mine, came = middle
        order.join(came)
        proj_grad, part = order.mark(
            project_back(order.after(dq), mine, came, *tables[j], weights[l][0])
        )
        grads[j] = (grads[j][0], *group_pair(part), *grads[j][3:])
        return kept[:2] + (proj_grad,) + kept[3:]

    def in_grad(l, kept):
        columns = list(zip(*kept))
        columns[0] = order.after(columns[0])
        sums["in", l] = Sum(order.mark(in_weights(*columns)), place)

    l = LAYERS - 1
    kept, mids = [None] * CHUNKS, [None] * CHUNKS
    kept[1] = ff_step(l, 1)
    cotangent.cross(order, 0)
    grads[0] = (cotangent.chunk(order, 0),)
    kept[0] = ff_step(l, 0)
    ff_grad(l, kept)
    sums["ff", l].flip(order)
    held, mids[1], kept[1] = attend_step(l, 1, None)
    sums["ff", l].start(order)
    order.join(mids[1][2])
    _, mids[0], kept[0] = attend_step(l, 0, held)
    kept[1] = project_step(l, 1, mids[1], kept[1])
    kept[0] = project_step(l, 0, mids[0], kept[0])
    in_grad(l, kept)
    l = 0
    kept, mids = [None] * CHUNKS, [None] * CHUNKS
    kept[1] = ff_step(l, 1)
    sums["ff", 1].second(order)
    kept[0] = ff_step(l, 0)
    sums["in", 1].flip(order)
    ff_grad(l, kept)
    sums["ff", 1].third(order)
    sums["ff", 0].flip(order)
    sums["in", 1].start(order)
    held, mids[1], kept[1] = attend_step(l, 1, None)
    order.join(mids[1][2])
    sums["in", 1].arrived(order)
    sums["ff", 0].start(order)
    _, mids[0], kept[0] = attend_step(l, 0, held)
    kept[1] = project_step(l, 1, mids[1], kept[1])
    kept[0] = project_step(l, 0, mids[0], kept[0])
    in_grad(l, kept)
    for g in grads:
        order.join(*g[1:3])
    ends = [finish_back(order.after(g[0]), *g[1:]) for g in grads]
    order.mark(tuple(g for g, _ in ends))
    gain_a[0] = sum(part for _, part in ends)
    sums["ff", 0].second(order)
    sums["ff", 1].across(order)
    sums["in", 0].flip(order)
    sums["in", 1].second(order)
    sums["ff", 0].third(order)
    sums["ff", 0].across(order)
    sums["in", 0].start(order)
    sums["in", 1].third(order)
    sums["ff", 1].fourth(order)
    sums["in", 1].across(order)
    sums["in", 0].second(order)
    sums["ff", 1].near(order)
    sums["in", 0].third(order)
    sums["in", 0].across(order)
    sums["ff", 1].fifth(order)
    sums["in", 1].fourth(order)
    input_grad = order.mark(leave(order.after([g for g, _ in ends]), hi, lo, core, block_rows))
    sums["in", 1].near(order)
    sums["ff", 1].done(order)
    ff_out = order.mark(spread_ff(order.after(spot), sums["ff", 1].pieces, 1, None))
    sums["in", 1].fifth(order)
    sums["ff", 0].fourth(order)
    sums["ff", 0].near(order)
    sums["in", 0].fourth(order)
    sums["in", 1].done(order)
    sums["ff", 0].fifth(order)
    sums["in", 0].near(order)
    in_out = order.mark(spread_in(order.after(spot), sums["in", 1].pieces, 1, None, q_width))
    sums["in", 0].fifth(order)
    tops = [group_pair(part) for part in order.after(pairs)]
    hidden = [
        h + left.astype(FULL) + right.astype(FULL) for h, (left, right) in zip(hidden, tops)
    ]
    activations = leave(hidden, hi, lo, core, block_rows)
    sums["in", 0].done(order)
    in_out = order.mark(spread_in(order.after(spot), sums["in", 0].pieces, 0, in_out, q_width))
    sums["ff", 0].done(order)
    ff_out = spread_ff(order.after(spot), sums["ff", 0].pieces, 0, ff_out)
    gain_grads = [jnp.concatenate([gain_a[l], gain_b[l]], axis=0) for l in range(LAYERS)]

    grad_gains = jnp.stack(gain_grads)
    width = grad_gains.shape[-1] // 2
    grad_gains = grad_gains[..., :width] + flip_core(grad_gains[..., width:])
    grad_gains = grad_gains + flip_hi(grad_gains)
    bit = 1
    while bit < lax.axis_size("dp"):
        grad_gains = grad_gains + hop(grad_gains, "dp", bit)
        bit *= 2
    return (activations, input_grad, *in_out, *ff_out, grad_gains)


def solution(mesh):
    data = P("cols", "dp", "rows")
    tall = P(None, "rows", "cols")
    flat = P(None, "cols", "rows")
    gains = P(None, None, "rows")
    in_specs = (data, data, tall, tall, tall, flat, tall, tall, flat, gains)
    out_specs = (data, data, tall, tall, tall, flat, tall, tall, flat, gains)
    return jax.shard_map(
        shards, mesh=mesh, in_specs=in_specs, out_specs=out_specs, check_vma=False
    )
```

```python
import functools

import jax
import jax.numpy as jnp
from jax import lax
from jax.experimental import pallas as pl
from jax.experimental.pallas import tpu as pltpu
from jax.sharding import PartitionSpec as P

HEAD = 96
LAYERS = 2
CHUNKS = 2
EPSILON = 1e-05
ROPE_BASE = 100000.0
NEGATIVE = -1e30
LOW = jnp.bfloat16
FULL = jnp.float32
NT = (((1,), (1,)), ((), ()))
TN = (((0,), (0,)), ((), ()))
ROOM = 56 * 2**20
SCALE = 30
AHEAD = 8 * 2**20


def hop(value, axis, distance):
    size = lax.axis_size(axis)
    return lax.ppermute(value, axis, [(i, i ^ distance) for i in range(size)])


def flip_hi(value):
    return hop(value, "cols", lax.axis_size("cols") // 2)


def flip_core(value):
    return hop(value, "rows", 1)


def low_bits():
    bits, bit = [], 1
    while bit < lax.axis_size("cols") // 2:
        bits.append(bit)
        bit *= 2
    return bits


def group_pair(part):
    bits = low_bits()
    for bit in bits[:-1]:
        part = add_low(part, hop(part, "cols", bit))
    return (part, hop(part, "cols", bits[-1]))


class Order:
    def __init__(self):
        self.last = ()

    def after(self, values):
        return lax.optimization_barrier((values, self.last))[0] if self.last else values

    def mark(self, value):
        self.last = (value,)
        return value

    def join(self, *values):
        self.last = (*self.last, values)


def add_low(left, right):
    return (left.astype(FULL) + right.astype(FULL)).astype(LOW)


def low_dot(left, right):
    return jnp.dot(left, right, preferred_element_type=FULL)


def dot_nt(left, right):
    return lax.dot_general(left, right, NT, preferred_element_type=FULL)


def dot_tn(left, right):
    return lax.dot_general(left, right, TN, preferred_element_type=FULL)


def whole(shape):
    return pl.BlockSpec(shape, lambda *_: (0,) * len(shape))


def far():
    return pl.BlockSpec(memory_space=pl.ANY)


def cost(flops, size, exps=0):
    return pl.CostEstimate(
        flops=int(flops * SCALE), bytes_accessed=int(size * SCALE), transcendentals=0
    )


def limits():
    return pltpu.CompilerParams(vmem_limit_bytes=ROOM)


class Part:
    def __init__(self, array, layer=None, row=0, rows=None, column=0, columns=None):
        self.array, self.layer, self.row, self.column = array, layer, row, column
        self.shape = (rows or array.shape[-2], columns or array.shape[-1])

    def view(self, ref):
        ref = ref if self.layer is None else ref.at[self.layer]
        if self.shape == tuple(ref.shape):
            return ref
        return ref.at[pl.ds(self.row, self.shape[0]), pl.ds(self.column, self.shape[1])]

    def scratch(self):
        return pltpu.VMEM(self.shape, self.array.dtype)


class Stream:
    def __init__(self, sources, buffers, sems, ahead):
        self.copies = [
            pltpu.make_async_copy(source, buffer, sems.at[i])
            for i, (source, buffer) in enumerate(zip(sources, buffers))
        ]
        self.buffers = buffers
        self.sizes = [
            b.shape[0] * b.shape[1] * (4 if b.dtype == FULL else 2) for b in buffers
        ]
        self.ahead, self.started, self.waited = ahead, 0, 0
        self.feed()

    def feed(self):
        while self.started < len(self.copies) and (
            sum(self.sizes[self.waited : self.started]) < self.ahead
        ):
            self.copies[self.started].start()
            self.started += 1

    def take(self, count):
        first = self.waited
        for i in range(first, first + count):
            if i >= self.started:
                self.copies[i].start()
                self.started += 1
            self.copies[i].wait()
            self.waited += 1
        self.feed()
        return self.buffers[first : first + count]


class Results:
    def __init__(self, buffers, targets, sems):
        self.buffers, self.targets, self.sems = buffers, targets, sems
        self.copies = []

    def put(self, index):
        copy = pltpu.make_async_copy(
            self.buffers[index], self.targets[index], self.sems.at[index]
        )
        copy.start()
        self.copies.append(copy)

    def finish(self):
        for copy in self.copies:
            copy.wait()


def half_dots(left, first, second):
    half = left.shape[1] // 2
    return low_dot(left[:, :half], first) + low_dot(left[:, half:], second)


def turn(value, cosine, sine):
    width = value.shape[1]
    q_width = cosine.shape[1]
    ahead = pltpu.roll(value, width - HEAD // 2, 1)
    behind = pltpu.roll(value, HEAD // 2, 1)
    column = lax.broadcasted_iota(jnp.int32, value.shape, 1)
    other = jnp.where(lax.rem(column, HEAD) < HEAD // 2, ahead, behind)
    is_key = lax.broadcasted_iota(jnp.int32, cosine.shape, 1) < q_width // 2
    query = value[:, :q_width] * cosine + other[:, :q_width] * sine
    rest = value[:, q_width:] * jnp.where(is_key, cosine, 1.0)
    rest = rest + other[:, q_width:] * jnp.where(is_key, sine, 0.0)
    return (query, rest)


def put_norm(refs, gain_ref, results, at):
    sum_ref, factor_ref, normed_ref = results.buffers[at : at + 3]
    hidden = refs[0][...].astype(FULL)
    for ref in refs[1:]:
        hidden = hidden + ref[...].astype(FULL)
    factor = lax.rsqrt(jnp.mean(hidden * hidden, axis=-1, keepdims=True) + EPSILON)
    sum_ref[...] = hidden
    factor_ref[...] = factor
    normed_ref[...] = (hidden * factor * gain_ref[...]).astype(LOW)
    for i in range(3):
        results.put(at + i)


def put_norm_back(refs, results, at):
    grad_ref, left_ref, right_ref, hidden_ref, factor_ref, gain_ref = refs
    sum_ref, low_ref, gain_out_ref = results.buffers[at : at + 3]
    grad_normed = left_ref[...].astype(FULL) + right_ref[...].astype(FULL)
    factor = factor_ref[...]
    unit = hidden_ref[...] * factor
    grad_unit = grad_normed * gain_ref[...]
    inner = jnp.mean(grad_unit * unit, axis=-1, keepdims=True)
    grad = grad_ref[...].astype(FULL) + factor * (grad_unit - unit * inner)
    sum_ref[...] = grad
    low_ref[...] = grad.astype(LOW)
    gain_out_ref[...] = jnp.sum(grad_normed * unit, axis=0, keepdims=True)
    for i in range(3):
        results.put(at + i)


def norm_shapes(rows, wide):
    return [((rows, wide), FULL), ((rows, 1), FULL), ((rows, wide), LOW)]


def norm_back_shapes(rows, wide):
    return [((rows, wide), FULL), ((rows, wide), LOW), ((1, wide), FULL)]


def call(body, name, inputs, outs, scratch, flops, exps=0, scalars=(), ahead=AHEAD):
    inputs = [v if isinstance(v, Part) else Part(v) for v in inputs]
    size = sum(2 * p.shape[0] * p.shape[1] for p in inputs)
    count, made = len(inputs), len(outs)

    def kernel(*refs):
        scalar_refs, refs = refs[: len(scalars)], refs[len(scalars) :]
        sources, targets, refs = refs[:count], refs[count : count + made], refs[count + made :]
        held, buffers, refs = refs[:count], refs[count : count + made], refs[count + made :]
        in_sems, out_sems, own = refs[0], refs[1], refs[2:]
        stream = Stream([p.view(r) for p, r in zip(inputs, sources)], held, in_sems, ahead)
        results = Results(buffers, targets, out_sems)
        body(stream, results, *scalar_refs, *own)
        results.finish()

    return pl.pallas_call(
        kernel,
        grid_spec=pltpu.PrefetchScalarGridSpec(
            num_scalar_prefetch=len(scalars),
            grid=(1,),
            in_specs=[far()] * count,
            out_specs=[far()] * made,
            scratch_shapes=[p.scratch() for p in inputs]
            + [pltpu.VMEM(s, k) for s, k in outs]
            + [pltpu.SemaphoreType.DMA((count,)), pltpu.SemaphoreType.DMA((made,))]
            + list(scratch),
        ),
        out_shape=[jax.ShapeDtypeStruct(s, k) for s, k in outs],
        compiler_params=limits(),
        cost_estimate=cost(flops, size, exps),
        name=name,
    )(*scalars, *[p.array for p in inputs])


def project(hidden, pair, gain, parts, cosine, sine):
    rows, wide = hidden.shape
    q_width = cosine.shape[1]
    ins = [hidden, *(pair or ())]

    def body(stream, results):
        refs = stream.take(len(ins))
        (gain_ref,) = stream.take(1)
        put_norm(refs, gain_ref, results, 0)
        cos_ref, sin_ref = stream.take(2)
        tokens = results.buffers[2][...]
        q_ref, kv_ref = results.buffers[3:]
        for side in range(2):
            first, second = stream.take(2)
            projected = half_dots(tokens, first[...], second[...])
            query, rest = turn(projected, cos_ref[...], sin_ref[...])
            here = slice(side * q_width, (side + 1) * q_width)
            q_ref[:, here] = query.astype(LOW)
            kv_ref[:, here] = rest.astype(LOW)
        results.put(4)
        results.put(3)

    return call(
        body,
        "project",
        [*ins, gain, cosine, sine, *parts],
        norm_shapes(rows, wide) + [((rows, 2 * q_width), LOW)] * 2,
        [],
        8 * rows * wide * q_width,
    )


def score(key, query, kind, core):
    raw = dot_nt(key, query) * HEAD ** (-0.5)
    if kind == "own":
        key_pos = lax.broadcasted_iota(jnp.int32, raw.shape, 0)
        query_pos = lax.broadcasted_iota(jnp.int32, raw.shape, 1)
        raw = jnp.where(query_pos >= key_pos, raw, NEGATIVE)
    if kind == "sib":
        raw = jnp.where(core == 1, raw, NEGATIVE)
    return raw


def kinds_of(chunks):
    return ["all"] * (2 * chunks - 2) + ["own", "sib"]


def attend(core, query, kvs, parts):
    rows, both = query.shape
    wide = 2 * parts[0].shape[1]
    chunks = len(kvs) // 2
    q_width, heads = both // 2, both // 2 // HEAD
    kv_width = q_width // 2

    def body(stream, results, core_ref):
        (q_ref,), kv_refs = stream.take(1), stream.take(2 * chunks)
        att_ref, lse_ref, part_ref = results.buffers
        side_core = core_ref[0]
        for h in range(2 * heads):
            group = (h // heads) * q_width + (h % heads) // 2 * HEAD
            mine = slice(h * HEAD, (h + 1) * HEAD)
            query = q_ref[:, mine]
            scores = [
                score(ref[:, group : group + HEAD], query, kind, side_core)
                for ref, kind in zip(kv_refs, kinds_of(chunks))
            ]
            highest = functools.reduce(
                jnp.maximum, [jnp.max(s, axis=0, keepdims=True) for s in scores]
            )
            exps = [jnp.exp(s - highest) for s in scores]
            total = sum(jnp.sum(e, axis=0, keepdims=True) for e in exps)
            share = 1.0 / total
            lse_ref[h : h + 1, :] = highest + jnp.log(total)
            spot = slice(group + kv_width, group + kv_width + HEAD)
            att = sum(
                dot_tn((e * share).astype(LOW), ref[:, spot]) for e, ref in zip(exps, kv_refs)
            )
            att_ref[:, mine] = att.astype(LOW)
        results.put(0)
        results.put(1)
        weights = stream.take(4)
        for side in range(2):
            columns = slice(side * wide // 2, (side + 1) * wide // 2)
            total = low_dot(att_ref[:, :q_width], weights[side][...])
            total = total + low_dot(att_ref[:, q_width:], weights[2 + side][...])
            part_ref[:, columns] = total.astype(LOW)
        results.put(2)

    return call(
        body,
        "attend",
        [query, *kvs, *parts],
        [((rows, both), LOW), ((2 * heads, rows), FULL), ((rows, wide), LOW)],
        [],
        16 * heads * rows * rows * len(kvs) * 128 + 2 * rows * both * wide,
        2 * heads * rows * rows * len(kvs),
        (core,),
    )


def attend_back(core, norm_ins, query, lse, kvs, held, parts):
    rows, both = query.shape
    wide = norm_ins[0].shape[1]
    chunks = len(kvs) // 2
    q_width, heads = both // 2, both // 2 // HEAD
    kv_width = q_width // 2
    half = wide // 2
    scale = HEAD ** (-0.5)

    def body(stream, results, core_ref, grad_ref):
        put_norm_back(stream.take(6), results, 0)
        g_ref = results.buffers[1]
        side_core = core_ref[0]
        for side in range(2):
            first, second = stream.take(2)
            grad = dot_nt(g_ref[:, :half], first[...])
            grad = grad + dot_nt(g_ref[:, half:], second[...])
            grad_ref[:, side * q_width : (side + 1) * q_width] = grad.astype(LOW)
        (q_ref,), (lse_ref,), kv_refs = stream.take(1), stream.take(1), stream.take(2 * chunks)
        held_refs = stream.take(2) if held is not None else None
        dq_ref, out_refs = results.buffers[3], results.buffers[4:]
        for first in range(0, 2 * heads, 2):
            group = (first // heads) * q_width + (first % heads) // 2 * HEAD
            key_spot = slice(group, group + HEAD)
            value_spot = slice(group + kv_width, group + kv_width + HEAD)
            key_sums, value_sums = [0.0] * len(kv_refs), [0.0] * len(kv_refs)
            for h in (first, first + 1):
                mine = slice(h * HEAD, (h + 1) * HEAD)
                query, grad, lse = q_ref[:, mine], grad_ref[:, mine], lse_ref[h : h + 1, :]
                probs = [
                    jnp.exp(score(ref[:, key_spot], query, kind, side_core) - lse)
                    for ref, kind in zip(kv_refs, kinds_of(chunks))
                ]
                prob_grads = [dot_nt(ref[:, value_spot], grad) for ref in kv_refs]
                delta = sum(
                    jnp.sum(p * d, axis=0, keepdims=True) for p, d in zip(probs, prob_grads)
                )
                query_grad = 0.0
                for i, (p, d, ref) in enumerate(zip(probs, prob_grads, kv_refs)):
                    score_grad = (p * (d - delta)).astype(LOW)
                    query_grad = query_grad + dot_tn(score_grad, ref[:, key_spot])
                    key_sums[i] = key_sums[i] + low_dot(score_grad, query)
                    value_sums[i] = value_sums[i] + low_dot(p.astype(LOW), grad)
                dq_ref[:, mine] = query_grad * scale
            for i, out_ref in enumerate(out_refs):
                for spot, value in ((key_spot, key_sums[i] * scale), (value_spot, value_sums[i])):
                    if held is not None and i >= 2 * chunks - 2:
                        value = value + held_refs[i - 2 * chunks + 2][:, spot]
                    out_ref[:, spot] = value.astype(out_ref.dtype)
        for i in range(3, 4 + 2 * chunks):
            results.put(i)

    kinds = [FULL] * (2 * chunks) + [LOW]
    return call(
        body,
        "attend_back",
        [*norm_ins, *parts, query, lse, *kvs, *(held or ())],
        norm_back_shapes(rows, wide) + [((rows, both), k) for k in kinds],
        [pltpu.VMEM((rows, both), LOW)],
        40 * heads * rows * rows * len(kvs) * 128 + 2 * rows * both * wide,
        2 * heads * rows * rows * len(kvs),
        (core,),
    )


def project_back(dq, own, came, cosine, sine, parts):
    rows, both = dq.shape
    wide = 2 * parts[0].shape[0]
    q_width, half = both // 2, wide // 2

    def body(stream, results):
        cos_ref, sin_ref, dq_ref, own_ref, came_ref = stream.take(5)
        proj_ref, part_ref = results.buffers
        for side in range(2):
            here = slice(side * q_width, (side + 1) * q_width)
            rest = own_ref[:, here] + came_ref[:, here].astype(FULL)
            flat = jnp.concatenate([dq_ref[:, here], rest], axis=1)
            query, rest = turn(flat, cos_ref[...], -sin_ref[...])
            start = 2 * side * q_width
            proj_ref[:, start : start + q_width] = query.astype(LOW)
            proj_ref[:, start + q_width : start + 2 * q_width] = rest.astype(LOW)
        results.put(0)
        for side in range(2):
            own_w, other_w = stream.take(2)
            total = dot_nt(proj_ref[:, : 2 * q_width], own_w[...])
            total = total + dot_nt(proj_ref[:, 2 * q_width :], other_w[...])
            part_ref[:, side * half : (side + 1) * half] = total.astype(LOW)
        results.put(1)

    return call(
        body,
        "project_back",
        [cosine, sine, dq, own, came, parts[0], parts[2], parts[1], parts[3]],
        [((rows, 2 * both), LOW), ((rows, wide), LOW)],
        [],
        4 * rows * wide * both,
    )


def feed_forward(hidden, pair, gain, pair_parts, down_parts):
    rows, wide = hidden.shape
    ff = down_parts[0].shape[0]
    half = wide // 2

    def body(stream, results):
        refs = stream.take(3)
        (gain_ref,) = stream.take(1)
        put_norm(refs, gain_ref, results, 0)
        tokens = results.buffers[2][...]
        gate_ref, up_ref, inner_ref, part_ref = results.buffers[3:]
        for side in range(2):
            here = slice(side * ff, (side + 1) * ff)
            first, second = stream.take(2)
            gate = half_dots(tokens, first[...], second[...])
            gate_ref[:, here] = gate.astype(LOW)
            gate = gate * jax.nn.sigmoid(gate)
            first, second = stream.take(2)
            up = half_dots(tokens, first[...], second[...])
            up_ref[:, here] = up.astype(LOW)
            inner_ref[:, here] = (gate * up).astype(LOW)
        for i in range(3, 6):
            results.put(i)
        for side in range(2):
            own, other = stream.take(2)
            total = low_dot(inner_ref[:, :ff], own[...])
            total = total + dot_nt(inner_ref[:, ff:], other[...])
            part_ref[:, side * half : (side + 1) * half] = total.astype(LOW)
        results.put(6)

    return call(
        body,
        "feed_forward",
        [hidden, *pair, gain, *pair_parts, *[down_parts[i] for i in (0, 2, 1, 3)]],
        norm_shapes(rows, wide) + [((rows, 2 * ff), LOW)] * 3 + [((rows, wide), LOW)],
        [],
        12 * rows * wide * ff,
        2 * rows * ff,
    )


def feed_back(norm_ins, gate, up, pair_parts, down_parts):
    rows, wide = norm_ins[0].shape
    ff = down_parts[0].shape[0]
    half = wide // 2
    first_layer = len(norm_ins) == 1
    order = (0, 2, 4, 6, 1, 3, 5, 7)
    base = 0 if first_layer else 3

    def body(stream, results):
        ins = stream.take(len(norm_ins))
        if first_layer:
            x_ref = ins[0]
        else:
            put_norm_back(ins, results, 0)
            x_ref = results.buffers[1]
        grad_ref, part_ref = results.buffers[base:]
        gate_ref, up_ref = stream.take(2)
        for side in range(2):
            here = slice(side * ff, (side + 1) * ff)
            first, second = stream.take(2)
            times = low_dot if side else dot_nt
            inner_grad = times(x_ref[:, :half], first[...])
            inner_grad = inner_grad + times(x_ref[:, half:], second[...])
            gate, up = gate_ref[:, here].astype(FULL), up_ref[:, here].astype(FULL)
            sigma = jax.nn.sigmoid(gate)
            grad_sigma = inner_grad * sigma
            start = 2 * side * ff
            grad_ref[:, start : start + ff] = (
                grad_sigma * up * (1.0 + gate * (1.0 - sigma))
            ).astype(LOW)
            grad_ref[:, start + ff : start + 2 * ff] = (grad_sigma * gate).astype(LOW)
        results.put(base)
        for side in range(2):
            total = 0.0
            for i in range(4):
                (weight,) = stream.take(1)
                total = total + dot_nt(grad_ref[:, i * ff : (i + 1) * ff], weight[...])
            part_ref[:, side * half : (side + 1) * half] = total.astype(LOW)
        results.put(base + 1)

    return call(
        body,
        "feed_back",
        [*norm_ins, gate, up, *down_parts, *[pair_parts[i] for i in order]],
        ([] if first_layer else norm_back_shapes(rows, wide))
        + [((rows, 4 * ff), LOW), ((rows, wide), LOW)],
        [],
        12 * rows * wide * ff,
        2 * rows * ff,
    )


def ff_weights_kernel(chunks, split, *refs):
    xb_refs, bb_refs, dg_refs, in_refs = [refs[i * chunks : (i + 1) * chunks] for i in range(4)]
    first_ref, second_ref, turned_ref = refs[4 * chunks :]
    j = pl.program_id(0)
    rows = xb_refs[0].shape[0]
    half = first_ref.shape[0]

    def take(x_refs):
        for i, ref in enumerate(x_refs):
            turned_ref[:, i * rows : (i + 1) * rows] = ref[...].T

    def work(y_refs):
        grads = jnp.concatenate([ref[...] for ref in y_refs], axis=0)
        second_ref[...] = low_dot(turned_ref[half:, :], grads).astype(LOW)
        first_ref[...] = low_dot(turned_ref[:half, :], grads).astype(LOW)

    @pl.when(j == 0)
    def _():
        take(xb_refs)

    @pl.when(j == split)
    def _():
        take(bb_refs)

    @pl.when(j < split)
    def _():
        work(dg_refs)

    @pl.when(j >= split)
    def _():
        work(in_refs)


def ff_weights(all_b, branch_b, grads, inner):
    chunks = len(all_b)
    rows, wide = all_b[0].shape
    ff = inner[0].shape[1] // 2
    step = min(512, ff)
    n = ff // step
    split = 4 * n
    full = whole((rows, wide))
    grad = pl.BlockSpec((rows, step), lambda j: (0, jnp.minimum(j, split - 1)))
    last = pl.BlockSpec((rows, step), lambda j: (0, jnp.maximum(j - split, 0)))

    def place(j):
        k = j - split
        early = jnp.where(j < 2 * n, j, j + n)
        late = jnp.where(k < n, 2 * n + k, 4 * n + k)
        return (0, jnp.where(j < split, early, late))

    out = pl.BlockSpec((wide // 2, step), place)
    shape = jax.ShapeDtypeStruct((wide // 2, 6 * ff), LOW)
    return pl.pallas_call(
        functools.partial(ff_weights_kernel, chunks, split),
        grid=(6 * n,),
        in_specs=[full] * (2 * chunks) + [grad] * chunks + [last] * chunks,
        out_specs=[out, out],
        scratch_shapes=[pltpu.VMEM((wide, rows * chunks), LOW)],
        out_shape=[shape, shape],
        compiler_params=limits(),
        cost_estimate=cost(12 * chunks * rows * wide * ff, 12 * wide * ff + 8 * chunks * rows * wide),
        name="ff_weights",
    )(*all_b, *branch_b, *grads, *inner)


def in_weights_kernel(chunks, *refs):
    xa_refs, ba_refs, dp_refs, at_refs = [refs[i * chunks : (i + 1) * chunks] for i in range(4)]
    first_ref, second_ref = refs[4 * chunks :]
    width = dp_refs[0].shape[1] // 2
    q_width = at_refs[0].shape[1] // 2
    half = first_ref.shape[0]
    for x_refs, y_refs, size, base in (
        (xa_refs, dp_refs, width, 0),
        (ba_refs, at_refs, q_width, width),
    ):
        turned = jnp.concatenate([ref[...].T for ref in x_refs], axis=1)
        for side in range(2):
            grads = jnp.concatenate(
                [ref[:, side * size : (side + 1) * size] for ref in y_refs], axis=0
            )
            start = side * (width + q_width) + base
            second_ref[:, start : start + size] = low_dot(turned[half:], grads).astype(LOW)
            first_ref[:, start : start + size] = low_dot(turned[:half], grads).astype(LOW)


def in_weights(all_a, branch_a, grads, attended):
    chunks = len(all_a)
    rows, wide = all_a[0].shape
    width = grads[0].shape[1] + attended[0].shape[1]
    operands = list(all_a) + list(branch_a) + list(grads) + list(attended)
    shape = (wide // 2, width)
    return pl.pallas_call(
        functools.partial(in_weights_kernel, chunks),
        grid=(1,),
        in_specs=[whole(v.shape) for v in operands],
        out_specs=[whole(shape)] * 2,
        out_shape=[jax.ShapeDtypeStruct(shape, LOW)] * 2,
        compiler_params=limits(),
        cost_estimate=cost(
            2 * chunks * rows * wide * width, 2 * wide * width + 4 * chunks * rows * wide
        ),
        name="in_weights",
    )(*operands)


def role_sum_kernel(row_ref, side_ref, left_ref, right_ref, *outs):
    step = pl.program_id(0)
    total = (left_ref[...].astype(FULL) + right_ref[...].astype(FULL)).astype(LOW)
    for i, out_ref in enumerate(outs):

        @pl.when(step // 2 == i)
        def _(out_ref=out_ref):
            out_ref[...] = total


def role_sums(place, left, right):
    rows, both = left.shape[0] // 4, left.shape[1]
    width = both // 2
    picks = [pick for role in ROLES for pick in role]
    row = place ^ jnp.array([m for m, _ in picks], jnp.int32)
    side = jnp.array([s for _, s in picks], jnp.int32)
    block = pl.BlockSpec((rows, width), lambda i, r, s: (r[i], s[i]))

    def out(k):
        return pl.BlockSpec((rows, width), lambda i, r, s: (jnp.where(i > 2 * k, 1, 0), 0))

    return pl.pallas_call(
        role_sum_kernel,
        grid_spec=pltpu.PrefetchScalarGridSpec(
            num_scalar_prefetch=2,
            grid=(8,),
            in_specs=[block, block],
            out_specs=[out(k) for k in range(4)],
        ),
        out_shape=[jax.ShapeDtypeStruct((2 * rows, width), LOW)] * 4,
        compiler_params=limits(),
        cost_estimate=cost(0, 12 * rows * both),
        name="role_sums",
    )(row, side, left, right)


def cut_kernel(place_ref, gate_ref, up_ref, down_ref, *refs):
    outs, turned_ref = refs[:3], refs[3]
    turned_ref[...] = down_ref[...].T
    outs[0][...] = gate_ref[...]
    outs[1][...] = up_ref[...]
    rows = outs[2].shape[0]
    start = pl.multiple_of(place_ref[0] * rows, rows)
    outs[2][...] = turned_ref[pl.ds(start, rows), :]


def cut_ff(place, layer, gate, up, down):
    wide, ff = gate.shape[1:]
    rows = wide // lax.axis_size("dp")
    block = pl.BlockSpec((None, rows, ff), lambda i, p: (layer, p[0], 0))
    return pl.pallas_call(
        cut_kernel,
        grid_spec=pltpu.PrefetchScalarGridSpec(
            num_scalar_prefetch=1,
            grid=(1,),
            in_specs=[block, block, pl.BlockSpec((None, ff, wide), lambda i, p: (layer, 0, 0))],
            out_specs=[whole((rows, ff))] * 3,
            scratch_shapes=[pltpu.VMEM((wide, ff), LOW)],
        ),
        out_shape=[jax.ShapeDtypeStruct((rows, ff), LOW)] * 3,
        compiler_params=limits(),
        cost_estimate=cost(0, 4 * wide * ff),
        name="cut_ff",
    )(place, gate, up, down)


def cut_in_kernel(place_ref, q_ref, k_ref, v_ref, o_ref, out_ref):
    rows, q_width = q_ref.shape
    kv_width = k_ref.shape[1]
    out_ref[:rows, :q_width] = q_ref[...]
    out_ref[:rows, q_width : q_width + kv_width] = k_ref[...]
    out_ref[:rows, q_width + kv_width :] = v_ref[...]
    out_ref[rows:, :] = o_ref[...]


def cut_in(place, layer, query, key, value, out):
    count = lax.axis_size("dp")
    blocks = [(v.shape[1] // count, v.shape[2]) for v in (query, key, value, out)]
    shape = (blocks[0][0] + blocks[3][0], blocks[3][1])
    return pl.pallas_call(
        cut_in_kernel,
        grid_spec=pltpu.PrefetchScalarGridSpec(
            num_scalar_prefetch=1,
            grid=(1,),
            in_specs=[pl.BlockSpec((None,) + b, lambda i, p: (layer, p[0], 0)) for b in blocks],
            out_specs=whole(shape),
        ),
        out_shape=jax.ShapeDtypeStruct(shape, LOW),
        compiler_params=limits(),
        cost_estimate=cost(0, 4 * shape[0] * shape[1]),
        name="cut_in",
    )(place, query, key, value, out)


def pick_kernel(hi_ref, block_ref, mine_ref, other_ref):
    first, second = block_ref[:, 0, :], block_ref[:, 1, :]
    mine_ref[...] = jnp.where(hi_ref[0] == 0, first, second)
    other_ref[...] = jnp.where(hi_ref[0] == 0, second, first)


def pick(hi, block):
    rows, _, width = block.shape
    return pl.pallas_call(
        pick_kernel,
        grid_spec=pltpu.PrefetchScalarGridSpec(
            num_scalar_prefetch=1,
            grid=(1,),
            in_specs=[whole(block.shape)],
            out_specs=[whole((rows, width))] * 2,
        ),
        out_shape=[jax.ShapeDtypeStruct((rows, width), LOW)] * 2,
        compiler_params=limits(),
        cost_estimate=cost(0, 8 * rows * width),
        name="pick",
    )(hi.astype(jnp.int32).reshape(1), block)


def spread_ff_kernel(spots, place_ref, *refs):
    count = len(spots)
    gate_refs, up_refs, down_refs = [refs[i * count : (i + 1) * count] for i in range(3)]
    outs, held_ref = refs[-4:-1], refs[-1]
    put_parts(place_ref, gate_refs, spots, outs[0].at[0])
    put_parts(place_ref, up_refs, spots, outs[1].at[0])
    put_parts(place_ref, down_refs, spots, held_ref)
    outs[2][0] = held_ref[...].T


def flatten(pieces):
    parts, spots = [], []
    for m, piece in enumerate(pieces):
        piece = piece if isinstance(piece, tuple) else (piece,)
        for i, part in enumerate(piece):
            if not isinstance(part, tuple):
                part = (part, 0, part.shape[0])
            parts.append((part[0], part[1] // part[2], part[2]))
            spots.append((m, i, len(piece)))
    return (parts, spots)


def put_parts(place_ref, refs, spots, out_ref):
    for ref, (m, i, count) in zip(refs, spots):
        rows = ref.shape[0]
        start = 0
        if len(spots) > 1:
            start = pl.multiple_of((place_ref[0] ^ m) * (rows * count) + i * rows, rows)
        out_ref[pl.ds(start, rows), :] = ref[...].astype(FULL)


def spread_ff(place, pieces, layer, earlier):
    pieces, spots = flatten(pieces)
    count = len(pieces)
    rows, wide = pieces[0][2], pieces[0][0].shape[1]
    ff = wide // 3
    step = min(256, ff)
    steps = ff // step
    tall = rows * count

    def block(k, at):
        return pl.BlockSpec((rows, step), lambda j, p: (at, j + k * steps))

    in_specs = [block(k, at) for k in range(3) for _, at, _ in pieces]
    operands = [array for array, _, _ in pieces] * 3
    aliases = {}
    if earlier is not None:
        aliases = {1 + len(operands) + i: i for i in range(3)}
        in_specs += [pl.BlockSpec(memory_space=pl.ANY)] * 3
        operands += list(earlier)

    def kernel(place_ref, *refs):
        refs = refs[: 3 * count] + refs[len(operands) :]
        spread_ff_kernel(spots, place_ref, *refs)

    tall_out = pl.BlockSpec((1, tall, step), lambda j, p: (layer, 0, j))
    flat_out = pl.BlockSpec((1, step, tall), lambda j, p: (layer, j, 0))
    return pl.pallas_call(
        kernel,
        grid_spec=pltpu.PrefetchScalarGridSpec(
            num_scalar_prefetch=1,
            grid=(steps,),
            in_specs=in_specs,
            out_specs=[tall_out, tall_out, flat_out],
            scratch_shapes=[pltpu.VMEM((tall, step), FULL)],
        ),
        out_shape=[
            jax.ShapeDtypeStruct((LAYERS, tall, ff), FULL),
            jax.ShapeDtypeStruct((LAYERS, tall, ff), FULL),
            jax.ShapeDtypeStruct((LAYERS, ff, tall), FULL),
        ],
        input_output_aliases=aliases,
        compiler_params=limits(),
        cost_estimate=cost(0, 18 * tall * ff),
        name="spread_ff",
    )(place, *operands)


def spread_in(place, pieces, layer, earlier, q_width):
    pieces, spots = flatten(pieces)
    count = len(pieces)
    rows, width = pieces[0][2], pieces[0][0].shape[1]
    tall = rows * count
    kv_width = q_width // 2
    operands = [array for array, _, _ in pieces]
    in_specs = [pl.BlockSpec((rows, width), lambda j, p, at=at: (at, 0)) for _, at, _ in pieces]
    aliases = {}
    if earlier is not None:
        aliases = {1 + count + i: i for i in range(4)}
        in_specs = in_specs + [pl.BlockSpec(memory_space=pl.ANY)] * 4
        operands += list(earlier)

    def kernel(place_ref, *refs):
        piece_refs, (q_ref, k_ref, v_ref, o_ref, held_ref) = refs[:count], refs[len(operands) :]
        put_parts(place_ref, piece_refs, spots, held_ref)
        at = 0
        for out_ref, size in ((q_ref, q_width), (k_ref, kv_width), (v_ref, kv_width)):
            out_ref[0] = held_ref[:, at : at + size]
            at += size
        o_ref[0] = held_ref[:, at:].T

    sizes = [(tall, q_width), (tall, kv_width), (tall, kv_width), (q_width, tall)]
    return pl.pallas_call(
        kernel,
        grid_spec=pltpu.PrefetchScalarGridSpec(
            num_scalar_prefetch=1,
            grid=(1,),
            in_specs=in_specs,
            out_specs=[pl.BlockSpec((1,) + s, lambda j, p: (layer, 0, 0)) for s in sizes],
            scratch_shapes=[pltpu.VMEM((tall, width), FULL)],
        ),
        out_shape=[jax.ShapeDtypeStruct((LAYERS,) + s, FULL) for s in sizes],
        input_output_aliases=aliases,
        compiler_params=limits(),
        cost_estimate=cost(0, 6 * tall * width),
        name="spread_in",
    )(place, *operands)


def gather_kernel(count, tops, place_ref, *refs):
    piece_refs, out_ref = refs[:count], refs[count]
    for m, ref in enumerate(piece_refs):
        row, part_row = 0, 0
        for size in tops:
            part = size // count
            start = pl.multiple_of(row + (place_ref[0] ^ m) * part, part)
            out_ref[pl.ds(start, part), :] = ref[part_row : part_row + part, :]
            row += size
            part_row += part


def gather_pieces(place, pieces, tops):
    count = len(pieces)
    shape = (sum(tops), pieces[0].shape[1])
    return pl.pallas_call(
        functools.partial(gather_kernel, count, tops),
        grid_spec=pltpu.PrefetchScalarGridSpec(
            num_scalar_prefetch=1,
            grid=(1,),
            in_specs=[whole(p.shape) for p in pieces],
            out_specs=whole(shape),
        ),
        out_shape=jax.ShapeDtypeStruct(shape, LOW),
        compiler_params=limits(),
        cost_estimate=cost(0, 4 * shape[0] * shape[1]),
        name="gather_pieces",
    )(place, *pieces)


def cut(weight, layer, place):
    rows = weight.shape[1] // lax.axis_size("dp")
    start = (jnp.int32(layer), place * rows, jnp.int32(0))
    return lax.dynamic_slice(weight, start, (1, rows, weight.shape[2]))[0]


class Group:
    def __init__(self, piece, tops, place):
        self.piece, self.tops, self.place = piece, tops, place
        self.count = lax.axis_size("dp")
        self.even = all(size // self.count % 16 == 0 for size in tops)

    def fetch(self, order):
        self.piece = flip_hi(order.after(self.piece))

    def gather(self, order):
        order.join(self.piece)
        piece = order.after(self.piece)
        if len(self.tops) == 1:
            self.first = lax.all_gather(piece, "dp", axis=0, tiled=True)
            return
        pieces = lax.all_gather(piece, "dp", axis=0)
        at, rows = 0, []
        for size in self.tops:
            part = size // self.count
            rows.append(pieces[:, at : at + part].reshape(size, -1))
            at += part
        self.first = jnp.concatenate(rows, axis=0)

    def cross(self, order, gated=False):
        first = order.after(self.first) if gated else self.first
        self.halves = (first, flip_core(first))

    def spread(self, order, near=(1, 2)):
        order.join(self.piece)
        if self.even:
            piece = order.after(self.piece)
            self.pieces = [piece] + [hop(piece, "dp", m) for m in near]
        else:
            self.gather(order)

    def spread_on(self, order):
        if self.even:
            order.join(*self.pieces[1:])
            piece = order.after(self.pieces[0])
            self.pieces += [hop(piece, "dp", m) for m in range(len(self.pieces), self.count)]

    def collect(self, order):
        if self.even:
            spot = self.place.astype(jnp.int32).reshape(1)
            order.join(*self.pieces[1:])
            pieces = [order.after(self.pieces[0])] + self.pieces[1:]
            self.first = gather_pieces(spot, pieces, self.tops)
        order.mark(self.first)
        self.halves = (self.first, flip_core(self.first))

    def done(self, order):
        order.join(self.halves[1])


def in_groups(layer, w_query, w_key, w_value, w_out, place):
    wide, q_width = w_query.shape[1:]
    width = q_width + 2 * w_key.shape[2]
    count = lax.axis_size("dp")
    if width == w_out.shape[2] and q_width // count % 16 == 0:
        spot = place.astype(jnp.int32).reshape(1)
        piece = cut_in(spot, layer, w_query, w_key, w_value, w_out)
        return [Group(piece, (wide, q_width), place)]
    piece = jnp.concatenate([cut(v, layer, place) for v in (w_query, w_key, w_value)], axis=1)
    return [Group(piece, (wide,), place), Group(cut(w_out, layer, place), (q_width,), place)]


ROLES = (((1, 0), (3, 0)), ((2, 1), (3, 1)), ((2, 0), (1, 1)), ((0, 0), (0, 1)))


class Sum:
    def __init__(self, parts, place, by_hops):
        self.first, self.last = parts
        self.place = place
        self.even = by_hops and lax.axis_size("dp") == 4

    def flip(self, order):
        self.came = flip_core(order.after(self.last))

    def start(self, order):
        order.join(self.came)
        if not self.even:
            total = order.mark(add_low(order.after(self.first), self.came))
            self.both = lax.psum_scatter(total, "dp", scatter_dimension=0, tiled=True)
            return
        spot = self.place.astype(jnp.int32).reshape(1)
        roles = role_sums(spot, order.after(self.first), self.came)
        to_x, to_y, self.on, self.keep = order.mark(roles)
        self.from_x, self.from_y = hop(to_x, "dp", 1), hop(to_y, "dp", 2)

    def second(self, order):
        if not self.even:
            return
        rows = self.on.shape[0] // 2
        on, keep, from_x, from_y = order.after((self.on, self.keep, self.from_x, self.from_y))
        to_y = add_low(on[:rows], from_x[rows:])
        to_x = add_low(on[rows:], from_y[rows:])
        self.own = add_low(keep[:rows], from_x[:rows])
        self.other = add_low(keep[rows:], from_y[:rows])
        order.mark((to_x, to_y))
        self.to_own, self.to_other = hop(to_y, "dp", 2), hop(to_x, "dp", 1)

    def third(self, order):
        if not self.even:
            both = order.after(self.both)
            width = both.shape[1] // 2
            self.own, self.other = order.mark((both[:, :width], both[:, width:]))
            return
        order.join(self.to_own)
        other, came = order.after((self.other, self.to_other))
        self.other = order.mark(add_low(other, came))

    def across(self, order):
        self.far = flip_hi(order.after(self.other))

    def fourth(self, order):
        own, far = order.after((self.own, self.far))
        total = own.astype(FULL) + far.astype(FULL)
        if self.even:
            total = total + order.after(self.to_own).astype(FULL)
        self.total = order.mark(total.astype(LOW))

    def gather(self, order):
        total = order.after(self.total)
        self.pieces = [lax.all_gather(total, "dp", axis=0, tiled=True)]

    def straight(self, order):
        total = order.after(self.total)
        self.pieces = [total] + [hop(total, "dp", m) for m in range(1, lax.axis_size("dp"))]

    def near(self, order):
        if not self.even:
            self.gather(order)
            return
        total = order.after(self.total)
        rows = total.shape[0] // 2
        self.mine = (total[:rows], total[rows:])
        self.beside = [hop(self.mine[0], "dp", 1), hop(self.mine[1], "dp", 2)]

    def fifth(self, order):
        if not self.even:
            return
        top, bottom = self.mine
        order.join(*self.beside)
        near_x, near_y = order.after(tuple(self.beside))
        tops = order.mark(jnp.concatenate([top, near_x], axis=0))
        bottoms = order.mark(jnp.concatenate([bottom, near_y], axis=0))
        tops, bottoms = hop(tops, "dp", 2), hop(bottoms, "dp", 1)
        rows = top.shape[0]
        self.pieces = [
            (top, bottom),
            (near_x, (bottoms, 0, rows)),
            ((tops, 0, rows), near_y),
            ((tops, rows, rows), (bottoms, rows, rows)),
        ]

    def done(self, order):
        order.join(*(part for piece in self.pieces if isinstance(piece, tuple) for part in piece))


def rope_tables(positions, width):
    indices = jnp.arange(HEAD // 2, dtype=FULL)
    inverse = ROPE_BASE ** (-2.0 * indices / HEAD)
    angles = positions.astype(FULL)[:, None] * inverse[None, :]
    cosine, sine = jnp.cos(angles), jnp.sin(angles)
    heads = width // HEAD
    return (
        jnp.concatenate([cosine, cosine] * heads, axis=1),
        jnp.concatenate([-sine, sine] * heads, axis=1),
    )


def finish_back(grad, left, right, hidden, factor, gain):
    unit = hidden * factor
    grad_normed = left.astype(FULL) + right.astype(FULL)
    grad_unit = grad_normed * gain
    inner = jnp.mean(grad_unit * unit, axis=-1, keepdims=True)
    return (
        grad + factor * (grad_unit - unit * inner),
        jnp.sum(grad_normed * unit, axis=0, keepdims=True),
    )


class Arrival:
    def __init__(self, block, hi, lo, core):
        self.block, self.hi, self.lo, self.core = block, hi, lo, core

    def pick(self, order):
        self.mine, self.other = order.mark(pick(self.hi, order.after(self.block)))

    def fetch_on(self, order):
        self.far = flip_hi(order.after(self.other))

    def fetch(self, order):
        self.pick(order)
        self.fetch_on(order)

    def share(self, order):
        order.join(self.far)
        mine, far = order.after((self.mine, self.far))
        self.parts = [jnp.where(self.hi == j, mine, far) for j in range(CHUNKS)]
        order.mark(tuple(self.parts))
        self.halves = [None] * CHUNKS
        self.near = [None] * CHUNKS

    def send(self, order, j):
        self.near[j] = hop(order.after(self.parts[j]), "cols", 1)

    def cross(self, order, j):
        lo, core = self.lo, self.core
        order.join(self.near[j])
        part, near = order.after((self.parts[j], self.near[j]))
        if len(low_bits()) == 1:
            at_home = lo == core
            first = jnp.where(at_home, part, near)
            second = jnp.where(at_home, near, part)
        else:
            for bit in low_bits():
                far = near if bit == 1 else hop(part, "cols", bit)
                part = jnp.where(
                    (lo & bit) == 0,
                    jnp.concatenate([part, far], axis=0),
                    jnp.concatenate([far, part], axis=0),
                )
            half = part.shape[0] // 2
            first = lax.dynamic_slice_in_dim(part, core * half, half, 0)
            second = lax.dynamic_slice_in_dim(part, (1 - core) * half, half, 0)
        first, second = order.mark((first, second))
        self.halves[j] = (first, flip_core(second))

    def chunk(self, order, j):
        order.join(self.halves[j][1])
        return order.mark(jnp.concatenate(order.after(self.halves[j]), axis=-1))


class Departure:
    def __init__(self, results, hi, lo, core, rows):
        self.results, self.hi, self.lo, self.core, self.rows = results, hi, lo, core, rows

    def cross(self, order):
        flat = order.after([chunk for chunks in self.results for chunk in chunks])
        half = flat[0].shape[1] // 2
        self.firsts = [chunk[:, :half] for chunk in flat]
        send = jnp.concatenate([chunk[:, half:].astype(LOW) for chunk in flat], axis=0)
        self.came = flip_core(order.mark(send))

    def away(self, order):
        came = order.after(self.came)
        size = self.firsts[0].shape[0]
        parts = []
        for i, first in enumerate(self.firsts):
            second = came[i * size : (i + 1) * size].astype(FULL)
            both = jnp.where(
                self.core == 0,
                jnp.concatenate([first, second], axis=0),
                jnp.concatenate([second, first], axis=0),
            )
            parts.append(lax.dynamic_slice_in_dim(both, self.lo * self.rows, self.rows, 0))
        pairs = list(zip(parts[0::2], parts[1::2]))
        self.mine = [jnp.where(self.hi == 0, a, b) for a, b in pairs]
        others = [jnp.where(self.hi == 0, b, a).astype(LOW) for a, b in pairs]
        self.mine, send = order.mark((self.mine, jnp.concatenate(others, axis=0)))
        self.far = flip_hi(send)

    def done(self, order):
        far = order.after(self.far)
        out = []
        for i, mine in enumerate(self.mine):
            other = far[i * self.rows : (i + 1) * self.rows].astype(FULL)
            out.append(
                jnp.where(
                    self.hi == 0, jnp.stack([mine, other], axis=1), jnp.stack([other, mine], axis=1)
                )
            )
        return out


def shards(
    block_input, block_cotangent, w_query, w_key, w_value, w_out, w_gate, w_up, w_down, norm_gains
):
    low_count = lax.axis_size("cols") // 2
    core, col, place = lax.axis_index("rows"), lax.axis_index("cols"), lax.axis_index("dp")
    hi, lo = col // low_count, col % low_count
    core_ref = core.astype(jnp.int32).reshape(1)
    block_rows = block_input.shape[0]
    rows = block_rows * low_count
    q_width = w_query.shape[2]
    half = rows // 2
    tables = [
        rope_tables(jnp.arange(half, dtype=jnp.int32) + j * rows + core * half, q_width)
        for j in range(CHUNKS)
    ]
    spot = place.astype(jnp.int32).reshape(1)
    order = Order()
    w_in = jnp.concatenate([w_query, w_key, w_value], axis=2)
    wide = w_in.shape[1]
    ff = w_gate.shape[2]
    arrival = Arrival(block_input, hi, lo, core)
    arrival.fetch(order)
    a_groups = [in_groups(0, order.after(w_query), w_key, w_value, w_out, place), None]
    order.mark([group.piece for group in a_groups[0]])
    for group in a_groups[0]:
        group.fetch(order)
    in_own, out_own, gates, ups, own_downs = [
        (v, flip_core(v)) for v in (w_in, w_out, w_gate, w_up, w_down)
    ]
    gains = jnp.concatenate([norm_gains, flip_core(norm_gains)], axis=-1)
    f_groups = []
    for l in range(LAYERS):
        pieces = order.mark(cut_ff(spot, l, order.after(w_gate), w_up, w_down))
        f_groups.append([Group(piece, (wide,), place) for piece in pieces])
        order.join(*((in_own[1], gains) if not l else (out_own[1],)))
    a_groups[1] = in_groups(1, order.after(w_query), w_key, w_value, w_out, place)
    order.mark([group.piece for group in a_groups[1]])
    order.join(gates[1], ups[1])
    cotangent = Arrival(block_cotangent, hi, lo, core)
    cotangent.pick(order)
    arrival.share(order)
    for group in a_groups[0]:
        group.spread(order)
    arrival.send(order, 0)
    f_groups[0][0].fetch(order)
    for group in a_groups[0]:
        group.spread_on(order)
    arrival.cross(order, 0)
    f_groups[0][0].gather(order)
    f_groups[0][1].fetch(order)
    for group in a_groups[0]:
        group.collect(order)
    hidden = [arrival.chunk(order, 0)]
    order.join(own_downs[1])
    arrival.send(order, 1)
    f_groups[0][1].gather(order)
    for group in a_groups[0]:
        group.done(order)

    stash = [[None] * CHUNKS for _ in range(LAYERS)]
    weights = [None] * LAYERS
    pairs = [None] * CHUNKS

    def front(l, j):
        block, factor_a, normed_a, query, mine = order.mark(
            project(order.after(hidden[j]), pairs[j], gains[l, 0:1], ins, *tables[j])
        )
        kvs.extend([mine, flip_core(mine)])
        return (block, factor_a, normed_a, query)

    def middle(l, j, kept):
        order.join(kvs[2 * j + 1])
        attended, lse, part = order.mark(
            attend(core_ref, order.after(kept[3]), kvs[: 2 * j + 2], outs)
        )
        pairs[j] = group_pair(part)
        return (*kept, kvs[: 2 * j + 2], lse, attended)

    def rear(l, j, kept):
        order.join(pairs[j])
        mixed, factor_b, normed_b, gate, up, inner, part = order.mark(
            feed_forward(order.after(kept[0]), pairs[j], gains[l, 1:2], pair_parts, down_parts)
        )
        hidden[j] = mixed
        pairs[j] = group_pair(part) if l + 1 < LAYERS else part
        stash[l][j] = kept + (mixed, factor_b, normed_b, gate, up, inner)

    for l in range(LAYERS):
        more = l + 1 < LAYERS
        halves = [group.halves for group in a_groups[l]]
        if len(halves) == 1:
            ins = [Part(v, None, 0, wide) for v in halves[0]]
            outs = [Part(v, None, wide, w_out.shape[1]) for v in halves[0]]
        else:
            ins, outs = [[Part(v) for v in pair] for pair in halves]
        ins = [Part(v, l) for v in in_own] + ins
        outs = [Part(v, l) for v in out_own] + outs
        kvs, kept = [], [None] * CHUNKS
        first, second, third = f_groups[l]
        if not l:
            third.fetch(order)
            kept[0] = front(l, 0)
            arrival.cross(order, 1)
            hidden.append(arrival.chunk(order, 1))
            kept[1] = front(l, 1)
            kept[0] = middle(l, 0, kept[0])
            kept[1] = middle(l, 1, kept[1])
            third.spread(order, range(1, lax.axis_size("dp")))
            order.join(pairs[0])
            for group in a_groups[1]:
                group.fetch(order)
            order.join(pairs[1])
            first.cross(order)
            third.collect(order)
            second.cross(order)
            first.done(order)
        else:
            order.join(pairs[0])
            kept[0] = front(l, 0)
            second.gather(order)
            third.fetch(order)
            order.join(pairs[1])
            kept[1] = front(l, 1)
            kept[0] = middle(l, 0, kept[0])
            third.spread(order, range(1, lax.axis_size("dp")))
            cotangent.fetch_on(order)
            kept[1] = middle(l, 1, kept[1])
            order.join(pairs[0])
            first.cross(order, True)
            third.collect(order)
            second.cross(order)
            first.done(order)
        second.done(order)
        third.done(order)
        packs = [group.halves for group in f_groups[l]]
        pair_parts = [Part(v, l) for v in (*gates, *ups)] + [
            Part(v) for pack in packs[:2] for v in pack
        ]
        down_parts = [Part(v, l) for v in own_downs] + [Part(v) for v in packs[2]]
        weights[l] = (ins, outs, pair_parts, down_parts)
        rear(l, 0, kept[0])
        if more:
            for group in a_groups[1]:
                group.gather(order)
            f_groups[1][0].fetch(order)
        else:
            cotangent.share(order)
            cotangent.send(order, 1)
            cotangent.send(order, 0)
        order.join(pairs[1])
        rear(l, 1, kept[1])
        if not more:
            cotangent.cross(order, 1)
        if more:
            f_groups[1][0].gather(order)
            f_groups[1][1].fetch(order)
            order.join(pairs[0])
            for group in a_groups[1]:
                group.cross(order, True)
                group.done(order)
    grads = [None] * CHUNKS
    grads[1] = (cotangent.chunk(order, 1),)

    gain_a, gain_b = [0.0] * LAYERS, [0.0] * LAYERS
    sums = {}

    def ff_step(l, j):
        pair_parts, down_parts = weights[l][2:]
        gate, up, inner = stash[l][j][-3:]
        if len(grads[j]) == 1:
            branch_b = order.after(grads[j][0])
            grad_hidden = branch_b.astype(FULL)
            pair_grad, part = order.mark(feed_back((branch_b,), gate, up, pair_parts, down_parts))
        else:
            order.join(*grads[j][1:3])
            grad_hidden, branch_b, gain_part, pair_grad, part = order.mark(
                feed_back(
                    (order.after(grads[j][0]), *grads[j][1:]), gate, up, pair_parts, down_parts
                )
            )
            gain_a[l + 1] = gain_a[l + 1] + gain_part
        mixed, factor_b, normed_b = stash[l][j][7:10]
        grads[j] = (grad_hidden, *group_pair(part), mixed, factor_b, gains[l, 1:2])
        return (normed_b, branch_b, pair_grad, inner)

    def ff_grad(l, kept):
        columns = list(zip(*kept))
        columns[0] = order.after(columns[0])
        sums["ff", l] = Sum(order.mark(ff_weights(*columns)), place, l == 0)

    def attend_step(l, j, held):
        block, factor_a, normed_a, query, kvs, lse, attended = stash[l][j][:7]
        order.join(*grads[j][1:3])
        grad_mixed, branch_a, gain_part, dq, *dkvs = order.mark(
            attend_back(
                core_ref,
                (order.after(grads[j][0]), *grads[j][1:]),
                query,
                lse,
                kvs,
                held,
                weights[l][1],
            )
        )
        gain_b[l] = gain_b[l] + gain_part
        grads[j] = (grad_mixed, None, None, block, factor_a, gains[l, 0:1])
        middle = (dq, dkvs[-2], flip_core(dkvs[-1]))
        return (dkvs[:2], middle, (normed_a, branch_a, None, attended))

    def project_step(l, j, middle, kept):
        dq, mine, came = middle
        order.join(came)
        proj_grad, part = order.mark(
            project_back(order.after(dq), mine, came, *tables[j], weights[l][0])
        )
        grads[j] = (grads[j][0], *group_pair(part), *grads[j][3:])
        return kept[:2] + (proj_grad,) + kept[3:]

    def in_grad(l, kept):
        columns = list(zip(*kept))
        columns[0] = order.after(columns[0])
        sums["in", l] = Sum(order.mark(in_weights(*columns)), place, l == 0)

    l = LAYERS - 1
    kept, mids = [None] * CHUNKS, [None] * CHUNKS
    kept[1] = ff_step(l, 1)
    cotangent.cross(order, 0)
    grads[0] = (cotangent.chunk(order, 0),)
    kept[0] = ff_step(l, 0)
    ff_grad(l, kept)
    sums["ff", l].flip(order)
    held, mids[1], kept[1] = attend_step(l, 1, None)
    sums["ff", l].start(order)
    order.join(mids[1][2])
    _, mids[0], kept[0] = attend_step(l, 0, held)
    kept[1] = project_step(l, 1, mids[1], kept[1])
    kept[0] = project_step(l, 0, mids[0], kept[0])
    in_grad(l, kept)
    l = 0
    kept, mids = [None] * CHUNKS, [None] * CHUNKS
    kept[1] = ff_step(l, 1)
    kept[0] = ff_step(l, 0)
    sums["in", 1].flip(order)
    ff_grad(l, kept)
    sums["ff", 1].third(order)
    sums["ff", 1].across(order)
    sums["in", 1].start(order)
    sums["ff", 0].flip(order)
    held, mids[1], kept[1] = attend_step(l, 1, None)
    sums["ff", 0].start(order)
    _, mids[0], kept[0] = attend_step(l, 0, held)
    kept[1] = project_step(l, 1, mids[1], kept[1])
    kept[0] = project_step(l, 0, mids[0], kept[0])
    sums["ff", 1].fourth(order)
    sums["ff", 1].gather(order)
    sums["in", 1].third(order)
    in_grad(l, kept)
    for g in reversed(grads):
        order.join(*g[1:3])
    ends = [finish_back(order.after(g[0]), *g[1:]) for g in grads]
    order.mark(tuple(g for g, _ in ends))
    gain_a[0] = sum(part for _, part in ends)
    tops = [group_pair(part) for part in order.after(pairs)]
    gain_grads = [jnp.concatenate([gain_a[l], gain_b[l]], axis=0) for l in range(LAYERS)]
    grad_gains = order.after(jnp.stack(gain_grads))
    width = grad_gains.shape[-1] // 2
    gains_came = flip_core(grad_gains[..., width:])
    sums["ff", 0].second(order)
    sums["in", 0].flip(order)
    sums["in", 1].across(order)
    grad_gains = order.mark(grad_gains[..., :width] + order.after(gains_came))
    gains_came = flip_hi(grad_gains)
    sums["in", 0].start(order)
    sums["in", 1].fourth(order)
    grad_gains = order.mark(grad_gains + order.after(gains_came))
    order.join(tops)
    sums["ff", 0].third(order)
    sums["ff", 0].across(order)
    sums["in", 1].gather(order)
    hidden = [
        h + left.astype(FULL) + right.astype(FULL)
        for h, (left, right) in order.after(list(zip(hidden, tops)))
    ]
    results = Departure((hidden, [g for g, _ in ends]), hi, lo, core, block_rows)
    results.cross(order)
    gains_came = hop(grad_gains, "dp", 1)
    sums["in", 0].second(order)
    sums["ff", 0].fourth(order)
    sums["ff", 0].near(order)
    sums["in", 0].third(order)
    sums["ff", 0].fifth(order)
    sums["in", 0].across(order)
    results.away(order)
    grad_gains = order.mark(grad_gains + order.after(gains_came))
    bit = 2
    while bit < lax.axis_size("dp"):
        gains_came = hop(grad_gains, "dp", bit)
        if 2 * bit < lax.axis_size("dp"):
            grad_gains = order.mark(grad_gains + order.after(gains_came))
        bit *= 2
    ff_out = order.mark(spread_ff(order.after(spot), sums["ff", 1].pieces, 1, None))
    sums["in", 0].fourth(order)
    sums["in", 0].straight(order)
    in_out = order.mark(spread_in(order.after(spot), sums["in", 1].pieces, 1, None, q_width))
    activations, input_grad = order.mark(results.done(order))
    sums["ff", 0].done(order)
    ff_out = order.mark(spread_ff(order.after(spot), sums["ff", 0].pieces, 0, ff_out))
    in_out = spread_in(order.after(spot), sums["in", 0].pieces, 0, in_out, q_width)
    grad_gains = grad_gains + gains_came
    return (activations, input_grad, *in_out, *ff_out, grad_gains)


def solution(mesh):
    data = P("cols", "dp", "rows")
    tall = P(None, "rows", "cols")
    flat = P(None, "cols", "rows")
    gains = P(None, None, "rows")
    in_specs = (data, data, tall, tall, tall, flat, tall, tall, flat, gains)
    out_specs = (data, data, tall, tall, tall, flat, tall, tall, flat, gains)
    return jax.shard_map(
        shards, mesh=mesh, in_specs=in_specs, out_specs=out_specs, check_vma=False
    )
```

```python
import functools

import jax
import jax.numpy as jnp
from jax import lax
from jax.experimental import pallas as pl
from jax.experimental.pallas import tpu as pltpu
from jax.sharding import PartitionSpec as P

HEAD = 96
LAYERS = 2
CHUNKS = 2
EPSILON = 1e-05
ROPE_BASE = 100000.0
NEGATIVE = -1e30
LOW = jnp.bfloat16
FULL = jnp.float32
NT = (((1,), (1,)), ((), ()))
TN = (((0,), (0,)), ((), ()))
ROOM = 56 * 2**20
SCALE = 30
AHEAD = 8 * 2**20


def hop(value, axis, distance):
    size = lax.axis_size(axis)
    return lax.ppermute(value, axis, [(i, i ^ distance) for i in range(size)])


def flip_hi(value):
    return hop(value, "cols", lax.axis_size("cols") // 2)


def flip_core(value):
    return hop(value, "rows", 1)


def low_bits():
    bits, bit = [], 1
    while bit < lax.axis_size("cols") // 2:
        bits.append(bit)
        bit *= 2
    return bits


def group_pair(part):
    bits = low_bits()
    for bit in bits[:-1]:
        part = add_low(part, hop(part, "cols", bit))
    return (part, hop(part, "cols", bits[-1]))


def last_pair(part):
    cols, bits = lax.axis_size("cols"), low_bits()
    if len(bits) != 1:
        return group_pair(part)
    pairs = []
    for core in range(2):
        for col in range(cols):
            if col % 2 != core:
                pairs.append((core * cols + col, core * cols + (col ^ 1)))
    return (part, lax.ppermute(part, ("rows", "cols"), pairs))


class Order:
    def __init__(self):
        self.last = ()

    def after(self, values):
        return lax.optimization_barrier((values, self.last))[0] if self.last else values

    def mark(self, value):
        self.last = (value,)
        return value

    def join(self, *values):
        self.last = (*self.last, values)


def add_low(left, right):
    return (left.astype(FULL) + right.astype(FULL)).astype(LOW)


def low_dot(left, right):
    return jnp.dot(left, right, preferred_element_type=FULL)


def dot_nt(left, right):
    return lax.dot_general(left, right, NT, preferred_element_type=FULL)


def dot_tn(left, right):
    return lax.dot_general(left, right, TN, preferred_element_type=FULL)


def whole(shape):
    return pl.BlockSpec(shape, lambda *_: (0,) * len(shape))


def far():
    return pl.BlockSpec(memory_space=pl.ANY)


def cost(flops, size, exps=0):
    return pl.CostEstimate(
        flops=int(flops * SCALE), bytes_accessed=int(size * SCALE), transcendentals=0
    )


def limits():
    return pltpu.CompilerParams(vmem_limit_bytes=ROOM)


class Part:
    def __init__(self, array, layer=None, row=0, rows=None, column=0, columns=None):
        self.array, self.layer, self.row, self.column = array, layer, row, column
        self.shape = (rows or array.shape[-2], columns or array.shape[-1])

    def view(self, ref):
        ref = ref if self.layer is None else ref.at[self.layer]
        if self.shape == tuple(ref.shape):
            return ref
        return ref.at[pl.ds(self.row, self.shape[0]), pl.ds(self.column, self.shape[1])]

    def scratch(self):
        return pltpu.VMEM(self.shape, self.array.dtype)


class Stream:
    def __init__(self, sources, buffers, sems, ahead):
        self.copies = [
            pltpu.make_async_copy(source, buffer, sems.at[i])
            for i, (source, buffer) in enumerate(zip(sources, buffers))
        ]
        self.buffers = buffers
        self.sizes = [
            b.shape[0] * b.shape[1] * (4 if b.dtype == FULL else 2) for b in buffers
        ]
        self.ahead, self.started, self.waited = ahead, 0, 0
        self.feed()

    def feed(self):
        while self.started < len(self.copies) and (
            sum(self.sizes[self.waited : self.started]) < self.ahead
        ):
            self.copies[self.started].start()
            self.started += 1

    def take(self, count):
        first = self.waited
        for i in range(first, first + count):
            if i >= self.started:
                self.copies[i].start()
                self.started += 1
            self.copies[i].wait()
            self.waited += 1
        self.feed()
        return self.buffers[first : first + count]


class Results:
    def __init__(self, buffers, targets, sems):
        self.buffers, self.targets, self.sems = buffers, targets, sems
        self.copies = []

    def put(self, index):
        copy = pltpu.make_async_copy(
            self.buffers[index], self.targets[index], self.sems.at[index]
        )
        copy.start()
        self.copies.append(copy)

    def finish(self):
        for copy in self.copies:
            copy.wait()


def half_dots(left, first, second):
    half = left.shape[1] // 2
    return low_dot(left[:, :half], first) + low_dot(left[:, half:], second)


def turn(value, cosine, sine):
    width = value.shape[1]
    q_width = cosine.shape[1]
    ahead = pltpu.roll(value, width - HEAD // 2, 1)
    behind = pltpu.roll(value, HEAD // 2, 1)
    column = lax.broadcasted_iota(jnp.int32, value.shape, 1)
    other = jnp.where(lax.rem(column, HEAD) < HEAD // 2, ahead, behind)
    is_key = lax.broadcasted_iota(jnp.int32, cosine.shape, 1) < q_width // 2
    query = value[:, :q_width] * cosine + other[:, :q_width] * sine
    rest = value[:, q_width:] * jnp.where(is_key, cosine, 1.0)
    rest = rest + other[:, q_width:] * jnp.where(is_key, sine, 0.0)
    return (query, rest)


def put_norm(refs, gain_ref, results, at):
    sum_ref, factor_ref, normed_ref = results.buffers[at : at + 3]
    hidden = refs[0][...].astype(FULL)
    for ref in refs[1:]:
        hidden = hidden + ref[...].astype(FULL)
    factor = lax.rsqrt(jnp.mean(hidden * hidden, axis=-1, keepdims=True) + EPSILON)
    sum_ref[...] = hidden
    factor_ref[...] = factor
    normed_ref[...] = (hidden * factor * gain_ref[...]).astype(LOW)
    for i in range(3):
        results.put(at + i)


def put_norm_back(refs, results, at):
    grad_ref, left_ref, right_ref, hidden_ref, factor_ref, gain_ref = refs
    sum_ref, low_ref, gain_out_ref = results.buffers[at : at + 3]
    grad_normed = left_ref[...].astype(FULL) + right_ref[...].astype(FULL)
    factor = factor_ref[...]
    unit = hidden_ref[...] * factor
    grad_unit = grad_normed * gain_ref[...]
    inner = jnp.mean(grad_unit * unit, axis=-1, keepdims=True)
    grad = grad_ref[...].astype(FULL) + factor * (grad_unit - unit * inner)
    sum_ref[...] = grad
    low_ref[...] = grad.astype(LOW)
    gain_out_ref[...] = jnp.sum(grad_normed * unit, axis=0, keepdims=True)
    for i in range(3):
        results.put(at + i)


def norm_shapes(rows, wide):
    return [((rows, wide), FULL), ((rows, 1), FULL), ((rows, wide), LOW)]


def norm_back_shapes(rows, wide):
    return [((rows, wide), FULL), ((rows, wide), LOW), ((1, wide), FULL)]


def call(body, name, inputs, outs, scratch, flops, exps=0, scalars=(), ahead=AHEAD):
    inputs = [v if isinstance(v, Part) else Part(v) for v in inputs]
    size = sum(2 * p.shape[0] * p.shape[1] for p in inputs)
    count, made = len(inputs), len(outs)

    def kernel(*refs):
        scalar_refs, refs = refs[: len(scalars)], refs[len(scalars) :]
        sources, targets, refs = refs[:count], refs[count : count + made], refs[count + made :]
        held, buffers, refs = refs[:count], refs[count : count + made], refs[count + made :]
        in_sems, out_sems, own = refs[0], refs[1], refs[2:]
        stream = Stream([p.view(r) for p, r in zip(inputs, sources)], held, in_sems, ahead)
        results = Results(buffers, targets, out_sems)
        body(stream, results, *scalar_refs, *own)
        results.finish()

    return pl.pallas_call(
        kernel,
        grid_spec=pltpu.PrefetchScalarGridSpec(
            num_scalar_prefetch=len(scalars),
            grid=(1,),
            in_specs=[far()] * count,
            out_specs=[far()] * made,
            scratch_shapes=[p.scratch() for p in inputs]
            + [pltpu.VMEM(s, k) for s, k in outs]
            + [pltpu.SemaphoreType.DMA((count,)), pltpu.SemaphoreType.DMA((made,))]
            + list(scratch),
        ),
        out_shape=[jax.ShapeDtypeStruct(s, k) for s, k in outs],
        compiler_params=limits(),
        cost_estimate=cost(flops, size, exps),
        name=name,
    )(*scalars, *[p.array for p in inputs])


def project(hidden, pair, gain, parts, cosine, sine):
    rows, wide = hidden.shape
    q_width = cosine.shape[1]
    ins = [hidden, *(pair or ())]

    def body(stream, results):
        refs = stream.take(len(ins))
        (gain_ref,) = stream.take(1)
        put_norm(refs, gain_ref, results, 0)
        cos_ref, sin_ref = stream.take(2)
        tokens = results.buffers[2][...]
        q_ref, kv_ref = results.buffers[3:]
        for side in range(2):
            first, second = stream.take(2)
            projected = half_dots(tokens, first[...], second[...])
            query, rest = turn(projected, cos_ref[...], sin_ref[...])
            here = slice(side * q_width, (side + 1) * q_width)
            q_ref[:, here] = query.astype(LOW)
            kv_ref[:, here] = rest.astype(LOW)
        results.put(4)
        results.put(3)

    return call(
        body,
        "project",
        [*ins, gain, cosine, sine, *parts],
        norm_shapes(rows, wide) + [((rows, 2 * q_width), LOW)] * 2,
        [],
        8 * rows * wide * q_width,
    )


def score(key, query, kind):
    raw = dot_nt(key, query) * HEAD ** (-0.5)
    if kind == "own":
        key_pos = lax.broadcasted_iota(jnp.int32, raw.shape, 0)
        query_pos = lax.broadcasted_iota(jnp.int32, raw.shape, 1)
        raw = jnp.where(query_pos >= key_pos, raw, NEGATIVE)
    return raw


def offsets_of(chunks, core):
    return [0.0] * (2 * chunks - 1) + [jnp.where(core == 1, 0.0, -NEGATIVE)]


def kinds_of(chunks):
    return ["all"] * (2 * chunks - 2) + ["own", "sib"]


def attend(core, query, kvs, parts):
    rows, both = query.shape
    wide = 2 * parts[0].shape[1]
    chunks = len(kvs) // 2
    q_width, heads = both // 2, both // 2 // HEAD
    kv_width = q_width // 2

    def body(stream, results, core_ref):
        (q_ref,), kv_refs = stream.take(1), stream.take(2 * chunks)
        att_ref, lse_ref, part_ref = results.buffers
        offsets = offsets_of(chunks, core_ref[0])
        for h in range(2 * heads):
            group = (h // heads) * q_width + (h % heads) // 2 * HEAD
            mine = slice(h * HEAD, (h + 1) * HEAD)
            query = q_ref[:, mine]
            scores = [
                score(ref[:, group : group + HEAD], query, kind)
                for ref, kind in zip(kv_refs, kinds_of(chunks))
            ]
            highest = functools.reduce(
                jnp.maximum,
                [jnp.max(s, axis=0, keepdims=True) - o for s, o in zip(scores, offsets)],
            )
            exps = [jnp.exp(s - (highest + o)) for s, o in zip(scores, offsets)]
            total = sum(jnp.sum(e, axis=0, keepdims=True) for e in exps)
            share = 1.0 / total
            lse_ref[h : h + 1, :] = highest + jnp.log(total)
            spot = slice(group + kv_width, group + kv_width + HEAD)
            att = sum(
                dot_tn((e * share).astype(LOW), ref[:, spot]) for e, ref in zip(exps, kv_refs)
            )
            att_ref[:, mine] = att.astype(LOW)
        results.put(0)
        results.put(1)
        weights = stream.take(4)
        for side in range(2):
            columns = slice(side * wide // 2, (side + 1) * wide // 2)
            total = low_dot(att_ref[:, :q_width], weights[side][...])
            total = total + low_dot(att_ref[:, q_width:], weights[2 + side][...])
            part_ref[:, columns] = total.astype(LOW)
        results.put(2)

    return call(
        body,
        "attend",
        [query, *kvs, *parts],
        [((rows, both), LOW), ((2 * heads, rows), FULL), ((rows, wide), LOW)],
        [],
        16 * heads * rows * rows * len(kvs) * 128 + 2 * rows * both * wide,
        2 * heads * rows * rows * len(kvs),
        (core,),
    )


def attend_back(core, norm_ins, query, lse, kvs, held, parts):
    rows, both = query.shape
    wide = norm_ins[0].shape[1]
    chunks = len(kvs) // 2
    q_width, heads = both // 2, both // 2 // HEAD
    kv_width = q_width // 2
    half = wide // 2
    scale = HEAD ** (-0.5)

    def body(stream, results, core_ref, grad_ref):
        put_norm_back(stream.take(6), results, 0)
        g_ref = results.buffers[1]
        offsets = offsets_of(chunks, core_ref[0])
        for side in range(2):
            first, second = stream.take(2)
            grad = dot_nt(g_ref[:, :half], first[...])
            grad = grad + dot_nt(g_ref[:, half:], second[...])
            grad_ref[:, side * q_width : (side + 1) * q_width] = grad.astype(LOW)
        (q_ref,), (lse_ref,), kv_refs = stream.take(1), stream.take(1), stream.take(2 * chunks)
        held_refs = stream.take(2) if held is not None else None
        dq_ref, out_refs = results.buffers[3], results.buffers[4:]
        for first in range(0, 2 * heads, 2):
            group = (first // heads) * q_width + (first % heads) // 2 * HEAD
            key_spot = slice(group, group + HEAD)
            value_spot = slice(group + kv_width, group + kv_width + HEAD)
            key_sums, value_sums = [0.0] * len(kv_refs), [0.0] * len(kv_refs)
            for h in (first, first + 1):
                mine = slice(h * HEAD, (h + 1) * HEAD)
                query, grad, lse = q_ref[:, mine], grad_ref[:, mine], lse_ref[h : h + 1, :]
                probs = [
                    jnp.exp(score(ref[:, key_spot], query, kind) - (lse + o))
                    for ref, kind, o in zip(kv_refs, kinds_of(chunks), offsets)
                ]
                prob_grads = [dot_nt(ref[:, value_spot], grad) for ref in kv_refs]
                delta = sum(
                    jnp.sum(p * d, axis=0, keepdims=True) for p, d in zip(probs, prob_grads)
                )
                query_grad = 0.0
                for i, (p, d, ref) in enumerate(zip(probs, prob_grads, kv_refs)):
                    score_grad = (p * (d - delta)).astype(LOW)
                    query_grad = query_grad + dot_tn(score_grad, ref[:, key_spot])
                    key_sums[i] = key_sums[i] + low_dot(score_grad, query)
                    value_sums[i] = value_sums[i] + low_dot(p.astype(LOW), grad)
                dq_ref[:, mine] = query_grad * scale
            for i, out_ref in enumerate(out_refs):
                for spot, value in ((key_spot, key_sums[i] * scale), (value_spot, value_sums[i])):
                    if held is not None and i >= 2 * chunks - 2:
                        value = value + held_refs[i - 2 * chunks + 2][:, spot]
                    out_ref[:, spot] = value.astype(out_ref.dtype)
        for i in range(3, 4 + 2 * chunks):
            results.put(i)

    kinds = [FULL] * (2 * chunks) + [LOW]
    return call(
        body,
        "attend_back",
        [*norm_ins, *parts, query, lse, *kvs, *(held or ())],
        norm_back_shapes(rows, wide) + [((rows, both), k) for k in kinds],
        [pltpu.VMEM((rows, both), LOW)],
        40 * heads * rows * rows * len(kvs) * 128 + 2 * rows * both * wide,
        2 * heads * rows * rows * len(kvs),
        (core,),
    )


def project_back(dq, own, came, cosine, sine, parts):
    rows, both = dq.shape
    wide = 2 * parts[0].shape[0]
    q_width, half = both // 2, wide // 2

    def body(stream, results):
        cos_ref, sin_ref, dq_ref, own_ref, came_ref = stream.take(5)
        proj_ref, part_ref = results.buffers
        for side in range(2):
            here = slice(side * q_width, (side + 1) * q_width)
            rest = own_ref[:, here] + came_ref[:, here].astype(FULL)
            flat = jnp.concatenate([dq_ref[:, here], rest], axis=1)
            query, rest = turn(flat, cos_ref[...], -sin_ref[...])
            start = 2 * side * q_width
            proj_ref[:, start : start + q_width] = query.astype(LOW)
            proj_ref[:, start + q_width : start + 2 * q_width] = rest.astype(LOW)
        results.put(0)
        for side in range(2):
            own_w, other_w = stream.take(2)
            total = dot_nt(proj_ref[:, : 2 * q_width], own_w[...])
            total = total + dot_nt(proj_ref[:, 2 * q_width :], other_w[...])
            part_ref[:, side * half : (side + 1) * half] = total.astype(LOW)
        results.put(1)

    return call(
        body,
        "project_back",
        [cosine, sine, dq, own, came, parts[0], parts[2], parts[1], parts[3]],
        [((rows, 2 * both), LOW), ((rows, wide), LOW)],
        [],
        4 * rows * wide * both,
    )


def feed_forward(hidden, pair, gain, pair_parts, down_parts):
    rows, wide = hidden.shape
    ff = down_parts[0].shape[0]
    half = wide // 2

    def body(stream, results):
        refs = stream.take(3)
        (gain_ref,) = stream.take(1)
        put_norm(refs, gain_ref, results, 0)
        tokens = results.buffers[2][...]
        gate_ref, up_ref, inner_ref, part_ref = results.buffers[3:]
        for side in range(2):
            here = slice(side * ff, (side + 1) * ff)
            first, second = stream.take(2)
            gate = half_dots(tokens, first[...], second[...])
            gate_ref[:, here] = gate.astype(LOW)
            gate = gate * jax.nn.sigmoid(gate)
            first, second = stream.take(2)
            up = half_dots(tokens, first[...], second[...])
            up_ref[:, here] = up.astype(LOW)
            inner_ref[:, here] = (gate * up).astype(LOW)
        for i in range(3, 6):
            results.put(i)
        for side in range(2):
            own, other = stream.take(2)
            total = low_dot(inner_ref[:, :ff], own[...])
            total = total + dot_nt(inner_ref[:, ff:], other[...])
            part_ref[:, side * half : (side + 1) * half] = total.astype(LOW)
        results.put(6)

    return call(
        body,
        "feed_forward",
        [hidden, *pair, gain, *pair_parts, *[down_parts[i] for i in (0, 2, 1, 3)]],
        norm_shapes(rows, wide) + [((rows, 2 * ff), LOW)] * 3 + [((rows, wide), LOW)],
        [],
        12 * rows * wide * ff,
        2 * rows * ff,
    )


def feed_back(norm_ins, gate, up, pair_parts, down_parts):
    rows, wide = norm_ins[0].shape
    ff = down_parts[0].shape[0]
    half = wide // 2
    first_layer = len(norm_ins) == 1
    order = (0, 2, 4, 6, 1, 3, 5, 7)
    base = 0 if first_layer else 3

    def body(stream, results):
        ins = stream.take(len(norm_ins))
        if first_layer:
            x_ref = ins[0]
        else:
            put_norm_back(ins, results, 0)
            x_ref = results.buffers[1]
        grad_ref, part_ref = results.buffers[base:]
        gate_ref, up_ref = stream.take(2)
        for side in range(2):
            here = slice(side * ff, (side + 1) * ff)
            first, second = stream.take(2)
            times = low_dot if side else dot_nt
            inner_grad = times(x_ref[:, :half], first[...])
            inner_grad = inner_grad + times(x_ref[:, half:], second[...])
            gate, up = gate_ref[:, here].astype(FULL), up_ref[:, here].astype(FULL)
            sigma = jax.nn.sigmoid(gate)
            grad_sigma = inner_grad * sigma
            start = 2 * side * ff
            grad_ref[:, start : start + ff] = (
                grad_sigma * up * (1.0 + gate * (1.0 - sigma))
            ).astype(LOW)
            grad_ref[:, start + ff : start + 2 * ff] = (grad_sigma * gate).astype(LOW)
        results.put(base)
        for side in range(2):
            total = 0.0
            for i in range(4):
                (weight,) = stream.take(1)
                total = total + dot_nt(grad_ref[:, i * ff : (i + 1) * ff], weight[...])
            part_ref[:, side * half : (side + 1) * half] = total.astype(LOW)
        results.put(base + 1)

    return call(
        body,
        "feed_back",
        [*norm_ins, gate, up, *down_parts, *[pair_parts[i] for i in order]],
        ([] if first_layer else norm_back_shapes(rows, wide))
        + [((rows, 4 * ff), LOW), ((rows, wide), LOW)],
        [],
        12 * rows * wide * ff,
        2 * rows * ff,
    )


def ff_weights_kernel(chunks, split, *refs):
    xb_refs, bb_refs, dg_refs, in_refs = [refs[i * chunks : (i + 1) * chunks] for i in range(4)]
    first_ref, second_ref, turned_ref = refs[4 * chunks :]
    j = pl.program_id(0)
    rows = xb_refs[0].shape[0]
    half = first_ref.shape[0]

    def take(x_refs):
        for i, ref in enumerate(x_refs):
            turned_ref[:, i * rows : (i + 1) * rows] = ref[...].T

    def work(y_refs):
        grads = jnp.concatenate([ref[...] for ref in y_refs], axis=0)
        total = low_dot(turned_ref[...], grads)
        first_ref[...] = total[:half].astype(LOW)
        second_ref[...] = total[half:].astype(LOW)

    @pl.when(j == 0)
    def _():
        take(xb_refs)

    @pl.when(j == split)
    def _():
        take(bb_refs)

    @pl.when(j < split)
    def _():
        work(dg_refs)

    @pl.when(j >= split)
    def _():
        work(in_refs)


def ff_weights(all_b, branch_b, grads, inner):
    chunks = len(all_b)
    rows, wide = all_b[0].shape
    ff = inner[0].shape[1] // 2
    step = min(1024, ff)
    n = ff // step
    split = 4 * n
    full = whole((rows, wide))
    grad = pl.BlockSpec((rows, step), lambda j: (0, jnp.minimum(j, split - 1)))
    last = pl.BlockSpec((rows, step), lambda j: (0, jnp.maximum(j - split, 0)))

    def place(j):
        k = j - split
        early = jnp.where(j < 2 * n, j, j + n)
        late = jnp.where(k < n, 2 * n + k, 4 * n + k)
        return (0, jnp.where(j < split, early, late))

    out = pl.BlockSpec((wide // 2, step), place)
    shape = jax.ShapeDtypeStruct((wide // 2, 6 * ff), LOW)
    return pl.pallas_call(
        functools.partial(ff_weights_kernel, chunks, split),
        grid=(6 * n,),
        in_specs=[full] * (2 * chunks) + [grad] * chunks + [last] * chunks,
        out_specs=[out, out],
        scratch_shapes=[pltpu.VMEM((wide, rows * chunks), LOW)],
        out_shape=[shape, shape],
        compiler_params=limits(),
        cost_estimate=cost(12 * chunks * rows * wide * ff, 12 * wide * ff + 8 * chunks * rows * wide),
        name="ff_weights",
    )(*all_b, *branch_b, *grads, *inner)


def in_weights_kernel(chunks, *refs):
    xa_refs, ba_refs, dp_refs, at_refs = [refs[i * chunks : (i + 1) * chunks] for i in range(4)]
    first_ref, second_ref = refs[4 * chunks :]
    width = dp_refs[0].shape[1] // 2
    q_width = at_refs[0].shape[1] // 2
    half = first_ref.shape[0]
    for x_refs, y_refs, size, base in (
        (xa_refs, dp_refs, width, 0),
        (ba_refs, at_refs, q_width, width),
    ):
        turned = jnp.concatenate([ref[...].T for ref in x_refs], axis=1)
        for side in range(2):
            grads = jnp.concatenate(
                [ref[:, side * size : (side + 1) * size] for ref in y_refs], axis=0
            )
            start = side * (width + q_width) + base
            total = low_dot(turned, grads)
            first_ref[:, start : start + size] = total[:half].astype(LOW)
            second_ref[:, start : start + size] = total[half:].astype(LOW)


def in_weights(all_a, branch_a, grads, attended):
    chunks = len(all_a)
    rows, wide = all_a[0].shape
    width = grads[0].shape[1] + attended[0].shape[1]
    operands = list(all_a) + list(branch_a) + list(grads) + list(attended)
    shape = (wide // 2, width)
    return pl.pallas_call(
        functools.partial(in_weights_kernel, chunks),
        grid=(1,),
        in_specs=[whole(v.shape) for v in operands],
        out_specs=[whole(shape)] * 2,
        out_shape=[jax.ShapeDtypeStruct(shape, LOW)] * 2,
        compiler_params=limits(),
        cost_estimate=cost(
            2 * chunks * rows * wide * width, 2 * wide * width + 4 * chunks * rows * wide
        ),
        name="in_weights",
    )(*operands)


def role_sum_kernel(row_ref, side_ref, left_ref, right_ref, *outs):
    step = pl.program_id(0)
    total = left_ref[...] + right_ref[...]
    for i, out_ref in enumerate(outs):

        @pl.when(step // 2 == i)
        def _(out_ref=out_ref):
            out_ref[...] = total


def role_sums(place, left, right):
    rows, both = left.shape[0] // 4, left.shape[1]
    width = both // 2
    picks = [pick for role in ROLES for pick in role]
    row = place ^ jnp.array([m for m, _ in picks], jnp.int32)
    side = jnp.array([s for _, s in picks], jnp.int32)
    block = pl.BlockSpec((rows, width), lambda i, r, s: (r[i], s[i]))

    def out(k):
        return pl.BlockSpec((rows, width), lambda i, r, s: (jnp.where(i > 2 * k, 1, 0), 0))

    return pl.pallas_call(
        role_sum_kernel,
        grid_spec=pltpu.PrefetchScalarGridSpec(
            num_scalar_prefetch=2,
            grid=(8,),
            in_specs=[block, block],
            out_specs=[out(k) for k in range(4)],
        ),
        out_shape=[jax.ShapeDtypeStruct((2 * rows, width), LOW)] * 4,
        compiler_params=limits(),
        cost_estimate=cost(0, 12 * rows * both),
        name="role_sums",
    )(row, side, left, right)


def cut_kernel(place_ref, gate_ref, up_ref, down_ref, *refs):
    outs, turned_ref = refs[:3], refs[3]
    turned_ref[...] = down_ref[...].T
    outs[0][...] = gate_ref[...]
    outs[1][...] = up_ref[...]
    rows = outs[2].shape[0]
    start = pl.multiple_of(place_ref[0] * rows, rows)
    outs[2][...] = turned_ref[pl.ds(start, rows), :]


def cut_ff(place, layer, gate, up, down):
    wide, ff = gate.shape[1:]
    rows = wide // lax.axis_size("dp")
    block = pl.BlockSpec((None, rows, ff), lambda i, p: (layer, p[0], 0))
    return pl.pallas_call(
        cut_kernel,
        grid_spec=pltpu.PrefetchScalarGridSpec(
            num_scalar_prefetch=1,
            grid=(1,),
            in_specs=[block, block, pl.BlockSpec((None, ff, wide), lambda i, p: (layer, 0, 0))],
            out_specs=[whole((rows, ff))] * 3,
            scratch_shapes=[pltpu.VMEM((wide, ff), LOW)],
        ),
        out_shape=[jax.ShapeDtypeStruct((rows, ff), LOW)] * 3,
        compiler_params=limits(),
        cost_estimate=cost(0, 4 * wide * ff),
        name="cut_ff",
    )(place, gate, up, down)


def cut_in_kernel(place_ref, q_ref, k_ref, v_ref, o_ref, out_ref):
    rows, q_width = q_ref.shape
    kv_width = k_ref.shape[1]
    out_ref[:rows, :q_width] = q_ref[...]
    out_ref[:rows, q_width : q_width + kv_width] = k_ref[...]
    out_ref[:rows, q_width + kv_width :] = v_ref[...]
    out_ref[rows:, :] = o_ref[...]


def cut_in(place, layer, query, key, value, out):
    count = lax.axis_size("dp")
    blocks = [(v.shape[1] // count, v.shape[2]) for v in (query, key, value, out)]
    shape = (blocks[0][0] + blocks[3][0], blocks[3][1])
    return pl.pallas_call(
        cut_in_kernel,
        grid_spec=pltpu.PrefetchScalarGridSpec(
            num_scalar_prefetch=1,
            grid=(1,),
            in_specs=[pl.BlockSpec((None,) + b, lambda i, p: (layer, p[0], 0)) for b in blocks],
            out_specs=whole(shape),
        ),
        out_shape=jax.ShapeDtypeStruct(shape, LOW),
        compiler_params=limits(),
        cost_estimate=cost(0, 4 * shape[0] * shape[1]),
        name="cut_in",
    )(place, query, key, value, out)


def pick_kernel(hi_ref, block_ref, mine_ref, other_ref):
    first, second = block_ref[:, 0, :], block_ref[:, 1, :]
    mine_ref[...] = jnp.where(hi_ref[0] == 0, first, second)
    other_ref[...] = jnp.where(hi_ref[0] == 0, second, first)


def pick(hi, block):
    rows, _, width = block.shape
    return pl.pallas_call(
        pick_kernel,
        grid_spec=pltpu.PrefetchScalarGridSpec(
            num_scalar_prefetch=1,
            grid=(1,),
            in_specs=[whole(block.shape)],
            out_specs=[whole((rows, width))] * 2,
        ),
        out_shape=[jax.ShapeDtypeStruct((rows, width), LOW)] * 2,
        compiler_params=limits(),
        cost_estimate=cost(0, 8 * rows * width),
        name="pick",
    )(hi.astype(jnp.int32).reshape(1), block)


def spread_ff_kernel(spots, place_ref, *refs):
    count = len(spots)
    gate_refs, up_refs, down_refs = [refs[i * count : (i + 1) * count] for i in range(3)]
    outs, held_ref = refs[-4:-1], refs[-1]
    put_parts(place_ref, gate_refs, spots, outs[0].at[0])
    put_parts(place_ref, up_refs, spots, outs[1].at[0])
    put_parts(place_ref, down_refs, spots, held_ref)
    outs[2][0] = held_ref[...].T


def flatten(pieces):
    parts, spots = [], []
    for m, piece in enumerate(pieces):
        piece = piece if isinstance(piece, tuple) else (piece,)
        for i, part in enumerate(piece):
            if not isinstance(part, tuple):
                part = (part, 0, part.shape[0])
            parts.append((part[0], part[1] // part[2], part[2]))
            spots.append((m, i, len(piece)))
    return (parts, spots)


def put_parts(place_ref, refs, spots, out_ref):
    for ref, (m, i, count) in zip(refs, spots):
        rows = ref.shape[0]
        start = 0
        if len(spots) > 1:
            start = pl.multiple_of((place_ref[0] ^ m) * (rows * count) + i * rows, rows)
        out_ref[pl.ds(start, rows), :] = ref[...].astype(FULL)


def spread_ff(place, pieces, layer, earlier):
    pieces, spots = flatten(pieces)
    count = len(pieces)
    rows, wide = pieces[0][2], pieces[0][0].shape[1]
    ff = wide // 3
    step = min(256, ff)
    steps = ff // step
    tall = rows * count

    def block(k, at):
        return pl.BlockSpec((rows, step), lambda j, p: (at, j + k * steps))

    in_specs = [block(k, at) for k in range(3) for _, at, _ in pieces]
    operands = [array for array, _, _ in pieces] * 3
    aliases = {}
    if earlier is not None:
        aliases = {1 + len(operands) + i: i for i in range(3)}
        in_specs += [pl.BlockSpec(memory_space=pl.ANY)] * 3
        operands += list(earlier)

    def kernel(place_ref, *refs):
        refs = refs[: 3 * count] + refs[len(operands) :]
        spread_ff_kernel(spots, place_ref, *refs)

    tall_out = pl.BlockSpec((1, tall, step), lambda j, p: (layer, 0, j))
    flat_out = pl.BlockSpec((1, step, tall), lambda j, p: (layer, j, 0))
    return pl.pallas_call(
        kernel,
        grid_spec=pltpu.PrefetchScalarGridSpec(
            num_scalar_prefetch=1,
            grid=(steps,),
            in_specs=in_specs,
            out_specs=[tall_out, tall_out, flat_out],
            scratch_shapes=[pltpu.VMEM((tall, step), FULL)],
        ),
        out_shape=[
            jax.ShapeDtypeStruct((LAYERS, tall, ff), FULL),
            jax.ShapeDtypeStruct((LAYERS, tall, ff), FULL),
            jax.ShapeDtypeStruct((LAYERS, ff, tall), FULL),
        ],
        input_output_aliases=aliases,
        compiler_params=limits(),
        cost_estimate=cost(0, 18 * tall * ff),
        name="spread_ff",
    )(place, *operands)


def spread_in(place, pieces, layer, earlier, q_width):
    pieces, spots = flatten(pieces)
    count = len(pieces)
    rows, width = pieces[0][2], pieces[0][0].shape[1]
    tall = rows * count
    kv_width = q_width // 2
    operands = [array for array, _, _ in pieces]
    in_specs = [pl.BlockSpec((rows, width), lambda j, p, at=at: (at, 0)) for _, at, _ in pieces]
    aliases = {}
    if earlier is not None:
        aliases = {1 + count + i: i for i in range(4)}
        in_specs = in_specs + [pl.BlockSpec(memory_space=pl.ANY)] * 4
        operands += list(earlier)

    def kernel(place_ref, *refs):
        piece_refs, (q_ref, k_ref, v_ref, o_ref, held_ref) = refs[:count], refs[len(operands) :]
        put_parts(place_ref, piece_refs, spots, held_ref)
        at = 0
        for out_ref, size in ((q_ref, q_width), (k_ref, kv_width), (v_ref, kv_width)):
            out_ref[0] = held_ref[:, at : at + size]
            at += size
        o_ref[0] = held_ref[:, at:].T

    sizes = [(tall, q_width), (tall, kv_width), (tall, kv_width), (q_width, tall)]
    return pl.pallas_call(
        kernel,
        grid_spec=pltpu.PrefetchScalarGridSpec(
            num_scalar_prefetch=1,
            grid=(1,),
            in_specs=in_specs,
            out_specs=[pl.BlockSpec((1,) + s, lambda j, p: (layer, 0, 0)) for s in sizes],
            scratch_shapes=[pltpu.VMEM((tall, width), FULL)],
        ),
        out_shape=[jax.ShapeDtypeStruct((LAYERS,) + s, FULL) for s in sizes],
        input_output_aliases=aliases,
        compiler_params=limits(),
        cost_estimate=cost(0, 6 * tall * width),
        name="spread_in",
    )(place, *operands)


def gather_kernel(count, tops, place_ref, *refs):
    piece_refs, out_ref = refs[:count], refs[count]
    for m, ref in enumerate(piece_refs):
        row, part_row = 0, 0
        for size in tops:
            part = size // count
            start = pl.multiple_of(row + (place_ref[0] ^ m) * part, part)
            out_ref[pl.ds(start, part), :] = ref[part_row : part_row + part, :]
            row += size
            part_row += part


def gather_pieces(place, pieces, tops):
    count = len(pieces)
    shape = (sum(tops), pieces[0].shape[1])
    return pl.pallas_call(
        functools.partial(gather_kernel, count, tops),
        grid_spec=pltpu.PrefetchScalarGridSpec(
            num_scalar_prefetch=1,
            grid=(1,),
            in_specs=[whole(p.shape) for p in pieces],
            out_specs=whole(shape),
        ),
        out_shape=jax.ShapeDtypeStruct(shape, LOW),
        compiler_params=limits(),
        cost_estimate=cost(0, 4 * shape[0] * shape[1]),
        name="gather_pieces",
    )(place, *pieces)


def cut(weight, layer, place):
    rows = weight.shape[1] // lax.axis_size("dp")
    start = (jnp.int32(layer), place * rows, jnp.int32(0))
    return lax.dynamic_slice(weight, start, (1, rows, weight.shape[2]))[0]


class Group:
    def __init__(self, piece, tops, place):
        self.piece, self.tops, self.place = piece, tops, place
        self.count = lax.axis_size("dp")
        self.even = all(size // self.count % 16 == 0 for size in tops)

    def fetch(self, order):
        self.piece = flip_hi(order.after(self.piece))

    def gather(self, order):
        order.join(self.piece)
        piece = order.after(self.piece)
        if len(self.tops) == 1:
            self.first = lax.all_gather(piece, "dp", axis=0, tiled=True)
            return
        pieces = lax.all_gather(piece, "dp", axis=0)
        at, rows = 0, []
        for size in self.tops:
            part = size // self.count
            rows.append(pieces[:, at : at + part].reshape(size, -1))
            at += part
        self.first = jnp.concatenate(rows, axis=0)

    def cross(self, order, gated=False):
        first = order.after(self.first) if gated else self.first
        self.halves = (first, flip_core(first))

    def spread(self, order, near=(1, 2)):
        order.join(self.piece)
        if self.even:
            piece = order.after(self.piece)
            self.pieces = [piece] + [hop(piece, "dp", m) for m in near]
        else:
            self.gather(order)

    def spread_on(self, order):
        if self.even:
            order.join(*self.pieces[1:])
            piece = order.after(self.pieces[0])
            self.pieces += [hop(piece, "dp", m) for m in range(len(self.pieces), self.count)]

    def collect(self, order):
        if self.even:
            spot = self.place.astype(jnp.int32).reshape(1)
            order.join(*self.pieces[1:])
            pieces = [order.after(self.pieces[0])] + self.pieces[1:]
            self.first = gather_pieces(spot, pieces, self.tops)
        order.mark(self.first)
        self.halves = (self.first, flip_core(self.first))

    def done(self, order):
        order.join(self.halves[1])


def in_groups(layer, w_query, w_key, w_value, w_out, place):
    wide, q_width = w_query.shape[1:]
    width = q_width + 2 * w_key.shape[2]
    count = lax.axis_size("dp")
    if width == w_out.shape[2] and q_width // count % 16 == 0:
        spot = place.astype(jnp.int32).reshape(1)
        piece = cut_in(spot, layer, w_query, w_key, w_value, w_out)
        return [Group(piece, (wide, q_width), place)]
    piece = jnp.concatenate([cut(v, layer, place) for v in (w_query, w_key, w_value)], axis=1)
    return [Group(piece, (wide,), place), Group(cut(w_out, layer, place), (q_width,), place)]


ROLES = (((1, 0), (3, 0)), ((2, 1), (3, 1)), ((2, 0), (1, 1)), ((0, 0), (0, 1)))


class Sum:
    def __init__(self, parts, place, by_hops):
        self.first, self.last = parts
        self.place = place
        self.even = by_hops and lax.axis_size("dp") == 4

    def flip(self, order):
        self.came = flip_core(order.after(self.last))

    def start(self, order):
        order.join(self.came)
        if not self.even:
            total = order.mark(add_low(order.after(self.first), self.came))
            self.both = lax.psum_scatter(total, "dp", scatter_dimension=0, tiled=True)
            return
        spot = self.place.astype(jnp.int32).reshape(1)
        roles = role_sums(spot, order.after(self.first), self.came)
        to_x, to_y, self.on, self.keep = order.mark(roles)
        self.from_x, self.from_y = hop(to_x, "dp", 1), hop(to_y, "dp", 2)

    def second(self, order):
        if not self.even:
            return
        rows = self.on.shape[0] // 2
        on, keep, from_x, from_y = order.after((self.on, self.keep, self.from_x, self.from_y))
        to_y = add_low(on[:rows], from_x[rows:])
        to_x = add_low(on[rows:], from_y[rows:])
        self.own = add_low(keep[:rows], from_x[:rows])
        self.other = add_low(keep[rows:], from_y[:rows])
        order.mark((to_x, to_y))
        self.to_own, self.to_other = hop(to_y, "dp", 2), hop(to_x, "dp", 1)

    def third(self, order):
        if not self.even:
            both = order.after(self.both)
            width = both.shape[1] // 2
            self.own, self.other = order.mark((both[:, :width], both[:, width:]))
            return
        order.join(self.to_own)
        other, came = order.after((self.other, self.to_other))
        self.other = order.mark(add_low(other, came))

    def across(self, order):
        self.far = flip_hi(order.after(self.other))

    def fourth(self, order):
        own, far = order.after((self.own, self.far))
        total = own.astype(FULL) + far.astype(FULL)
        if self.even:
            total = total + order.after(self.to_own).astype(FULL)
        self.total = order.mark(total.astype(LOW))

    def gather(self, order):
        total = order.after(self.total)
        self.pieces = [lax.all_gather(total, "dp", axis=0, tiled=True)]

    def straight(self, order):
        total = order.after(self.total)
        self.pieces = [total] + [hop(total, "dp", m) for m in range(1, lax.axis_size("dp"))]

    def near(self, order):
        if not self.even:
            self.gather(order)
            return
        total = order.after(self.total)
        rows = total.shape[0] // 2
        self.mine = (total[:rows], total[rows:])
        self.beside = [hop(self.mine[0], "dp", 1), hop(self.mine[1], "dp", 2)]

    def fifth(self, order):
        if not self.even:
            return
        top, bottom = self.mine
        order.join(*self.beside)
        near_x, near_y = order.after(tuple(self.beside))
        tops = order.mark(jnp.concatenate([top, near_x], axis=0))
        bottoms = order.mark(jnp.concatenate([bottom, near_y], axis=0))
        tops, bottoms = hop(tops, "dp", 2), hop(bottoms, "dp", 1)
        rows = top.shape[0]
        self.pieces = [
            (top, bottom),
            (near_x, (bottoms, 0, rows)),
            ((tops, 0, rows), near_y),
            ((tops, rows, rows), (bottoms, rows, rows)),
        ]

    def done(self, order):
        order.join(*(part for piece in self.pieces if isinstance(piece, tuple) for part in piece))


def rope_tables(positions, width):
    indices = jnp.arange(HEAD // 2, dtype=FULL)
    inverse = ROPE_BASE ** (-2.0 * indices / HEAD)
    angles = positions.astype(FULL)[:, None] * inverse[None, :]
    cosine, sine = jnp.cos(angles), jnp.sin(angles)
    heads = width // HEAD
    return (
        jnp.concatenate([cosine, cosine] * heads, axis=1),
        jnp.concatenate([-sine, sine] * heads, axis=1),
    )


def finish_back(grad, left, right, hidden, factor, gain):
    unit = hidden * factor
    grad_normed = left.astype(FULL) + right.astype(FULL)
    grad_unit = grad_normed * gain
    inner = jnp.mean(grad_unit * unit, axis=-1, keepdims=True)
    return (
        grad + factor * (grad_unit - unit * inner),
        jnp.sum(grad_normed * unit, axis=0, keepdims=True),
    )


class Arrival:
    def __init__(self, block, hi, lo, core):
        self.block, self.hi, self.lo, self.core = block, hi, lo, core

    def pick(self, order):
        self.mine, self.other = order.mark(pick(self.hi, order.after(self.block)))

    def fetch_on(self, order):
        self.far = flip_hi(order.after(self.other))

    def fetch(self, order):
        self.pick(order)
        self.fetch_on(order)

    def share(self, order):
        order.join(self.far)
        mine, far = order.after((self.mine, self.far))
        self.parts = [jnp.where(self.hi == j, mine, far) for j in range(CHUNKS)]
        order.mark(tuple(self.parts))
        self.halves = [None] * CHUNKS
        self.near = [None] * CHUNKS

    def send(self, order, j):
        self.near[j] = hop(order.after(self.parts[j]), "cols", 1)

    def cross(self, order, j):
        lo, core = self.lo, self.core
        order.join(self.near[j])
        part, near = order.after((self.parts[j], self.near[j]))
        if len(low_bits()) == 1:
            at_home = lo == core
            first = jnp.where(at_home, part, near)
            second = jnp.where(at_home, near, part)
        else:
            for bit in low_bits():
                far = near if bit == 1 else hop(part, "cols", bit)
                part = jnp.where(
                    (lo & bit) == 0,
                    jnp.concatenate([part, far], axis=0),
                    jnp.concatenate([far, part], axis=0),
                )
            half = part.shape[0] // 2
            first = lax.dynamic_slice_in_dim(part, core * half, half, 0)
            second = lax.dynamic_slice_in_dim(part, (1 - core) * half, half, 0)
        first, second = order.mark((first, second))
        self.halves[j] = (first, flip_core(second))

    def chunk(self, order, j):
        order.join(self.halves[j][1])
        return order.mark(jnp.concatenate(order.after(self.halves[j]), axis=-1))


class Departure:
    def __init__(self, results, hi, lo, core, rows):
        self.results, self.hi, self.lo, self.core, self.rows = results, hi, lo, core, rows

    def cross(self, order):
        flat = order.after([chunk for chunks in self.results for chunk in chunks])
        half = flat[0].shape[1] // 2
        self.firsts = [chunk[:, :half] for chunk in flat]
        send = jnp.concatenate([chunk[:, half:].astype(LOW) for chunk in flat], axis=0)
        self.came = flip_core(order.mark(send))

    def away(self, order):
        came = order.after(self.came)
        size = self.firsts[0].shape[0]
        parts = []
        for i, first in enumerate(self.firsts):
            second = came[i * size : (i + 1) * size].astype(FULL)
            both = jnp.where(
                self.core == 0,
                jnp.concatenate([first, second], axis=0),
                jnp.concatenate([second, first], axis=0),
            )
            parts.append(lax.dynamic_slice_in_dim(both, self.lo * self.rows, self.rows, 0))
        pairs = list(zip(parts[0::2], parts[1::2]))
        self.mine = [jnp.where(self.hi == 0, a, b) for a, b in pairs]
        others = [jnp.where(self.hi == 0, b, a).astype(LOW) for a, b in pairs]
        self.mine, send = order.mark((self.mine, jnp.concatenate(others, axis=0)))
        self.far = flip_hi(send)

    def done(self, order):
        far = order.after(self.far)
        out = []
        for i, mine in enumerate(self.mine):
            other = far[i * self.rows : (i + 1) * self.rows].astype(FULL)
            out.append(
                jnp.where(
                    self.hi == 0, jnp.stack([mine, other], axis=1), jnp.stack([other, mine], axis=1)
                )
            )
        return out


def shards(
    block_input, block_cotangent, w_query, w_key, w_value, w_out, w_gate, w_up, w_down, norm_gains
):
    low_count = lax.axis_size("cols") // 2
    core, col, place = lax.axis_index("rows"), lax.axis_index("cols"), lax.axis_index("dp")
    hi, lo = col // low_count, col % low_count
    core_ref = core.astype(jnp.int32).reshape(1)
    block_rows = block_input.shape[0]
    rows = block_rows * low_count
    q_width = w_query.shape[2]
    half = rows // 2
    tables = [
        rope_tables(jnp.arange(half, dtype=jnp.int32) + j * rows + core * half, q_width)
        for j in range(CHUNKS)
    ]
    spot = place.astype(jnp.int32).reshape(1)
    order = Order()
    w_in = jnp.concatenate([w_query, w_key, w_value], axis=2)
    wide = w_in.shape[1]
    ff = w_gate.shape[2]
    arrival = Arrival(block_input, hi, lo, core)
    arrival.fetch(order)
    a_groups = [in_groups(0, order.after(w_query), w_key, w_value, w_out, place), None]
    order.mark([group.piece for group in a_groups[0]])
    for group in a_groups[0]:
        group.fetch(order)
    in_own, out_own, gates, ups, own_downs = [
        (v, flip_core(v)) for v in (w_in, w_out, w_gate, w_up, w_down)
    ]
    gains = jnp.concatenate([norm_gains, flip_core(norm_gains)], axis=-1)
    f_groups = []
    for l in range(LAYERS):
        pieces = order.mark(cut_ff(spot, l, order.after(w_gate), w_up, w_down))
        f_groups.append([Group(piece, (wide,), place) for piece in pieces])
        order.join(*((in_own[1], gains) if not l else (out_own[1],)))
    a_groups[1] = in_groups(1, order.after(w_query), w_key, w_value, w_out, place)
    order.mark([group.piece for group in a_groups[1]])
    order.join(gates[1], ups[1])
    cotangent = Arrival(block_cotangent, hi, lo, core)
    cotangent.pick(order)
    arrival.share(order)
    for group in a_groups[0]:
        group.spread(order)
    arrival.send(order, 0)
    f_groups[0][0].fetch(order)
    for group in a_groups[0]:
        group.spread_on(order)
    arrival.cross(order, 0)
    f_groups[0][0].gather(order)
    f_groups[0][1].fetch(order)
    for group in a_groups[0]:
        group.collect(order)
    hidden = [arrival.chunk(order, 0)]
    order.join(own_downs[1])
    arrival.send(order, 1)
    f_groups[0][1].gather(order)
    for group in a_groups[0]:
        group.done(order)

    stash = [[None] * CHUNKS for _ in range(LAYERS)]
    weights = [None] * LAYERS
    pairs = [None] * CHUNKS

    def front(l, j):
        block, factor_a, normed_a, query, mine = order.mark(
            project(order.after(hidden[j]), pairs[j], gains[l, 0:1], ins, *tables[j])
        )
        kvs.extend([mine, flip_core(mine)])
        return (block, factor_a, normed_a, query)

    def middle(l, j, kept):
        order.join(kvs[2 * j + 1])
        attended, lse, part = order.mark(
            attend(core_ref, order.after(kept[3]), kvs[: 2 * j + 2], outs)
        )
        pairs[j] = group_pair(part)
        return (*kept, kvs[: 2 * j + 2], lse, attended)

    def rear(l, j, kept):
        order.join(pairs[j])
        mixed, factor_b, normed_b, gate, up, inner, part = order.mark(
            feed_forward(order.after(kept[0]), pairs[j], gains[l, 1:2], pair_parts, down_parts)
        )
        hidden[j] = mixed
        pairs[j] = group_pair(part) if l + 1 < LAYERS else part
        stash[l][j] = kept + (mixed, factor_b, normed_b, gate, up, inner)

    for l in range(LAYERS):
        more = l + 1 < LAYERS
        halves = [group.halves for group in a_groups[l]]
        if len(halves) == 1:
            ins = [Part(v, None, 0, wide) for v in halves[0]]
            outs = [Part(v, None, wide, w_out.shape[1]) for v in halves[0]]
        else:
            ins, outs = [[Part(v) for v in pair] for pair in halves]
        ins = [Part(v, l) for v in in_own] + ins
        outs = [Part(v, l) for v in out_own] + outs
        kvs, kept = [], [None] * CHUNKS
        first, second, third = f_groups[l]
        if not l:
            third.fetch(order)
            kept[0] = front(l, 0)
            arrival.cross(order, 1)
            hidden.append(arrival.chunk(order, 1))
            kept[1] = front(l, 1)
            kept[0] = middle(l, 0, kept[0])
            kept[1] = middle(l, 1, kept[1])
            third.spread(order, range(1, lax.axis_size("dp")))
            order.join(pairs[0])
            for group in a_groups[1]:
                group.fetch(order)
            order.join(pairs[1])
            first.cross(order)
            for group in a_groups[1]:
                order.join(group.piece)
            third.collect(order)
            for group in a_groups[1]:
                group.gather(order)
            f_groups[1][0].fetch(order)
            second.cross(order)
            first.done(order)
        else:
            order.join(pairs[0])
            kept[0] = front(l, 0)
            second.gather(order)
            third.fetch(order)
            order.join(pairs[1])
            kept[1] = front(l, 1)
            kept[0] = middle(l, 0, kept[0])
            third.spread(order, range(1, lax.axis_size("dp")))
            cotangent.fetch_on(order)
            kept[1] = middle(l, 1, kept[1])
            order.join(pairs[0])
            first.cross(order, True)
            third.collect(order)
            second.cross(order)
            first.done(order)
        second.done(order)
        third.done(order)
        packs = [group.halves for group in f_groups[l]]
        pair_parts = [Part(v, l) for v in (*gates, *ups)] + [
            Part(v) for pack in packs[:2] for v in pack
        ]
        down_parts = [Part(v, l) for v in own_downs] + [Part(v) for v in packs[2]]
        weights[l] = (ins, outs, pair_parts, down_parts)
        rear(l, 0, kept[0])
        if not more:
            cotangent.share(order)
            cotangent.send(order, 1)
            cotangent.send(order, 0)
        order.join(pairs[1])
        rear(l, 1, kept[1])
        if not more:
            cotangent.cross(order, 1)
        if more:
            f_groups[1][0].gather(order)
            f_groups[1][1].fetch(order)
            order.join(pairs[0])
            for group in a_groups[1]:
                group.cross(order, True)
                group.done(order)
    grads = [None] * CHUNKS
    grads[1] = (cotangent.chunk(order, 1),)

    gain_a, gain_b = [0.0] * LAYERS, [0.0] * LAYERS
    sums = {}

    def ff_step(l, j):
        pair_parts, down_parts = weights[l][2:]
        gate, up, inner = stash[l][j][-3:]
        if len(grads[j]) == 1:
            branch_b = order.after(grads[j][0])
            grad_hidden = branch_b.astype(FULL)
            pair_grad, part = order.mark(feed_back((branch_b,), gate, up, pair_parts, down_parts))
        else:
            order.join(*grads[j][1:3])
            grad_hidden, branch_b, gain_part, pair_grad, part = order.mark(
                feed_back(
                    (order.after(grads[j][0]), *grads[j][1:]), gate, up, pair_parts, down_parts
                )
            )
            gain_a[l + 1] = gain_a[l + 1] + gain_part
        mixed, factor_b, normed_b = stash[l][j][7:10]
        grads[j] = (grad_hidden, *group_pair(part), mixed, factor_b, gains[l, 1:2])
        return (normed_b, branch_b, pair_grad, inner)

    def ff_grad(l, kept):
        columns = list(zip(*kept))
        columns[0] = order.after(columns[0])
        sums["ff", l] = Sum(order.mark(ff_weights(*columns)), place, l == 0)

    def attend_step(l, j, held):
        block, factor_a, normed_a, query, kvs, lse, attended = stash[l][j][:7]
        order.join(*grads[j][1:3])
        grad_mixed, branch_a, gain_part, dq, *dkvs = order.mark(
            attend_back(
                core_ref,
                (order.after(grads[j][0]), *grads[j][1:]),
                query,
                lse,
                kvs,
                held,
                weights[l][1],
            )
        )
        gain_b[l] = gain_b[l] + gain_part
        grads[j] = (grad_mixed, None, None, block, factor_a, gains[l, 0:1])
        middle = (dq, dkvs[-2], flip_core(dkvs[-1]))
        return (dkvs[:2], middle, (normed_a, branch_a, None, attended))

    def project_step(l, j, middle, kept):
        dq, mine, came = middle
        order.join(came)
        proj_grad, part = order.mark(
            project_back(order.after(dq), mine, came, *tables[j], weights[l][0])
        )
        pair = group_pair(part) if l else last_pair(part)
        grads[j] = (grads[j][0], *pair, *grads[j][3:])
        return kept[:2] + (proj_grad,) + kept[3:]

    def in_grad(l, kept):
        columns = list(zip(*kept))
        columns[0] = order.after(columns[0])
        sums["in", l] = Sum(order.mark(in_weights(*columns)), place, l == 0)

    l = LAYERS - 1
    kept, mids = [None] * CHUNKS, [None] * CHUNKS
    kept[1] = ff_step(l, 1)
    cotangent.cross(order, 0)
    grads[0] = (cotangent.chunk(order, 0),)
    kept[0] = ff_step(l, 0)
    ff_grad(l, kept)
    sums["ff", l].flip(order)
    held, mids[1], kept[1] = attend_step(l, 1, None)
    sums["ff", l].start(order)
    order.join(mids[1][2])
    _, mids[0], kept[0] = attend_step(l, 0, held)
    kept[1] = project_step(l, 1, mids[1], kept[1])
    kept[0] = project_step(l, 0, mids[0], kept[0])
    in_grad(l, kept)
    l = 0
    kept, mids = [None] * CHUNKS, [None] * CHUNKS
    kept[1] = ff_step(l, 1)
    kept[0] = ff_step(l, 0)
    sums["in", 1].flip(order)
    ff_grad(l, kept)
    sums["ff", 1].third(order)
    sums["ff", 1].across(order)
    sums["in", 1].start(order)
    sums["ff", 0].flip(order)
    held, mids[1], kept[1] = attend_step(l, 1, None)
    sums["ff", 0].start(order)
    _, mids[0], kept[0] = attend_step(l, 0, held)
    kept[1] = project_step(l, 1, mids[1], kept[1])
    kept[0] = project_step(l, 0, mids[0], kept[0])
    sums["in", 1].third(order)
    in_grad(l, kept)
    sums["ff", 1].fourth(order)
    sums["ff", 1].gather(order)
    for g in reversed(grads):
        order.join(*g[1:3])
    ends = [finish_back(order.after(g[0]), *g[1:]) for g in grads]
    order.mark(tuple(g for g, _ in ends))
    gain_a[0] = sum(part for _, part in ends)
    if len(low_bits()) == 1:
        gain_a[0] = jnp.where(lo == core, gain_a[0], 0.0)
        gain_a[0] = gain_a[0] + hop(gain_a[0], "cols", 1)
    tops = [last_pair(part) for part in order.after(pairs)]
    gain_grads = [jnp.concatenate([gain_a[l], gain_b[l]], axis=0) for l in range(LAYERS)]
    grad_gains = order.after(jnp.stack(gain_grads))
    width = grad_gains.shape[-1] // 2
    gains_came = flip_core(grad_gains[..., width:])
    sums["ff", 0].second(order)
    sums["in", 0].flip(order)
    sums["in", 1].across(order)
    grad_gains = order.mark(grad_gains[..., :width] + order.after(gains_came))
    gains_came = flip_hi(grad_gains)
    sums["in", 0].start(order)
    sums["in", 1].fourth(order)
    grad_gains = order.mark(grad_gains + order.after(gains_came))
    order.join(tops)
    hidden = [
        h + left.astype(FULL) + right.astype(FULL)
        for h, (left, right) in order.after(list(zip(hidden, tops)))
    ]
    results = Departure((hidden, [g for g, _ in ends]), hi, lo, core, block_rows)
    results.cross(order)
    sums["ff", 0].third(order)
    sums["ff", 0].across(order)
    gains_came = hop(order.after(grad_gains), "dp", 1)
    sums["in", 1].gather(order)
    sums["in", 0].second(order)
    sums["ff", 0].fourth(order)
    sums["ff", 0].near(order)
    sums["in", 0].third(order)
    sums["in", 0].across(order)
    ff_out = order.mark(spread_ff(order.after(spot), sums["ff", 1].pieces, 1, None))
    bit = 1
    while bit < lax.axis_size("dp"):
        grad_gains = order.mark(grad_gains + order.after(gains_came))
        bit *= 2
        if bit < lax.axis_size("dp"):
            gains_came = hop(grad_gains, "dp", bit)
        if bit == 2:
            sums["ff", 0].fifth(order)
            sums["in", 0].fourth(order)
            sums["in", 0].straight(order)
            results.away(order)
    in_out = order.mark(spread_in(order.after(spot), sums["in", 1].pieces, 1, None, q_width))
    sums["ff", 0].done(order)
    ff_out = order.mark(spread_ff(order.after(spot), sums["ff", 0].pieces, 0, ff_out))
    in_out = order.mark(spread_in(order.after(spot), sums["in", 0].pieces, 0, in_out, q_width))
    activations, input_grad = results.done(order)
    return (activations, input_grad, *in_out, *ff_out, grad_gains)


def solution(mesh):
    data = P("cols", "dp", "rows")
    tall = P(None, "rows", "cols")
    flat = P(None, "cols", "rows")
    gains = P(None, None, "rows")
    in_specs = (data, data, tall, tall, tall, flat, tall, tall, flat, gains)
    out_specs = (data, data, tall, tall, tall, flat, tall, tall, flat, gains)
    return jax.shard_map(
        shards, mesh=mesh, in_specs=in_specs, out_specs=out_specs, check_vma=False
    )
```

```python
import functools

import jax
import jax.numpy as jnp
from jax import lax
from jax.experimental import pallas as pl
from jax.experimental.pallas import tpu as pltpu
from jax.sharding import PartitionSpec as P

HEAD = 96
LAYERS = 2
CHUNKS = 2
EPSILON = 1e-05
ROPE_BASE = 100000.0
NEGATIVE = -1e30
LOW = jnp.bfloat16
FULL = jnp.float32
NT = (((1,), (1,)), ((), ()))
TN = (((0,), (0,)), ((), ()))
ROOM = 56 * 2**20
SCALE = 30
AHEAD = 8 * 2**20


def hop(value, axis, distance):
    size = lax.axis_size(axis)
    return lax.ppermute(value, axis, [(i, i ^ distance) for i in range(size)])


def flip_hi(value):
    return hop(value, "cols", lax.axis_size("cols") // 2)


def flip_core(value):
    return hop(value, "rows", 1)


def low_bits():
    bits, bit = [], 1
    while bit < lax.axis_size("cols") // 2:
        bits.append(bit)
        bit *= 2
    return bits


def group_pair(part):
    bits = low_bits()
    for bit in bits[:-1]:
        part = add_low(part, hop(part, "cols", bit))
    return (part, hop(part, "cols", bits[-1]))


def last_pair(part):
    cols, bits = lax.axis_size("cols"), low_bits()
    if len(bits) != 1:
        return group_pair(part)
    pairs = []
    for core in range(2):
        for col in range(cols):
            if col % 2 != core:
                pairs.append((core * cols + col, core * cols + (col ^ 1)))
    return (part, lax.ppermute(part, ("rows", "cols"), pairs))


class Order:
    def __init__(self):
        self.last = ()

    def after(self, values):
        return lax.optimization_barrier((values, self.last))[0] if self.last else values

    def mark(self, value):
        self.last = (value,)
        return value

    def join(self, *values):
        self.last = (*self.last, values)


def add_low(left, right):
    return (left.astype(FULL) + right.astype(FULL)).astype(LOW)


def low_dot(left, right):
    return jnp.dot(left, right, preferred_element_type=FULL)


def dot_nt(left, right):
    return lax.dot_general(left, right, NT, preferred_element_type=FULL)


def dot_tn(left, right):
    return lax.dot_general(left, right, TN, preferred_element_type=FULL)


def whole(shape):
    return pl.BlockSpec(shape, lambda *_: (0,) * len(shape))


def far():
    return pl.BlockSpec(memory_space=pl.ANY)


def cost(flops, size, exps=0):
    return pl.CostEstimate(
        flops=int(flops * SCALE), bytes_accessed=int(size * SCALE), transcendentals=0
    )


def limits():
    return pltpu.CompilerParams(vmem_limit_bytes=ROOM)


class Part:
    def __init__(self, array, layer=None, row=0, rows=None, column=0, columns=None):
        self.array, self.layer, self.row, self.column = array, layer, row, column
        self.shape = (rows or array.shape[-2], columns or array.shape[-1])

    def view(self, ref):
        ref = ref if self.layer is None else ref.at[self.layer]
        if self.shape == tuple(ref.shape):
            return ref
        return ref.at[pl.ds(self.row, self.shape[0]), pl.ds(self.column, self.shape[1])]

    def scratch(self):
        return pltpu.VMEM(self.shape, self.array.dtype)


class Stream:
    def __init__(self, sources, buffers, sems, ahead):
        self.copies = [
            pltpu.make_async_copy(source, buffer, sems.at[i])
            for i, (source, buffer) in enumerate(zip(sources, buffers))
        ]
        self.buffers = buffers
        self.sizes = [
            b.shape[0] * b.shape[1] * (4 if b.dtype == FULL else 2) for b in buffers
        ]
        self.ahead, self.started, self.waited = ahead, 0, 0
        self.feed()

    def feed(self):
        while self.started < len(self.copies) and (
            sum(self.sizes[self.waited : self.started]) < self.ahead
        ):
            self.copies[self.started].start()
            self.started += 1

    def take(self, count):
        first = self.waited
        for i in range(first, first + count):
            if i >= self.started:
                self.copies[i].start()
                self.started += 1
            self.copies[i].wait()
            self.waited += 1
        self.feed()
        return self.buffers[first : first + count]


class Results:
    def __init__(self, buffers, targets, sems):
        self.buffers, self.targets, self.sems = buffers, targets, sems
        self.copies = []

    def put(self, index):
        copy = pltpu.make_async_copy(
            self.buffers[index], self.targets[index], self.sems.at[index]
        )
        copy.start()
        self.copies.append(copy)

    def finish(self):
        for copy in self.copies:
            copy.wait()


def half_dots(left, first, second):
    half = left.shape[1] // 2
    return low_dot(left[:, :half], first) + low_dot(left[:, half:], second)


def turn(value, cosine, sine):
    width = value.shape[1]
    q_width = cosine.shape[1]
    ahead = pltpu.roll(value, width - HEAD // 2, 1)
    behind = pltpu.roll(value, HEAD // 2, 1)
    column = lax.broadcasted_iota(jnp.int32, value.shape, 1)
    other = jnp.where(lax.rem(column, HEAD) < HEAD // 2, ahead, behind)
    is_key = lax.broadcasted_iota(jnp.int32, cosine.shape, 1) < q_width // 2
    query = value[:, :q_width] * cosine + other[:, :q_width] * sine
    rest = value[:, q_width:] * jnp.where(is_key, cosine, 1.0)
    rest = rest + other[:, q_width:] * jnp.where(is_key, sine, 0.0)
    return (query, rest)


def put_norm(refs, gain_ref, results, at):
    sum_ref, factor_ref, normed_ref = results.buffers[at : at + 3]
    hidden = refs[0][...].astype(FULL)
    for ref in refs[1:]:
        hidden = hidden + ref[...].astype(FULL)
    factor = lax.rsqrt(jnp.mean(hidden * hidden, axis=-1, keepdims=True) + EPSILON)
    sum_ref[...] = hidden
    factor_ref[...] = factor
    normed_ref[...] = (hidden * factor * gain_ref[...]).astype(LOW)
    for i in range(3):
        results.put(at + i)


def put_norm_back(refs, results, at):
    grad_ref, left_ref, right_ref, hidden_ref, factor_ref, gain_ref = refs
    sum_ref, low_ref, gain_out_ref = results.buffers[at : at + 3]
    grad_normed = left_ref[...].astype(FULL) + right_ref[...].astype(FULL)
    factor = factor_ref[...]
    unit = hidden_ref[...] * factor
    grad_unit = grad_normed * gain_ref[...]
    inner = jnp.mean(grad_unit * unit, axis=-1, keepdims=True)
    grad = grad_ref[...].astype(FULL) + factor * (grad_unit - unit * inner)
    sum_ref[...] = grad
    low_ref[...] = grad.astype(LOW)
    gain_out_ref[...] = jnp.sum(grad_normed * unit, axis=0, keepdims=True)
    for i in range(3):
        results.put(at + i)


def norm_shapes(rows, wide):
    return [((rows, wide), FULL), ((rows, 1), FULL), ((rows, wide), LOW)]


def norm_back_shapes(rows, wide):
    return [((rows, wide), FULL), ((rows, wide), LOW), ((1, wide), FULL)]


def call(body, name, inputs, outs, scratch, flops, exps=0, scalars=(), ahead=AHEAD):
    inputs = [v if isinstance(v, Part) else Part(v) for v in inputs]
    size = sum(2 * p.shape[0] * p.shape[1] for p in inputs)
    count, made = len(inputs), len(outs)

    def kernel(*refs):
        scalar_refs, refs = refs[: len(scalars)], refs[len(scalars) :]
        sources, targets, refs = refs[:count], refs[count : count + made], refs[count + made :]
        held, buffers, refs = refs[:count], refs[count : count + made], refs[count + made :]
        in_sems, out_sems, own = refs[0], refs[1], refs[2:]
        stream = Stream([p.view(r) for p, r in zip(inputs, sources)], held, in_sems, ahead)
        results = Results(buffers, targets, out_sems)
        body(stream, results, *scalar_refs, *own)
        results.finish()

    return pl.pallas_call(
        kernel,
        grid_spec=pltpu.PrefetchScalarGridSpec(
            num_scalar_prefetch=len(scalars),
            grid=(1,),
            in_specs=[far()] * count,
            out_specs=[far()] * made,
            scratch_shapes=[p.scratch() for p in inputs]
            + [pltpu.VMEM(s, k) for s, k in outs]
            + [pltpu.SemaphoreType.DMA((count,)), pltpu.SemaphoreType.DMA((made,))]
            + list(scratch),
        ),
        out_shape=[jax.ShapeDtypeStruct(s, k) for s, k in outs],
        compiler_params=limits(),
        cost_estimate=cost(flops, size, exps),
        name=name,
    )(*scalars, *[p.array for p in inputs])


def project(hidden, pair, gain, parts, cosine, sine):
    rows, wide = hidden.shape
    q_width = cosine.shape[1]
    ins = [hidden, *(pair or ())]

    def body(stream, results):
        refs = stream.take(len(ins))
        (gain_ref,) = stream.take(1)
        put_norm(refs, gain_ref, results, 0)
        cos_ref, sin_ref = stream.take(2)
        tokens = results.buffers[2][...]
        q_ref, kv_ref = results.buffers[3:]
        for side in range(2):
            first, second = stream.take(2)
            projected = half_dots(tokens, first[...], second[...])
            query, rest = turn(projected, cos_ref[...], sin_ref[...])
            here = slice(side * q_width, (side + 1) * q_width)
            q_ref[:, here] = query.astype(LOW)
            kv_ref[:, here] = rest.astype(LOW)
        results.put(4)
        results.put(3)

    return call(
        body,
        "project",
        [*ins, gain, cosine, sine, *parts],
        norm_shapes(rows, wide) + [((rows, 2 * q_width), LOW)] * 2,
        [],
        8 * rows * wide * q_width,
    )


def score(key, query, kind):
    raw = dot_nt(key, query) * HEAD ** (-0.5)
    if kind == "own":
        key_pos = lax.broadcasted_iota(jnp.int32, raw.shape, 0)
        query_pos = lax.broadcasted_iota(jnp.int32, raw.shape, 1)
        raw = jnp.where(query_pos >= key_pos, raw, NEGATIVE)
    return raw


def offsets_of(chunks, core):
    return [0.0] * (2 * chunks - 1) + [jnp.where(core == 1, 0.0, -NEGATIVE)]


def kinds_of(chunks):
    return ["all"] * (2 * chunks - 2) + ["own", "sib"]


def attend(core, query, kvs, parts):
    rows, both = query.shape
    wide = 2 * parts[0].shape[1]
    chunks = len(kvs) // 2
    q_width, heads = both // 2, both // 2 // HEAD
    kv_width = q_width // 2

    def body(stream, results, core_ref):
        (q_ref,), kv_refs = stream.take(1), stream.take(2 * chunks)
        att_ref, lse_ref, part_ref = results.buffers
        offsets = offsets_of(chunks, core_ref[0])
        for h in range(2 * heads):
            group = (h // heads) * q_width + (h % heads) // 2 * HEAD
            mine = slice(h * HEAD, (h + 1) * HEAD)
            query = q_ref[:, mine]
            scores = [
                score(ref[:, group : group + HEAD], query, kind)
                for ref, kind in zip(kv_refs, kinds_of(chunks))
            ]
            highest = functools.reduce(
                jnp.maximum,
                [jnp.max(s, axis=0, keepdims=True) - o for s, o in zip(scores, offsets)],
            )
            exps = [jnp.exp(s - (highest + o)) for s, o in zip(scores, offsets)]
            total = sum(jnp.sum(e, axis=0, keepdims=True) for e in exps)
            share = 1.0 / total
            lse_ref[h : h + 1, :] = highest + jnp.log(total)
            spot = slice(group + kv_width, group + kv_width + HEAD)
            att = sum(
                dot_tn((e * share).astype(LOW), ref[:, spot]) for e, ref in zip(exps, kv_refs)
            )
            att_ref[:, mine] = att.astype(LOW)
        results.put(0)
        results.put(1)
        weights = stream.take(4)
        for side in range(2):
            columns = slice(side * wide // 2, (side + 1) * wide // 2)
            total = low_dot(att_ref[:, :q_width], weights[side][...])
            total = total + low_dot(att_ref[:, q_width:], weights[2 + side][...])
            part_ref[:, columns] = total.astype(LOW)
        results.put(2)

    return call(
        body,
        "attend",
        [query, *kvs, *parts],
        [((rows, both), LOW), ((2 * heads, rows), FULL), ((rows, wide), LOW)],
        [],
        16 * heads * rows * rows * len(kvs) * 128 + 2 * rows * both * wide,
        2 * heads * rows * rows * len(kvs),
        (core,),
    )


def attend_back(core, norm_ins, query, lse, kvs, held, parts):
    rows, both = query.shape
    wide = norm_ins[0].shape[1]
    chunks = len(kvs) // 2
    q_width, heads = both // 2, both // 2 // HEAD
    kv_width = q_width // 2
    half = wide // 2
    scale = HEAD ** (-0.5)

    def body(stream, results, core_ref, grad_ref):
        put_norm_back(stream.take(6), results, 0)
        g_ref = results.buffers[1]
        offsets = offsets_of(chunks, core_ref[0])
        for side in range(2):
            first, second = stream.take(2)
            grad = dot_nt(g_ref[:, :half], first[...])
            grad = grad + dot_nt(g_ref[:, half:], second[...])
            grad_ref[:, side * q_width : (side + 1) * q_width] = grad.astype(LOW)
        (q_ref,), (lse_ref,), kv_refs = stream.take(1), stream.take(1), stream.take(2 * chunks)
        held_refs = stream.take(2) if held is not None else None
        dq_ref, out_refs = results.buffers[3], results.buffers[4:]
        for first in range(0, 2 * heads, 2):
            group = (first // heads) * q_width + (first % heads) // 2 * HEAD
            key_spot = slice(group, group + HEAD)
            value_spot = slice(group + kv_width, group + kv_width + HEAD)
            key_sums, value_sums = [0.0] * len(kv_refs), [0.0] * len(kv_refs)
            for h in (first, first + 1):
                mine = slice(h * HEAD, (h + 1) * HEAD)
                query, grad, lse = q_ref[:, mine], grad_ref[:, mine], lse_ref[h : h + 1, :]
                probs = [
                    jnp.exp(score(ref[:, key_spot], query, kind) - (lse + o))
                    for ref, kind, o in zip(kv_refs, kinds_of(chunks), offsets)
                ]
                prob_grads = [dot_nt(ref[:, value_spot], grad) for ref in kv_refs]
                delta = sum(
                    jnp.sum(p * d, axis=0, keepdims=True) for p, d in zip(probs, prob_grads)
                )
                query_grad = 0.0
                for i, (p, d, ref) in enumerate(zip(probs, prob_grads, kv_refs)):
                    score_grad = (p * (d - delta)).astype(LOW)
                    query_grad = query_grad + dot_tn(score_grad, ref[:, key_spot])
                    key_sums[i] = key_sums[i] + low_dot(score_grad, query)
                    value_sums[i] = value_sums[i] + low_dot(p.astype(LOW), grad)
                dq_ref[:, mine] = query_grad * scale
            for i, out_ref in enumerate(out_refs):
                for spot, value in ((key_spot, key_sums[i] * scale), (value_spot, value_sums[i])):
                    if held is not None and i >= 2 * chunks - 2:
                        value = value + held_refs[i - 2 * chunks + 2][:, spot]
                    out_ref[:, spot] = value.astype(out_ref.dtype)
        for i in range(3, 4 + 2 * chunks):
            results.put(i)

    kinds = [FULL] * (2 * chunks) + [LOW]
    return call(
        body,
        "attend_back",
        [*norm_ins, *parts, query, lse, *kvs, *(held or ())],
        norm_back_shapes(rows, wide) + [((rows, both), k) for k in kinds],
        [pltpu.VMEM((rows, both), LOW)],
        40 * heads * rows * rows * len(kvs) * 128 + 2 * rows * both * wide,
        2 * heads * rows * rows * len(kvs),
        (core,),
    )


def project_back(dq, own, came, cosine, sine, parts):
    rows, both = dq.shape
    wide = 2 * parts[0].shape[0]
    q_width, half = both // 2, wide // 2

    def body(stream, results):
        cos_ref, sin_ref, dq_ref, own_ref, came_ref = stream.take(5)
        proj_ref, part_ref = results.buffers
        for side in range(2):
            here = slice(side * q_width, (side + 1) * q_width)
            rest = own_ref[:, here] + came_ref[:, here].astype(FULL)
            flat = jnp.concatenate([dq_ref[:, here], rest], axis=1)
            query, rest = turn(flat, cos_ref[...], -sin_ref[...])
            start = 2 * side * q_width
            proj_ref[:, start : start + q_width] = query.astype(LOW)
            proj_ref[:, start + q_width : start + 2 * q_width] = rest.astype(LOW)
        results.put(0)
        for side in range(2):
            own_w, other_w = stream.take(2)
            total = dot_nt(proj_ref[:, : 2 * q_width], own_w[...])
            total = total + dot_nt(proj_ref[:, 2 * q_width :], other_w[...])
            part_ref[:, side * half : (side + 1) * half] = total.astype(LOW)
        results.put(1)

    return call(
        body,
        "project_back",
        [cosine, sine, dq, own, came, parts[0], parts[2], parts[1], parts[3]],
        [((rows, 2 * both), LOW), ((rows, wide), LOW)],
        [],
        4 * rows * wide * both,
    )


def feed_forward(hidden, pair, gain, pair_parts, down_parts):
    rows, wide = hidden.shape
    ff = down_parts[0].shape[0]
    half = wide // 2

    def body(stream, results):
        refs = stream.take(3)
        (gain_ref,) = stream.take(1)
        put_norm(refs, gain_ref, results, 0)
        tokens = results.buffers[2][...]
        gate_ref, up_ref, inner_ref, part_ref = results.buffers[3:]
        for side in range(2):
            here = slice(side * ff, (side + 1) * ff)
            first, second = stream.take(2)
            gate = half_dots(tokens, first[...], second[...])
            gate_ref[:, here] = gate.astype(LOW)
            gate = gate * jax.nn.sigmoid(gate)
            first, second = stream.take(2)
            up = half_dots(tokens, first[...], second[...])
            up_ref[:, here] = up.astype(LOW)
            inner_ref[:, here] = (gate * up).astype(LOW)
        for i in range(3, 6):
            results.put(i)
        for side in range(2):
            own, other = stream.take(2)
            total = low_dot(inner_ref[:, :ff], own[...])
            total = total + dot_nt(inner_ref[:, ff:], other[...])
            part_ref[:, side * half : (side + 1) * half] = total.astype(LOW)
        results.put(6)

    return call(
        body,
        "feed_forward",
        [hidden, *pair, gain, *pair_parts, *[down_parts[i] for i in (0, 2, 1, 3)]],
        norm_shapes(rows, wide) + [((rows, 2 * ff), LOW)] * 3 + [((rows, wide), LOW)],
        [],
        12 * rows * wide * ff,
        2 * rows * ff,
    )


def feed_back(norm_ins, gate, up, pair_parts, down_parts):
    rows, wide = norm_ins[0].shape
    ff = down_parts[0].shape[0]
    half = wide // 2
    first_layer = len(norm_ins) == 1
    order = (0, 2, 4, 6, 1, 3, 5, 7)
    base = 0 if first_layer else 3

    def body(stream, results):
        ins = stream.take(len(norm_ins))
        if first_layer:
            x_ref = ins[0]
        else:
            put_norm_back(ins, results, 0)
            x_ref = results.buffers[1]
        grad_ref, part_ref = results.buffers[base:]
        gate_ref, up_ref = stream.take(2)
        for side in range(2):
            here = slice(side * ff, (side + 1) * ff)
            first, second = stream.take(2)
            times = low_dot if side else dot_nt
            inner_grad = times(x_ref[:, :half], first[...])
            inner_grad = inner_grad + times(x_ref[:, half:], second[...])
            gate, up = gate_ref[:, here].astype(FULL), up_ref[:, here].astype(FULL)
            sigma = jax.nn.sigmoid(gate)
            grad_sigma = inner_grad * sigma
            start = 2 * side * ff
            grad_ref[:, start : start + ff] = (
                grad_sigma * up * (1.0 + gate * (1.0 - sigma))
            ).astype(LOW)
            grad_ref[:, start + ff : start + 2 * ff] = (grad_sigma * gate).astype(LOW)
        results.put(base)
        for side in range(2):
            total = 0.0
            for i in range(4):
                (weight,) = stream.take(1)
                total = total + dot_nt(grad_ref[:, i * ff : (i + 1) * ff], weight[...])
            part_ref[:, side * half : (side + 1) * half] = total.astype(LOW)
        results.put(base + 1)

    return call(
        body,
        "feed_back",
        [*norm_ins, gate, up, *down_parts, *[pair_parts[i] for i in order]],
        ([] if first_layer else norm_back_shapes(rows, wide))
        + [((rows, 4 * ff), LOW), ((rows, wide), LOW)],
        [],
        12 * rows * wide * ff,
        2 * rows * ff,
    )


def ff_weights_kernel(chunks, split, *refs):
    xb_refs, bb_refs, dg_refs, in_refs = [refs[i * chunks : (i + 1) * chunks] for i in range(4)]
    first_ref, second_ref, turned_ref = refs[4 * chunks :]
    j = pl.program_id(0)
    rows = xb_refs[0].shape[0]
    half = first_ref.shape[0]

    def take(x_refs):
        for i, ref in enumerate(x_refs):
            turned_ref[:, i * rows : (i + 1) * rows] = ref[...].T

    def work(y_refs):
        grads = jnp.concatenate([ref[...] for ref in y_refs], axis=0)
        total = low_dot(turned_ref[...], grads)
        first_ref[...] = total[:half].astype(LOW)
        second_ref[...] = total[half:].astype(LOW)

    @pl.when(j == 0)
    def _():
        take(xb_refs)

    @pl.when(j == split)
    def _():
        take(bb_refs)

    @pl.when(j < split)
    def _():
        work(dg_refs)

    @pl.when(j >= split)
    def _():
        work(in_refs)


def ff_weights(all_b, branch_b, grads, inner):
    chunks = len(all_b)
    rows, wide = all_b[0].shape
    ff = inner[0].shape[1] // 2
    step = min(1024, ff)
    n = ff // step
    split = 4 * n
    full = whole((rows, wide))
    grad = pl.BlockSpec((rows, step), lambda j: (0, jnp.minimum(j, split - 1)))
    last = pl.BlockSpec((rows, step), lambda j: (0, jnp.maximum(j - split, 0)))

    def place(j):
        k = j - split
        early = jnp.where(j < 2 * n, j, j + n)
        late = jnp.where(k < n, 2 * n + k, 4 * n + k)
        return (0, jnp.where(j < split, early, late))

    out = pl.BlockSpec((wide // 2, step), place)
    shape = jax.ShapeDtypeStruct((wide // 2, 6 * ff), LOW)
    return pl.pallas_call(
        functools.partial(ff_weights_kernel, chunks, split),
        grid=(6 * n,),
        in_specs=[full] * (2 * chunks) + [grad] * chunks + [last] * chunks,
        out_specs=[out, out],
        scratch_shapes=[pltpu.VMEM((wide, rows * chunks), LOW)],
        out_shape=[shape, shape],
        compiler_params=limits(),
        cost_estimate=cost(12 * chunks * rows * wide * ff, 12 * wide * ff + 8 * chunks * rows * wide),
        name="ff_weights",
    )(*all_b, *branch_b, *grads, *inner)


def in_weights_kernel(chunks, *refs):
    xa_refs, ba_refs, dp_refs, at_refs = [refs[i * chunks : (i + 1) * chunks] for i in range(4)]
    first_ref, second_ref = refs[4 * chunks :]
    width = dp_refs[0].shape[1] // 2
    q_width = at_refs[0].shape[1] // 2
    half = first_ref.shape[0]
    for x_refs, y_refs, size, base in (
        (xa_refs, dp_refs, width, 0),
        (ba_refs, at_refs, q_width, width),
    ):
        turned = jnp.concatenate([ref[...].T for ref in x_refs], axis=1)
        for side in range(2):
            grads = jnp.concatenate(
                [ref[:, side * size : (side + 1) * size] for ref in y_refs], axis=0
            )
            start = side * (width + q_width) + base
            total = low_dot(turned, grads)
            first_ref[:, start : start + size] = total[:half].astype(LOW)
            second_ref[:, start : start + size] = total[half:].astype(LOW)


def in_weights(all_a, branch_a, grads, attended):
    chunks = len(all_a)
    rows, wide = all_a[0].shape
    width = grads[0].shape[1] + attended[0].shape[1]
    operands = list(all_a) + list(branch_a) + list(grads) + list(attended)
    shape = (wide // 2, width)
    return pl.pallas_call(
        functools.partial(in_weights_kernel, chunks),
        grid=(1,),
        in_specs=[whole(v.shape) for v in operands],
        out_specs=[whole(shape)] * 2,
        out_shape=[jax.ShapeDtypeStruct(shape, LOW)] * 2,
        compiler_params=limits(),
        cost_estimate=cost(
            2 * chunks * rows * wide * width, 2 * wide * width + 4 * chunks * rows * wide
        ),
        name="in_weights",
    )(*operands)


def role_sum_kernel(row_ref, side_ref, left_ref, right_ref, *outs):
    step = pl.program_id(0)
    total = left_ref[...] + right_ref[...]
    for i, out_ref in enumerate(outs):

        @pl.when(step // 2 == i)
        def _(out_ref=out_ref):
            out_ref[...] = total


def role_sums(place, left, right):
    rows, both = left.shape[0] // 4, left.shape[1]
    width = both // 2
    picks = [pick for role in ROLES for pick in role]
    row = place ^ jnp.array([m for m, _ in picks], jnp.int32)
    side = jnp.array([s for _, s in picks], jnp.int32)
    block = pl.BlockSpec((rows, width), lambda i, r, s: (r[i], s[i]))

    def out(k):
        return pl.BlockSpec((rows, width), lambda i, r, s: (jnp.where(i > 2 * k, 1, 0), 0))

    return pl.pallas_call(
        role_sum_kernel,
        grid_spec=pltpu.PrefetchScalarGridSpec(
            num_scalar_prefetch=2,
            grid=(8,),
            in_specs=[block, block],
            out_specs=[out(k) for k in range(4)],
        ),
        out_shape=[jax.ShapeDtypeStruct((2 * rows, width), LOW)] * 4,
        compiler_params=limits(),
        cost_estimate=cost(0, 12 * rows * both),
        name="role_sums",
    )(row, side, left, right)


def cut_kernel(place_ref, gate_ref, up_ref, down_ref, *refs):
    outs, turned_ref = refs[:3], refs[3]
    turned_ref[...] = down_ref[...].T
    outs[0][...] = gate_ref[...]
    outs[1][...] = up_ref[...]
    rows = outs[2].shape[0]
    start = pl.multiple_of(place_ref[0] * rows, rows)
    outs[2][...] = turned_ref[pl.ds(start, rows), :]


def cut_ff(place, layer, gate, up, down):
    wide, ff = gate.shape[1:]
    rows = wide // lax.axis_size("dp")
    block = pl.BlockSpec((None, rows, ff), lambda i, p: (layer, p[0], 0))
    return pl.pallas_call(
        cut_kernel,
        grid_spec=pltpu.PrefetchScalarGridSpec(
            num_scalar_prefetch=1,
            grid=(1,),
            in_specs=[block, block, pl.BlockSpec((None, ff, wide), lambda i, p: (layer, 0, 0))],
            out_specs=[whole((rows, ff))] * 3,
            scratch_shapes=[pltpu.VMEM((wide, ff), LOW)],
        ),
        out_shape=[jax.ShapeDtypeStruct((rows, ff), LOW)] * 3,
        compiler_params=limits(),
        cost_estimate=cost(0, 4 * wide * ff),
        name="cut_ff",
    )(place, gate, up, down)


def cut_in_kernel(place_ref, q_ref, k_ref, v_ref, o_ref, out_ref):
    rows, q_width = q_ref.shape
    kv_width = k_ref.shape[1]
    out_ref[:rows, :q_width] = q_ref[...]
    out_ref[:rows, q_width : q_width + kv_width] = k_ref[...]
    out_ref[:rows, q_width + kv_width :] = v_ref[...]
    out_ref[rows:, :] = o_ref[...]


def cut_in(place, layer, query, key, value, out):
    count = lax.axis_size("dp")
    blocks = [(v.shape[1] // count, v.shape[2]) for v in (query, key, value, out)]
    shape = (blocks[0][0] + blocks[3][0], blocks[3][1])
    return pl.pallas_call(
        cut_in_kernel,
        grid_spec=pltpu.PrefetchScalarGridSpec(
            num_scalar_prefetch=1,
            grid=(1,),
            in_specs=[pl.BlockSpec((None,) + b, lambda i, p: (layer, p[0], 0)) for b in blocks],
            out_specs=whole(shape),
        ),
        out_shape=jax.ShapeDtypeStruct(shape, LOW),
        compiler_params=limits(),
        cost_estimate=cost(0, 4 * shape[0] * shape[1]),
        name="cut_in",
    )(place, query, key, value, out)


def pick_kernel(hi_ref, block_ref, mine_ref, other_ref):
    first, second = block_ref[:, 0, :], block_ref[:, 1, :]
    mine_ref[...] = jnp.where(hi_ref[0] == 0, first, second)
    other_ref[...] = jnp.where(hi_ref[0] == 0, second, first)


def pick(hi, block):
    rows, _, width = block.shape
    return pl.pallas_call(
        pick_kernel,
        grid_spec=pltpu.PrefetchScalarGridSpec(
            num_scalar_prefetch=1,
            grid=(1,),
            in_specs=[whole(block.shape)],
            out_specs=[whole((rows, width))] * 2,
        ),
        out_shape=[jax.ShapeDtypeStruct((rows, width), LOW)] * 2,
        compiler_params=limits(),
        cost_estimate=cost(0, 8 * rows * width),
        name="pick",
    )(hi.astype(jnp.int32).reshape(1), block)


def spread_ff_kernel(spots, place_ref, *refs):
    count = len(spots)
    gate_refs, up_refs, down_refs = [refs[i * count : (i + 1) * count] for i in range(3)]
    outs, held_ref = refs[-4:-1], refs[-1]
    put_parts(place_ref, gate_refs, spots, outs[0].at[0])
    put_parts(place_ref, up_refs, spots, outs[1].at[0])
    put_parts(place_ref, down_refs, spots, held_ref)
    outs[2][0] = held_ref[...].T


def flatten(pieces):
    parts, spots = [], []
    for m, piece in enumerate(pieces):
        piece = piece if isinstance(piece, tuple) else (piece,)
        for i, part in enumerate(piece):
            if not isinstance(part, tuple):
                part = (part, 0, part.shape[0])
            parts.append((part[0], part[1] // part[2], part[2]))
            spots.append((m, i, len(piece)))
    return (parts, spots)


def put_parts(place_ref, refs, spots, out_ref):
    for ref, (m, i, count) in zip(refs, spots):
        rows = ref.shape[0]
        start = 0
        if len(spots) > 1:
            start = pl.multiple_of((place_ref[0] ^ m) * (rows * count) + i * rows, rows)
        out_ref[pl.ds(start, rows), :] = ref[...].astype(FULL)


def spread_ff(place, pieces, layer, earlier):
    pieces, spots = flatten(pieces)
    count = len(pieces)
    rows, wide = pieces[0][2], pieces[0][0].shape[1]
    ff = wide // 3
    step = min(256, ff)
    steps = ff // step
    tall = rows * count

    def block(k, at):
        return pl.BlockSpec((rows, step), lambda j, p: (at, j + k * steps))

    in_specs = [block(k, at) for k in range(3) for _, at, _ in pieces]
    operands = [array for array, _, _ in pieces] * 3
    aliases = {}
    if earlier is not None:
        aliases = {1 + len(operands) + i: i for i in range(3)}
        in_specs += [pl.BlockSpec(memory_space=pl.ANY)] * 3
        operands += list(earlier)

    def kernel(place_ref, *refs):
        refs = refs[: 3 * count] + refs[len(operands) :]
        spread_ff_kernel(spots, place_ref, *refs)

    tall_out = pl.BlockSpec((1, tall, step), lambda j, p: (layer, 0, j))
    flat_out = pl.BlockSpec((1, step, tall), lambda j, p: (layer, j, 0))
    return pl.pallas_call(
        kernel,
        grid_spec=pltpu.PrefetchScalarGridSpec(
            num_scalar_prefetch=1,
            grid=(steps,),
            in_specs=in_specs,
            out_specs=[tall_out, tall_out, flat_out],
            scratch_shapes=[pltpu.VMEM((tall, step), FULL)],
        ),
        out_shape=[
            jax.ShapeDtypeStruct((LAYERS, tall, ff), FULL),
            jax.ShapeDtypeStruct((LAYERS, tall, ff), FULL),
            jax.ShapeDtypeStruct((LAYERS, ff, tall), FULL),
        ],
        input_output_aliases=aliases,
        compiler_params=limits(),
        cost_estimate=cost(0, 18 * tall * ff),
        name="spread_ff",
    )(place, *operands)


def spread_in(place, pieces, layer, earlier, q_width):
    pieces, spots = flatten(pieces)
    count = len(pieces)
    rows, width = pieces[0][2], pieces[0][0].shape[1]
    tall = rows * count
    kv_width = q_width // 2
    operands = [array for array, _, _ in pieces]
    in_specs = [pl.BlockSpec((rows, width), lambda j, p, at=at: (at, 0)) for _, at, _ in pieces]
    aliases = {}
    if earlier is not None:
        aliases = {1 + count + i: i for i in range(4)}
        in_specs = in_specs + [pl.BlockSpec(memory_space=pl.ANY)] * 4
        operands += list(earlier)

    def kernel(place_ref, *refs):
        piece_refs, (q_ref, k_ref, v_ref, o_ref, held_ref) = refs[:count], refs[len(operands) :]
        put_parts(place_ref, piece_refs, spots, held_ref)
        at = 0
        for out_ref, size in ((q_ref, q_width), (k_ref, kv_width), (v_ref, kv_width)):
            out_ref[0] = held_ref[:, at : at + size]
            at += size
        o_ref[0] = held_ref[:, at:].T

    sizes = [(tall, q_width), (tall, kv_width), (tall, kv_width), (q_width, tall)]
    return pl.pallas_call(
        kernel,
        grid_spec=pltpu.PrefetchScalarGridSpec(
            num_scalar_prefetch=1,
            grid=(1,),
            in_specs=in_specs,
            out_specs=[pl.BlockSpec((1,) + s, lambda j, p: (layer, 0, 0)) for s in sizes],
            scratch_shapes=[pltpu.VMEM((tall, width), FULL)],
        ),
        out_shape=[jax.ShapeDtypeStruct((LAYERS,) + s, FULL) for s in sizes],
        input_output_aliases=aliases,
        compiler_params=limits(),
        cost_estimate=cost(0, 6 * tall * width),
        name="spread_in",
    )(place, *operands)


def gather_kernel(count, tops, place_ref, *refs):
    piece_refs, out_ref = refs[:count], refs[count]
    for m, ref in enumerate(piece_refs):
        row, part_row = 0, 0
        for size in tops:
            part = size // count
            start = pl.multiple_of(row + (place_ref[0] ^ m) * part, part)
            out_ref[pl.ds(start, part), :] = ref[part_row : part_row + part, :]
            row += size
            part_row += part


def gather_pieces(place, pieces, tops):
    count = len(pieces)
    shape = (sum(tops), pieces[0].shape[1])
    return pl.pallas_call(
        functools.partial(gather_kernel, count, tops),
        grid_spec=pltpu.PrefetchScalarGridSpec(
            num_scalar_prefetch=1,
            grid=(1,),
            in_specs=[whole(p.shape) for p in pieces],
            out_specs=whole(shape),
        ),
        out_shape=jax.ShapeDtypeStruct(shape, LOW),
        compiler_params=limits(),
        cost_estimate=cost(0, 4 * shape[0] * shape[1]),
        name="gather_pieces",
    )(place, *pieces)


def cut(weight, layer, place):
    rows = weight.shape[1] // lax.axis_size("dp")
    start = (jnp.int32(layer), place * rows, jnp.int32(0))
    return lax.dynamic_slice(weight, start, (1, rows, weight.shape[2]))[0]


class Group:
    def __init__(self, piece, tops, place):
        self.piece, self.tops, self.place = piece, tops, place
        self.count = lax.axis_size("dp")
        self.even = all(size // self.count % 16 == 0 for size in tops)

    def fetch(self, order):
        self.piece = flip_hi(order.after(self.piece))

    def gather(self, order):
        order.join(self.piece)
        piece = order.after(self.piece)
        if len(self.tops) == 1:
            self.first = lax.all_gather(piece, "dp", axis=0, tiled=True)
            return
        pieces = lax.all_gather(piece, "dp", axis=0)
        at, rows = 0, []
        for size in self.tops:
            part = size // self.count
            rows.append(pieces[:, at : at + part].reshape(size, -1))
            at += part
        self.first = jnp.concatenate(rows, axis=0)

    def cross(self, order, gated=False):
        first = order.after(self.first) if gated else self.first
        self.halves = (first, flip_core(first))

    def spread(self, order, near=(1, 2)):
        order.join(self.piece)
        if self.even:
            piece = order.after(self.piece)
            self.pieces = [piece] + [hop(piece, "dp", m) for m in near]
        else:
            self.gather(order)

    def spread_on(self, order):
        if self.even:
            order.join(*self.pieces[1:])
            piece = order.after(self.pieces[0])
            self.pieces += [hop(piece, "dp", m) for m in range(len(self.pieces), self.count)]

    def collect(self, order):
        if self.even:
            spot = self.place.astype(jnp.int32).reshape(1)
            order.join(*self.pieces[1:])
            pieces = [order.after(self.pieces[0])] + self.pieces[1:]
            self.first = gather_pieces(spot, pieces, self.tops)
        order.mark(self.first)
        self.halves = (self.first, flip_core(self.first))

    def done(self, order):
        order.join(self.halves[1])


def in_groups(layer, w_query, w_key, w_value, w_out, place):
    wide, q_width = w_query.shape[1:]
    width = q_width + 2 * w_key.shape[2]
    count = lax.axis_size("dp")
    if width == w_out.shape[2] and q_width // count % 16 == 0:
        spot = place.astype(jnp.int32).reshape(1)
        piece = cut_in(spot, layer, w_query, w_key, w_value, w_out)
        return [Group(piece, (wide, q_width), place)]
    piece = jnp.concatenate([cut(v, layer, place) for v in (w_query, w_key, w_value)], axis=1)
    return [Group(piece, (wide,), place), Group(cut(w_out, layer, place), (q_width,), place)]


ROLES = (((1, 0), (3, 0)), ((2, 1), (3, 1)), ((2, 0), (1, 1)), ((0, 0), (0, 1)))


class Sum:
    def __init__(self, parts, place, by_hops):
        self.first, self.last = parts
        self.place = place
        self.even = by_hops and lax.axis_size("dp") == 4

    def flip(self, order):
        self.came = flip_core(order.after(self.last))

    def start(self, order):
        order.join(self.came)
        if not self.even:
            total = order.mark(add_low(order.after(self.first), self.came))
            self.both = lax.psum_scatter(total, "dp", scatter_dimension=0, tiled=True)
            return
        spot = self.place.astype(jnp.int32).reshape(1)
        roles = role_sums(spot, order.after(self.first), self.came)
        to_x, to_y, self.on, self.keep = order.mark(roles)
        self.from_x, self.from_y = hop(to_x, "dp", 1), hop(to_y, "dp", 2)

    def second(self, order):
        if not self.even:
            return
        rows = self.on.shape[0] // 2
        on, keep, from_x, from_y = order.after((self.on, self.keep, self.from_x, self.from_y))
        to_y = add_low(on[:rows], from_x[rows:])
        to_x = add_low(on[rows:], from_y[rows:])
        self.own = add_low(keep[:rows], from_x[:rows])
        self.other = add_low(keep[rows:], from_y[:rows])
        order.mark((to_x, to_y))
        self.to_own, self.to_other = hop(to_y, "dp", 2), hop(to_x, "dp", 1)

    def third(self, order):
        if not self.even:
            both = order.after(self.both)
            width = both.shape[1] // 2
            self.own, self.other = order.mark((both[:, :width], both[:, width:]))
            return
        order.join(self.to_own)
        other, came = order.after((self.other, self.to_other))
        self.other = order.mark(add_low(other, came))

    def across(self, order):
        self.far = flip_hi(order.after(self.other))

    def fourth(self, order):
        own, far = order.after((self.own, self.far))
        total = own.astype(FULL) + far.astype(FULL)
        if self.even:
            total = total + order.after(self.to_own).astype(FULL)
        self.total = order.mark(total.astype(LOW))

    def gather(self, order):
        total = order.after(self.total)
        self.pieces = [lax.all_gather(total, "dp", axis=0, tiled=True)]

    def straight(self, order):
        total = order.after(self.total)
        self.pieces = [total] + [hop(total, "dp", m) for m in range(1, lax.axis_size("dp"))]

    def near(self, order):
        if not self.even:
            self.gather(order)
            return
        total = order.after(self.total)
        rows = total.shape[0] // 2
        self.mine = (total[:rows], total[rows:])
        self.beside = [hop(self.mine[0], "dp", 1), hop(self.mine[1], "dp", 2)]

    def fifth(self, order):
        if not self.even:
            return
        top, bottom = self.mine
        order.join(*self.beside)
        near_x, near_y = order.after(tuple(self.beside))
        tops = order.mark(jnp.concatenate([top, near_x], axis=0))
        bottoms = order.mark(jnp.concatenate([bottom, near_y], axis=0))
        tops, bottoms = hop(tops, "dp", 2), hop(bottoms, "dp", 1)
        rows = top.shape[0]
        self.pieces = [
            (top, bottom),
            (near_x, (bottoms, 0, rows)),
            ((tops, 0, rows), near_y),
            ((tops, rows, rows), (bottoms, rows, rows)),
        ]

    def done(self, order):
        order.join(*(part for piece in self.pieces if isinstance(piece, tuple) for part in piece))


def rope_tables(positions, width):
    indices = jnp.arange(HEAD // 2, dtype=FULL)
    inverse = ROPE_BASE ** (-2.0 * indices / HEAD)
    angles = positions.astype(FULL)[:, None] * inverse[None, :]
    cosine, sine = jnp.cos(angles), jnp.sin(angles)
    heads = width // HEAD
    return (
        jnp.concatenate([cosine, cosine] * heads, axis=1),
        jnp.concatenate([-sine, sine] * heads, axis=1),
    )


def finish_back(grad, left, right, hidden, factor, gain):
    unit = hidden * factor
    grad_normed = left.astype(FULL) + right.astype(FULL)
    grad_unit = grad_normed * gain
    inner = jnp.mean(grad_unit * unit, axis=-1, keepdims=True)
    return (
        grad + factor * (grad_unit - unit * inner),
        jnp.sum(grad_normed * unit, axis=0, keepdims=True),
    )


class Arrival:
    def __init__(self, block, hi, lo, core):
        self.block, self.hi, self.lo, self.core = block, hi, lo, core

    def pick(self, order):
        self.mine, self.other = order.mark(pick(self.hi, order.after(self.block)))

    def fetch_on(self, order):
        self.far = flip_hi(order.after(self.other))

    def fetch(self, order):
        self.pick(order)
        self.fetch_on(order)

    def share(self, order):
        order.join(self.far)
        mine, far = order.after((self.mine, self.far))
        self.parts = [jnp.where(self.hi == j, mine, far) for j in range(CHUNKS)]
        order.mark(tuple(self.parts))
        self.halves = [None] * CHUNKS
        self.near = [None] * CHUNKS

    def send(self, order, j):
        self.near[j] = hop(order.after(self.parts[j]), "cols", 1)

    def cross(self, order, j):
        lo, core = self.lo, self.core
        order.join(self.near[j])
        part, near = order.after((self.parts[j], self.near[j]))
        if len(low_bits()) == 1:
            at_home = lo == core
            first = jnp.where(at_home, part, near)
            second = jnp.where(at_home, near, part)
        else:
            for bit in low_bits():
                far = near if bit == 1 else hop(part, "cols", bit)
                part = jnp.where(
                    (lo & bit) == 0,
                    jnp.concatenate([part, far], axis=0),
                    jnp.concatenate([far, part], axis=0),
                )
            half = part.shape[0] // 2
            first = lax.dynamic_slice_in_dim(part, core * half, half, 0)
            second = lax.dynamic_slice_in_dim(part, (1 - core) * half, half, 0)
        first, second = order.mark((first, second))
        self.halves[j] = (first, flip_core(second))

    def chunk(self, order, j):
        order.join(self.halves[j][1])
        return order.mark(jnp.concatenate(order.after(self.halves[j]), axis=-1))


class Departure:
    def __init__(self, results, hi, lo, core, rows):
        self.results, self.hi, self.lo, self.core, self.rows = results, hi, lo, core, rows

    def cross(self, order):
        flat = order.after([chunk for chunks in self.results for chunk in chunks])
        half = flat[0].shape[1] // 2
        self.firsts = [chunk[:, :half] for chunk in flat]
        send = jnp.concatenate([chunk[:, half:].astype(LOW) for chunk in flat], axis=0)
        self.came = flip_core(order.mark(send))

    def away(self, order):
        came = order.after(self.came)
        size = self.firsts[0].shape[0]
        parts = []
        for i, first in enumerate(self.firsts):
            second = came[i * size : (i + 1) * size].astype(FULL)
            both = jnp.where(
                self.core == 0,
                jnp.concatenate([first, second], axis=0),
                jnp.concatenate([second, first], axis=0),
            )
            parts.append(lax.dynamic_slice_in_dim(both, self.lo * self.rows, self.rows, 0))
        pairs = list(zip(parts[0::2], parts[1::2]))
        self.mine = [jnp.where(self.hi == 0, a, b) for a, b in pairs]
        others = [jnp.where(self.hi == 0, b, a).astype(LOW) for a, b in pairs]
        self.mine, send = order.mark((self.mine, jnp.concatenate(others, axis=0)))
        self.far = flip_hi(send)

    def done(self, order):
        far = order.after(self.far)
        out = []
        for i, mine in enumerate(self.mine):
            other = far[i * self.rows : (i + 1) * self.rows].astype(FULL)
            out.append(
                jnp.where(
                    self.hi == 0, jnp.stack([mine, other], axis=1), jnp.stack([other, mine], axis=1)
                )
            )
        return out


def shards(
    block_input, block_cotangent, w_query, w_key, w_value, w_out, w_gate, w_up, w_down, norm_gains
):
    low_count = lax.axis_size("cols") // 2
    core, col, place = lax.axis_index("rows"), lax.axis_index("cols"), lax.axis_index("dp")
    hi, lo = col // low_count, col % low_count
    core_ref = core.astype(jnp.int32).reshape(1)
    block_rows = block_input.shape[0]
    rows = block_rows * low_count
    q_width = w_query.shape[2]
    half = rows // 2
    tables = [
        rope_tables(jnp.arange(half, dtype=jnp.int32) + j * rows + core * half, q_width)
        for j in range(CHUNKS)
    ]
    spot = place.astype(jnp.int32).reshape(1)
    order = Order()
    w_in = jnp.concatenate([w_query, w_key, w_value], axis=2)
    wide = w_in.shape[1]
    ff = w_gate.shape[2]
    arrival = Arrival(block_input, hi, lo, core)
    arrival.fetch(order)
    a_groups = [in_groups(0, order.after(w_query), w_key, w_value, w_out, place), None]
    order.mark([group.piece for group in a_groups[0]])
    for group in a_groups[0]:
        group.fetch(order)
    in_own, out_own, gates, ups, own_downs = [
        (v, flip_core(v)) for v in (w_in, w_out, w_gate, w_up, w_down)
    ]
    gains = jnp.concatenate([norm_gains, flip_core(norm_gains)], axis=-1)
    f_groups = []
    for l in range(LAYERS):
        pieces = order.mark(cut_ff(spot, l, order.after(w_gate), w_up, w_down))
        f_groups.append([Group(piece, (wide,), place) for piece in pieces])
        order.join(*((in_own[1], gains) if not l else (out_own[1],)))
    a_groups[1] = in_groups(1, order.after(w_query), w_key, w_value, w_out, place)
    order.mark([group.piece for group in a_groups[1]])
    order.join(gates[1], ups[1])
    cotangent = Arrival(block_cotangent, hi, lo, core)
    cotangent.pick(order)
    arrival.share(order)
    for group in a_groups[0]:
        group.spread(order)
    arrival.send(order, 0)
    f_groups[0][0].fetch(order)
    for group in a_groups[0]:
        group.spread_on(order)
    arrival.cross(order, 0)
    f_groups[0][0].gather(order)
    f_groups[0][1].fetch(order)
    for group in a_groups[0]:
        group.collect(order)
    hidden = [arrival.chunk(order, 0)]
    order.join(own_downs[1])
    arrival.send(order, 1)
    f_groups[0][1].gather(order)
    for group in a_groups[0]:
        group.done(order)

    stash = [[None] * CHUNKS for _ in range(LAYERS)]
    weights = [None] * LAYERS
    pairs = [None] * CHUNKS

    def front(l, j):
        block, factor_a, normed_a, query, mine = order.mark(
            project(order.after(hidden[j]), pairs[j], gains[l, 0:1], ins, *tables[j])
        )
        kvs.extend([mine, flip_core(mine)])
        return (block, factor_a, normed_a, query)

    def middle(l, j, kept):
        order.join(kvs[2 * j + 1])
        attended, lse, part = order.mark(
            attend(core_ref, order.after(kept[3]), kvs[: 2 * j + 2], outs)
        )
        pairs[j] = group_pair(part)
        return (*kept, kvs[: 2 * j + 2], lse, attended)

    def rear(l, j, kept):
        order.join(pairs[j])
        mixed, factor_b, normed_b, gate, up, inner, part = order.mark(
            feed_forward(order.after(kept[0]), pairs[j], gains[l, 1:2], pair_parts, down_parts)
        )
        hidden[j] = mixed
        pairs[j] = group_pair(part) if l + 1 < LAYERS else part
        stash[l][j] = kept + (mixed, factor_b, normed_b, gate, up, inner)

    for l in range(LAYERS):
        more = l + 1 < LAYERS
        halves = [group.halves for group in a_groups[l]]
        if len(halves) == 1:
            ins = [Part(v, None, 0, wide) for v in halves[0]]
            outs = [Part(v, None, wide, w_out.shape[1]) for v in halves[0]]
        else:
            ins, outs = [[Part(v) for v in pair] for pair in halves]
        ins = [Part(v, l) for v in in_own] + ins
        outs = [Part(v, l) for v in out_own] + outs
        kvs, kept = [], [None] * CHUNKS
        first, second, third = f_groups[l]
        if not l:
            third.fetch(order)
            kept[0] = front(l, 0)
            arrival.cross(order, 1)
            hidden.append(arrival.chunk(order, 1))
            kept[1] = front(l, 1)
            kept[0] = middle(l, 0, kept[0])
            kept[1] = middle(l, 1, kept[1])
            third.spread(order, range(1, lax.axis_size("dp")))
            order.join(pairs[0])
            for group in a_groups[1]:
                group.fetch(order)
            order.join(pairs[1])
            first.cross(order)
            for group in a_groups[1]:
                order.join(group.piece)
            third.collect(order)
            for group in a_groups[1]:
                group.gather(order)
            f_groups[1][0].fetch(order)
            second.cross(order)
            first.done(order)
        else:
            order.join(pairs[0])
            kept[0] = front(l, 0)
            second.gather(order)
            third.fetch(order)
            order.join(pairs[1])
            kept[1] = front(l, 1)
            kept[0] = middle(l, 0, kept[0])
            third.spread(order, range(1, lax.axis_size("dp")))
            cotangent.fetch_on(order)
            kept[1] = middle(l, 1, kept[1])
            order.join(pairs[0], cotangent.far)
            first.cross(order, True)
            third.collect(order)
            second.cross(order)
            first.done(order)
        second.done(order)
        third.done(order)
        packs = [group.halves for group in f_groups[l]]
        pair_parts = [Part(v, l) for v in (*gates, *ups)] + [
            Part(v) for pack in packs[:2] for v in pack
        ]
        down_parts = [Part(v, l) for v in own_downs] + [Part(v) for v in packs[2]]
        weights[l] = (ins, outs, pair_parts, down_parts)
        rear(l, 0, kept[0])
        if not more:
            cotangent.share(order)
            cotangent.send(order, 1)
            cotangent.send(order, 0)
        order.join(pairs[1])
        rear(l, 1, kept[1])
        if not more:
            cotangent.cross(order, 1)
        if more:
            f_groups[1][0].gather(order)
            f_groups[1][1].fetch(order)
            order.join(pairs[0])
            for group in a_groups[1]:
                group.cross(order, True)
                group.done(order)
    grads = [None] * CHUNKS
    grads[1] = (cotangent.chunk(order, 1),)

    gain_a, gain_b = [0.0] * LAYERS, [0.0] * LAYERS
    sums = {}

    def ff_step(l, j):
        pair_parts, down_parts = weights[l][2:]
        gate, up, inner = stash[l][j][-3:]
        if len(grads[j]) == 1:
            branch_b = order.after(grads[j][0])
            grad_hidden = branch_b.astype(FULL)
            pair_grad, part = order.mark(feed_back((branch_b,), gate, up, pair_parts, down_parts))
        else:
            order.join(*grads[j][1:3])
            grad_hidden, branch_b, gain_part, pair_grad, part = order.mark(
                feed_back(
                    (order.after(grads[j][0]), *grads[j][1:]), gate, up, pair_parts, down_parts
                )
            )
            gain_a[l + 1] = gain_a[l + 1] + gain_part
        mixed, factor_b, normed_b = stash[l][j][7:10]
        grads[j] = (grad_hidden, *group_pair(part), mixed, factor_b, gains[l, 1:2])
        return (normed_b, branch_b, pair_grad, inner)

    def ff_grad(l, kept):
        columns = list(zip(*kept))
        columns[0] = order.after(columns[0])
        sums["ff", l] = Sum(order.mark(ff_weights(*columns)), place, l == 0)

    def attend_step(l, j, held):
        block, factor_a, normed_a, query, kvs, lse, attended = stash[l][j][:7]
        order.join(*grads[j][1:3])
        grad_mixed, branch_a, gain_part, dq, *dkvs = order.mark(
            attend_back(
                core_ref,
                (order.after(grads[j][0]), *grads[j][1:]),
                query,
                lse,
                kvs,
                held,
                weights[l][1],
            )
        )
        gain_b[l] = gain_b[l] + gain_part
        grads[j] = (grad_mixed, None, None, block, factor_a, gains[l, 0:1])
        middle = (dq, dkvs[-2], flip_core(dkvs[-1]))
        return (dkvs[:2], middle, (normed_a, branch_a, None, attended))

    def project_step(l, j, middle, kept):
        dq, mine, came = middle
        order.join(came)
        proj_grad, part = order.mark(
            project_back(order.after(dq), mine, came, *tables[j], weights[l][0])
        )
        pair = group_pair(part) if l else last_pair(part)
        grads[j] = (grads[j][0], *pair, *grads[j][3:])
        return kept[:2] + (proj_grad,) + kept[3:]

    def in_grad(l, kept):
        columns = list(zip(*kept))
        columns[0] = order.after(columns[0])
        sums["in", l] = Sum(order.mark(in_weights(*columns)), place, l == 0)

    l = LAYERS - 1
    kept, mids = [None] * CHUNKS, [None] * CHUNKS
    kept[1] = ff_step(l, 1)
    cotangent.cross(order, 0)
    grads[0] = (cotangent.chunk(order, 0),)
    kept[0] = ff_step(l, 0)
    ff_grad(l, kept)
    sums["ff", l].flip(order)
    held, mids[1], kept[1] = attend_step(l, 1, None)
    sums["ff", l].start(order)
    order.join(mids[1][2])
    _, mids[0], kept[0] = attend_step(l, 0, held)
    kept[1] = project_step(l, 1, mids[1], kept[1])
    kept[0] = project_step(l, 0, mids[0], kept[0])
    in_grad(l, kept)
    l = 0
    kept, mids = [None] * CHUNKS, [None] * CHUNKS
    kept[1] = ff_step(l, 1)
    kept[0] = ff_step(l, 0)
    sums["in", 1].flip(order)
    ff_grad(l, kept)
    sums["ff", 1].third(order)
    sums["ff", 1].across(order)
    sums["in", 1].start(order)
    sums["ff", 0].flip(order)
    held, mids[1], kept[1] = attend_step(l, 1, None)
    sums["ff", 0].start(order)
    _, mids[0], kept[0] = attend_step(l, 0, held)
    kept[1] = project_step(l, 1, mids[1], kept[1])
    kept[0] = project_step(l, 0, mids[0], kept[0])
    sums["in", 1].third(order)
    in_grad(l, kept)
    sums["ff", 1].fourth(order)
    sums["ff", 1].gather(order)
    for g in reversed(grads):
        order.join(*g[1:3])
    ends = [finish_back(order.after(g[0]), *g[1:]) for g in grads]
    order.mark(tuple(g for g, _ in ends))
    gain_a[0] = sum(part for _, part in ends)
    if len(low_bits()) == 1:
        gain_a[0] = jnp.where(lo == core, gain_a[0], 0.0)
        gain_a[0] = gain_a[0] + hop(gain_a[0], "cols", 1)
    gain_grads = [jnp.concatenate([gain_a[l], gain_b[l]], axis=0) for l in range(LAYERS)]
    grad_gains = order.after(jnp.stack(gain_grads))
    width = grad_gains.shape[-1] // 2
    gains_came = flip_core(grad_gains[..., width:])
    sums["ff", 0].second(order)
    sums["in", 0].flip(order)
    sums["in", 1].across(order)
    grad_gains = order.mark(grad_gains[..., :width] + order.after(gains_came))
    gains_came = flip_hi(grad_gains)
    sums["in", 0].start(order)
    sums["in", 1].fourth(order)
    grad_gains = order.mark(grad_gains + order.after(gains_came))
    sums["ff", 0].third(order)
    sums["ff", 0].across(order)
    tops = [last_pair(part) for part in order.after(pairs)]
    sums["in", 1].gather(order)
    sums["in", 0].second(order)
    order.join(tops)
    hidden = [
        h + left.astype(FULL) + right.astype(FULL)
        for h, (left, right) in order.after(list(zip(hidden, tops)))
    ]
    results = Departure((hidden, [g for g, _ in ends]), hi, lo, core, block_rows)
    results.cross(order)
    gains_came = hop(order.after(grad_gains), "dp", 1)
    sums["ff", 0].fourth(order)
    sums["ff", 0].near(order)
    sums["in", 0].third(order)
    sums["in", 0].across(order)
    ff_out = order.mark(spread_ff(order.after(spot), sums["ff", 1].pieces, 1, None))
    bit = 1
    while bit < lax.axis_size("dp"):
        grad_gains = order.mark(grad_gains + order.after(gains_came))
        bit *= 2
        if bit < lax.axis_size("dp"):
            gains_came = hop(grad_gains, "dp", bit)
        if bit == 2:
            sums["ff", 0].fifth(order)
            sums["in", 0].fourth(order)
            sums["in", 0].straight(order)
            results.away(order)
    in_out = order.mark(spread_in(order.after(spot), sums["in", 1].pieces, 1, None, q_width))
    sums["ff", 0].done(order)
    ff_out = order.mark(spread_ff(order.after(spot), sums["ff", 0].pieces, 0, ff_out))
    in_out = order.mark(spread_in(order.after(spot), sums["in", 0].pieces, 0, in_out, q_width))
    activations, input_grad = results.done(order)
    return (activations, input_grad, *in_out, *ff_out, grad_gains)


def solution(mesh):
    data = P("cols", "dp", "rows")
    tall = P(None, "rows", "cols")
    flat = P(None, "cols", "rows")
    gains = P(None, None, "rows")
    in_specs = (data, data, tall, tall, tall, flat, tall, tall, flat, gains)
    out_specs = (data, data, tall, tall, tall, flat, tall, tall, flat, gains)
    return jax.shard_map(
        shards, mesh=mesh, in_specs=in_specs, out_specs=out_specs, check_vma=False
    )
```

```python
import functools

import jax
import jax.numpy as jnp
from jax import lax
from jax.experimental import pallas as pl
from jax.experimental.pallas import tpu as pltpu
from jax.sharding import PartitionSpec as P

HEAD = 96
LAYERS = 2
CHUNKS = 2
EPSILON = 1e-05
ROPE_BASE = 100000.0
NEGATIVE = -1e30
LOW = jnp.bfloat16
FULL = jnp.float32
NT = (((1,), (1,)), ((), ()))
TN = (((0,), (0,)), ((), ()))
ROOM = 56 * 2**20
SCALE = 30
AHEAD = 8 * 2**20


def hop(value, axis, distance):
    size = lax.axis_size(axis)
    return lax.ppermute(value, axis, [(i, i ^ distance) for i in range(size)])


def flip_hi(value):
    return hop(value, "cols", lax.axis_size("cols") // 2)


def flip_core(value):
    return hop(value, "rows", 1)


def low_bits():
    bits, bit = [], 1
    while bit < lax.axis_size("cols") // 2:
        bits.append(bit)
        bit *= 2
    return bits


def group_pair(part):
    bits = low_bits()
    for bit in bits[:-1]:
        part = add_low(part, hop(part, "cols", bit))
    return (part, hop(part, "cols", bits[-1]))


def last_pair(part):
    cols, bits = lax.axis_size("cols"), low_bits()
    if len(bits) != 1:
        return group_pair(part)
    pairs = []
    for core in range(2):
        for col in range(cols):
            if col % 2 != core:
                pairs.append((core * cols + col, core * cols + (col ^ 1)))
    return (part, lax.ppermute(part, ("rows", "cols"), pairs))


class Order:
    def __init__(self):
        self.last = ()

    def after(self, values):
        return lax.optimization_barrier((values, self.last))[0] if self.last else values

    def mark(self, value):
        self.last = (value,)
        return value

    def join(self, *values):
        self.last = (*self.last, values)


def add_low(left, right):
    return (left.astype(FULL) + right.astype(FULL)).astype(LOW)


def low_dot(left, right):
    return jnp.dot(left, right, preferred_element_type=FULL)


def dot_nt(left, right):
    return lax.dot_general(left, right, NT, preferred_element_type=FULL)


def dot_tn(left, right):
    return lax.dot_general(left, right, TN, preferred_element_type=FULL)


def whole(shape):
    return pl.BlockSpec(shape, lambda *_: (0,) * len(shape))


def far():
    return pl.BlockSpec(memory_space=pl.ANY)


def cost(flops, size, exps=0):
    return pl.CostEstimate(
        flops=int(flops * SCALE), bytes_accessed=int(size * SCALE), transcendentals=0
    )


def limits():
    return pltpu.CompilerParams(vmem_limit_bytes=ROOM)


class Part:
    def __init__(self, array, layer=None, row=0, rows=None, column=0, columns=None):
        self.array, self.layer, self.row, self.column = array, layer, row, column
        self.shape = (rows or array.shape[-2], columns or array.shape[-1])

    def view(self, ref):
        ref = ref if self.layer is None else ref.at[self.layer]
        if self.shape == tuple(ref.shape):
            return ref
        return ref.at[pl.ds(self.row, self.shape[0]), pl.ds(self.column, self.shape[1])]

    def scratch(self):
        return pltpu.VMEM(self.shape, self.array.dtype)


class Stream:
    def __init__(self, sources, buffers, sems, ahead):
        self.copies = [
            pltpu.make_async_copy(source, buffer, sems.at[i])
            for i, (source, buffer) in enumerate(zip(sources, buffers))
        ]
        self.buffers = buffers
        self.sizes = [
            b.shape[0] * b.shape[1] * (4 if b.dtype == FULL else 2) for b in buffers
        ]
        self.ahead, self.started, self.waited = ahead, 0, 0
        self.feed()

    def feed(self):
        while self.started < len(self.copies) and (
            sum(self.sizes[self.waited : self.started]) < self.ahead
        ):
            self.copies[self.started].start()
            self.started += 1

    def take(self, count):
        first = self.waited
        for i in range(first, first + count):
            if i >= self.started:
                self.copies[i].start()
                self.started += 1
            self.copies[i].wait()
            self.waited += 1
        self.feed()
        return self.buffers[first : first + count]


class Results:
    def __init__(self, buffers, targets, sems):
        self.buffers, self.targets, self.sems = buffers, targets, sems
        self.copies = []

    def put(self, index):
        copy = pltpu.make_async_copy(
            self.buffers[index], self.targets[index], self.sems.at[index]
        )
        copy.start()
        self.copies.append(copy)

    def finish(self):
        for copy in self.copies:
            copy.wait()


def half_dots(left, first, second):
    half = left.shape[1] // 2
    return low_dot(left[:, :half], first) + low_dot(left[:, half:], second)


def turn(value, cosine, sine):
    width = value.shape[1]
    q_width = cosine.shape[1]
    ahead = pltpu.roll(value, width - HEAD // 2, 1)
    behind = pltpu.roll(value, HEAD // 2, 1)
    column = lax.broadcasted_iota(jnp.int32, value.shape, 1)
    other = jnp.where(lax.rem(column, HEAD) < HEAD // 2, ahead, behind)
    is_key = lax.broadcasted_iota(jnp.int32, cosine.shape, 1) < q_width // 2
    query = value[:, :q_width] * cosine + other[:, :q_width] * sine
    rest = value[:, q_width:] * jnp.where(is_key, cosine, 1.0)
    rest = rest + other[:, q_width:] * jnp.where(is_key, sine, 0.0)
    return (query, rest)


def put_norm(refs, gain_ref, results, at):
    sum_ref, factor_ref, normed_ref = results.buffers[at : at + 3]
    hidden = refs[0][...].astype(FULL)
    for ref in refs[1:]:
        hidden = hidden + ref[...].astype(FULL)
    factor = lax.rsqrt(jnp.mean(hidden * hidden, axis=-1, keepdims=True) + EPSILON)
    sum_ref[...] = hidden
    factor_ref[...] = factor
    normed_ref[...] = (hidden * factor * gain_ref[...]).astype(LOW)
    for i in range(3):
        results.put(at + i)


def put_norm_back(refs, results, at):
    grad_ref, left_ref, right_ref, hidden_ref, factor_ref, gain_ref = refs
    sum_ref, low_ref, gain_out_ref = results.buffers[at : at + 3]
    grad_normed = left_ref[...].astype(FULL) + right_ref[...].astype(FULL)
    factor = factor_ref[...]
    unit = hidden_ref[...] * factor
    grad_unit = grad_normed * gain_ref[...]
    inner = jnp.mean(grad_unit * unit, axis=-1, keepdims=True)
    grad = grad_ref[...].astype(FULL) + factor * (grad_unit - unit * inner)
    sum_ref[...] = grad
    low_ref[...] = grad.astype(LOW)
    gain_out_ref[...] = jnp.sum(grad_normed * unit, axis=0, keepdims=True)
    for i in range(3):
        results.put(at + i)


def norm_shapes(rows, wide):
    return [((rows, wide), FULL), ((rows, 1), FULL), ((rows, wide), LOW)]


def norm_back_shapes(rows, wide):
    return [((rows, wide), FULL), ((rows, wide), LOW), ((1, wide), FULL)]


def call(body, name, inputs, outs, scratch, flops, exps=0, scalars=(), ahead=AHEAD):
    inputs = [v if isinstance(v, Part) else Part(v) for v in inputs]
    size = sum(2 * p.shape[0] * p.shape[1] for p in inputs)
    count, made = len(inputs), len(outs)

    def kernel(*refs):
        scalar_refs, refs = refs[: len(scalars)], refs[len(scalars) :]
        sources, targets, refs = refs[:count], refs[count : count + made], refs[count + made :]
        held, buffers, refs = refs[:count], refs[count : count + made], refs[count + made :]
        in_sems, out_sems, own = refs[0], refs[1], refs[2:]
        stream = Stream([p.view(r) for p, r in zip(inputs, sources)], held, in_sems, ahead)
        results = Results(buffers, targets, out_sems)
        body(stream, results, *scalar_refs, *own)
        results.finish()

    return pl.pallas_call(
        kernel,
        grid_spec=pltpu.PrefetchScalarGridSpec(
            num_scalar_prefetch=len(scalars),
            grid=(1,),
            in_specs=[far()] * count,
            out_specs=[far()] * made,
            scratch_shapes=[p.scratch() for p in inputs]
            + [pltpu.VMEM(s, k) for s, k in outs]
            + [pltpu.SemaphoreType.DMA((count,)), pltpu.SemaphoreType.DMA((made,))]
            + list(scratch),
        ),
        out_shape=[jax.ShapeDtypeStruct(s, k) for s, k in outs],
        compiler_params=limits(),
        cost_estimate=cost(flops, size, exps),
        name=name,
    )(*scalars, *[p.array for p in inputs])


def project(hidden, pair, gain, parts, cosine, sine):
    rows, wide = hidden.shape
    q_width = cosine.shape[1]
    ins = [hidden, *(pair or ())]

    def body(stream, results):
        refs = stream.take(len(ins))
        (gain_ref,) = stream.take(1)
        put_norm(refs, gain_ref, results, 0)
        cos_ref, sin_ref = stream.take(2)
        tokens = results.buffers[2][...]
        q_ref, kv_ref = results.buffers[3:]
        for side in range(2):
            first, second = stream.take(2)
            projected = half_dots(tokens, first[...], second[...])
            query, rest = turn(projected, cos_ref[...], sin_ref[...])
            here = slice(side * q_width, (side + 1) * q_width)
            q_ref[:, here] = query.astype(LOW)
            kv_ref[:, here] = rest.astype(LOW)
        results.put(4)
        results.put(3)

    return call(
        body,
        "project",
        [*ins, gain, cosine, sine, *parts],
        norm_shapes(rows, wide) + [((rows, 2 * q_width), LOW)] * 2,
        [],
        8 * rows * wide * q_width,
    )


def score(key, query, kind):
    raw = dot_nt(key, query) * HEAD ** (-0.5)
    if kind == "own":
        key_pos = lax.broadcasted_iota(jnp.int32, raw.shape, 0)
        query_pos = lax.broadcasted_iota(jnp.int32, raw.shape, 1)
        raw = jnp.where(query_pos >= key_pos, raw, NEGATIVE)
    return raw


def offsets_of(chunks, core):
    return [0.0] * (2 * chunks - 1) + [jnp.where(core == 1, 0.0, -NEGATIVE)]


def kinds_of(chunks):
    return ["all"] * (2 * chunks - 2) + ["own", "sib"]


def attend(core, query, kvs, parts):
    rows, both = query.shape
    wide = 2 * parts[0].shape[1]
    chunks = len(kvs) // 2
    q_width, heads = both // 2, both // 2 // HEAD
    kv_width = q_width // 2

    def body(stream, results, core_ref):
        (q_ref,), kv_refs = stream.take(1), stream.take(2 * chunks)
        att_ref, lse_ref, part_ref = results.buffers
        offsets = offsets_of(chunks, core_ref[0])
        for h in range(2 * heads):
            group = (h // heads) * q_width + (h % heads) // 2 * HEAD
            mine = slice(h * HEAD, (h + 1) * HEAD)
            query = q_ref[:, mine]
            scores = [
                score(ref[:, group : group + HEAD], query, kind)
                for ref, kind in zip(kv_refs, kinds_of(chunks))
            ]
            highest = functools.reduce(
                jnp.maximum,
                [jnp.max(s, axis=0, keepdims=True) - o for s, o in zip(scores, offsets)],
            )
            exps = [jnp.exp(s - (highest + o)) for s, o in zip(scores, offsets)]
            total = sum(jnp.sum(e, axis=0, keepdims=True) for e in exps)
            share = 1.0 / total
            lse_ref[h : h + 1, :] = highest + jnp.log(total)
            spot = slice(group + kv_width, group + kv_width + HEAD)
            att = sum(
                dot_tn((e * share).astype(LOW), ref[:, spot]) for e, ref in zip(exps, kv_refs)
            )
            att_ref[:, mine] = att.astype(LOW)
        results.put(0)
        results.put(1)
        weights = stream.take(4)
        for side in range(2):
            columns = slice(side * wide // 2, (side + 1) * wide // 2)
            total = low_dot(att_ref[:, :q_width], weights[side][...])
            total = total + low_dot(att_ref[:, q_width:], weights[2 + side][...])
            part_ref[:, columns] = total.astype(LOW)
        results.put(2)

    return call(
        body,
        "attend",
        [query, *kvs, *parts],
        [((rows, both), LOW), ((2 * heads, rows), FULL), ((rows, wide), LOW)],
        [],
        16 * heads * rows * rows * len(kvs) * 128 + 2 * rows * both * wide,
        2 * heads * rows * rows * len(kvs),
        (core,),
    )


def attend_back(core, norm_ins, query, lse, kvs, held, parts):
    rows, both = query.shape
    wide = norm_ins[0].shape[1]
    chunks = len(kvs) // 2
    q_width, heads = both // 2, both // 2 // HEAD
    kv_width = q_width // 2
    half = wide // 2
    scale = HEAD ** (-0.5)

    def body(stream, results, core_ref, grad_ref):
        put_norm_back(stream.take(6), results, 0)
        g_ref = results.buffers[1]
        offsets = offsets_of(chunks, core_ref[0])
        for side in range(2):
            first, second = stream.take(2)
            grad = dot_nt(g_ref[:, :half], first[...])
            grad = grad + dot_nt(g_ref[:, half:], second[...])
            grad_ref[:, side * q_width : (side + 1) * q_width] = grad.astype(LOW)
        (q_ref,), (lse_ref,), kv_refs = stream.take(1), stream.take(1), stream.take(2 * chunks)
        held_refs = stream.take(2) if held is not None else None
        dq_ref, out_refs = results.buffers[3], results.buffers[4:]
        for first in range(0, 2 * heads, 2):
            group = (first // heads) * q_width + (first % heads) // 2 * HEAD
            key_spot = slice(group, group + HEAD)
            value_spot = slice(group + kv_width, group + kv_width + HEAD)
            key_sums, value_sums = [0.0] * len(kv_refs), [0.0] * len(kv_refs)
            for h in (first, first + 1):
                mine = slice(h * HEAD, (h + 1) * HEAD)
                query, grad, lse = q_ref[:, mine], grad_ref[:, mine], lse_ref[h : h + 1, :]
                probs = [
                    jnp.exp(score(ref[:, key_spot], query, kind) - (lse + o))
                    for ref, kind, o in zip(kv_refs, kinds_of(chunks), offsets)
                ]
                prob_grads = [dot_nt(ref[:, value_spot], grad) for ref in kv_refs]
                delta = sum(
                    jnp.sum(p * d, axis=0, keepdims=True) for p, d in zip(probs, prob_grads)
                )
                query_grad = 0.0
                for i, (p, d, ref) in enumerate(zip(probs, prob_grads, kv_refs)):
                    score_grad = (p * (d - delta)).astype(LOW)
                    query_grad = query_grad + dot_tn(score_grad, ref[:, key_spot])
                    key_sums[i] = key_sums[i] + low_dot(score_grad, query)
                    value_sums[i] = value_sums[i] + low_dot(p.astype(LOW), grad)
                dq_ref[:, mine] = query_grad * scale
            for i, out_ref in enumerate(out_refs):
                for spot, value in ((key_spot, key_sums[i] * scale), (value_spot, value_sums[i])):
                    if held is not None and i >= 2 * chunks - 2:
                        value = value + held_refs[i - 2 * chunks + 2][:, spot]
                    out_ref[:, spot] = value.astype(out_ref.dtype)
        for i in range(3, 4 + 2 * chunks):
            results.put(i)

    kinds = [FULL] * (2 * chunks) + [LOW]
    return call(
        body,
        "attend_back",
        [*norm_ins, *parts, query, lse, *kvs, *(held or ())],
        norm_back_shapes(rows, wide) + [((rows, both), k) for k in kinds],
        [pltpu.VMEM((rows, both), LOW)],
        40 * heads * rows * rows * len(kvs) * 128 + 2 * rows * both * wide,
        2 * heads * rows * rows * len(kvs),
        (core,),
    )


def project_back(dq, own, came, cosine, sine, parts):
    rows, both = dq.shape
    wide = 2 * parts[0].shape[0]
    q_width, half = both // 2, wide // 2

    def body(stream, results):
        cos_ref, sin_ref, dq_ref, own_ref, came_ref = stream.take(5)
        proj_ref, part_ref = results.buffers
        for side in range(2):
            here = slice(side * q_width, (side + 1) * q_width)
            rest = own_ref[:, here] + came_ref[:, here].astype(FULL)
            flat = jnp.concatenate([dq_ref[:, here], rest], axis=1)
            query, rest = turn(flat, cos_ref[...], -sin_ref[...])
            start = 2 * side * q_width
            proj_ref[:, start : start + q_width] = query.astype(LOW)
            proj_ref[:, start + q_width : start + 2 * q_width] = rest.astype(LOW)
        results.put(0)
        for side in range(2):
            own_w, other_w = stream.take(2)
            total = dot_nt(proj_ref[:, : 2 * q_width], own_w[...])
            total = total + dot_nt(proj_ref[:, 2 * q_width :], other_w[...])
            part_ref[:, side * half : (side + 1) * half] = total.astype(LOW)
        results.put(1)

    return call(
        body,
        "project_back",
        [cosine, sine, dq, own, came, parts[0], parts[2], parts[1], parts[3]],
        [((rows, 2 * both), LOW), ((rows, wide), LOW)],
        [],
        4 * rows * wide * both,
    )


def feed_forward(hidden, pair, gain, pair_parts, down_parts):
    rows, wide = hidden.shape
    ff = down_parts[0].shape[0]
    half = wide // 2

    def body(stream, results):
        refs = stream.take(3)
        (gain_ref,) = stream.take(1)
        put_norm(refs, gain_ref, results, 0)
        tokens = results.buffers[2][...]
        gate_ref, up_ref, inner_ref, part_ref = results.buffers[3:]
        for side in range(2):
            here = slice(side * ff, (side + 1) * ff)
            first, second = stream.take(2)
            gate = half_dots(tokens, first[...], second[...])
            gate_ref[:, here] = gate.astype(LOW)
            gate = gate * jax.nn.sigmoid(gate)
            first, second = stream.take(2)
            up = half_dots(tokens, first[...], second[...])
            up_ref[:, here] = up.astype(LOW)
            inner_ref[:, here] = (gate * up).astype(LOW)
        for i in range(3, 6):
            results.put(i)
        for side in range(2):
            own, other = stream.take(2)
            total = low_dot(inner_ref[:, :ff], own[...])
            total = total + dot_nt(inner_ref[:, ff:], other[...])
            part_ref[:, side * half : (side + 1) * half] = total.astype(LOW)
        results.put(6)

    return call(
        body,
        "feed_forward",
        [hidden, *pair, gain, *pair_parts, *[down_parts[i] for i in (0, 2, 1, 3)]],
        norm_shapes(rows, wide) + [((rows, 2 * ff), LOW)] * 3 + [((rows, wide), LOW)],
        [],
        12 * rows * wide * ff,
        2 * rows * ff,
    )


def feed_back(norm_ins, gate, up, pair_parts, down_parts):
    rows, wide = norm_ins[0].shape
    ff = down_parts[0].shape[0]
    half = wide // 2
    first_layer = len(norm_ins) == 1
    order = (0, 2, 4, 6, 1, 3, 5, 7)
    base = 0 if first_layer else 3

    def body(stream, results):
        ins = stream.take(len(norm_ins))
        if first_layer:
            x_ref = ins[0]
        else:
            put_norm_back(ins, results, 0)
            x_ref = results.buffers[1]
        grad_ref, part_ref = results.buffers[base:]
        gate_ref, up_ref = stream.take(2)
        for side in range(2):
            here = slice(side * ff, (side + 1) * ff)
            first, second = stream.take(2)
            times = low_dot if side else dot_nt
            inner_grad = times(x_ref[:, :half], first[...])
            inner_grad = inner_grad + times(x_ref[:, half:], second[...])
            gate, up = gate_ref[:, here].astype(FULL), up_ref[:, here].astype(FULL)
            sigma = jax.nn.sigmoid(gate)
            grad_sigma = inner_grad * sigma
            start = 2 * side * ff
            grad_ref[:, start : start + ff] = (
                grad_sigma * up * (1.0 + gate * (1.0 - sigma))
            ).astype(LOW)
            grad_ref[:, start + ff : start + 2 * ff] = (grad_sigma * gate).astype(LOW)
        results.put(base)
        for side in range(2):
            total = 0.0
            for i in range(4):
                (weight,) = stream.take(1)
                total = total + dot_nt(grad_ref[:, i * ff : (i + 1) * ff], weight[...])
            part_ref[:, side * half : (side + 1) * half] = total.astype(LOW)
        results.put(base + 1)

    return call(
        body,
        "feed_back",
        [*norm_ins, gate, up, *down_parts, *[pair_parts[i] for i in order]],
        ([] if first_layer else norm_back_shapes(rows, wide))
        + [((rows, 4 * ff), LOW), ((rows, wide), LOW)],
        [],
        12 * rows * wide * ff,
        2 * rows * ff,
    )


def ff_weights_kernel(chunks, split, *refs):
    xb_refs, bb_refs, dg_refs, in_refs = [refs[i * chunks : (i + 1) * chunks] for i in range(4)]
    first_ref, second_ref, turned_ref = refs[4 * chunks :]
    j = pl.program_id(0)
    rows = xb_refs[0].shape[0]
    half = first_ref.shape[0]

    def take(x_refs):
        for i, ref in enumerate(x_refs):
            turned_ref[:, i * rows : (i + 1) * rows] = ref[...].T

    def work(y_refs):
        grads = jnp.concatenate([ref[...] for ref in y_refs], axis=0)
        total = low_dot(turned_ref[...], grads)
        first_ref[...] = total[:half].astype(LOW)
        second_ref[...] = total[half:].astype(LOW)

    @pl.when(j == 0)
    def _():
        take(xb_refs)

    @pl.when(j == split)
    def _():
        take(bb_refs)

    @pl.when(j < split)
    def _():
        work(dg_refs)

    @pl.when(j >= split)
    def _():
        work(in_refs)


def ff_weights(all_b, branch_b, grads, inner):
    chunks = len(all_b)
    rows, wide = all_b[0].shape
    ff = inner[0].shape[1] // 2
    step = min(1024, ff)
    n = ff // step
    split = 4 * n
    full = whole((rows, wide))
    grad = pl.BlockSpec((rows, step), lambda j: (0, jnp.minimum(j, split - 1)))
    last = pl.BlockSpec((rows, step), lambda j: (0, jnp.maximum(j - split, 0)))

    def place(j):
        k = j - split
        early = jnp.where(j < 2 * n, j, j + n)
        late = jnp.where(k < n, 2 * n + k, 4 * n + k)
        return (0, jnp.where(j < split, early, late))

    out = pl.BlockSpec((wide // 2, step), place)
    shape = jax.ShapeDtypeStruct((wide // 2, 6 * ff), LOW)
    return pl.pallas_call(
        functools.partial(ff_weights_kernel, chunks, split),
        grid=(6 * n,),
        in_specs=[full] * (2 * chunks) + [grad] * chunks + [last] * chunks,
        out_specs=[out, out],
        scratch_shapes=[pltpu.VMEM((wide, rows * chunks), LOW)],
        out_shape=[shape, shape],
        compiler_params=limits(),
        cost_estimate=cost(12 * chunks * rows * wide * ff, 12 * wide * ff + 8 * chunks * rows * wide),
        name="ff_weights",
    )(*all_b, *branch_b, *grads, *inner)


def in_weights_kernel(chunks, *refs):
    xa_refs, ba_refs, dp_refs, at_refs = [refs[i * chunks : (i + 1) * chunks] for i in range(4)]
    first_ref, second_ref = refs[4 * chunks :]
    width = dp_refs[0].shape[1] // 2
    q_width = at_refs[0].shape[1] // 2
    half = first_ref.shape[0]
    for x_refs, y_refs, size, base in (
        (xa_refs, dp_refs, width, 0),
        (ba_refs, at_refs, q_width, width),
    ):
        turned = jnp.concatenate([ref[...].T for ref in x_refs], axis=1)
        for side in range(2):
            grads = jnp.concatenate(
                [ref[:, side * size : (side + 1) * size] for ref in y_refs], axis=0
            )
            start = side * (width + q_width) + base
            total = low_dot(turned, grads)
            first_ref[:, start : start + size] = total[:half].astype(LOW)
            second_ref[:, start : start + size] = total[half:].astype(LOW)


def in_weights(all_a, branch_a, grads, attended):
    chunks = len(all_a)
    rows, wide = all_a[0].shape
    width = grads[0].shape[1] + attended[0].shape[1]
    operands = list(all_a) + list(branch_a) + list(grads) + list(attended)
    shape = (wide // 2, width)
    return pl.pallas_call(
        functools.partial(in_weights_kernel, chunks),
        grid=(1,),
        in_specs=[whole(v.shape) for v in operands],
        out_specs=[whole(shape)] * 2,
        out_shape=[jax.ShapeDtypeStruct(shape, LOW)] * 2,
        compiler_params=limits(),
        cost_estimate=cost(
            2 * chunks * rows * wide * width, 2 * wide * width + 4 * chunks * rows * wide
        ),
        name="in_weights",
    )(*operands)


def role_sum_kernel(row_ref, side_ref, left_ref, right_ref, *outs):
    step = pl.program_id(0)
    total = left_ref[...] + right_ref[...]
    for i, out_ref in enumerate(outs):

        @pl.when(step // 2 == i)
        def _(out_ref=out_ref):
            out_ref[...] = total


def role_sums(place, left, right):
    rows, both = left.shape[0] // 4, left.shape[1]
    width = both // 2
    picks = [pick for role in ROLES for pick in role]
    row = place ^ jnp.array([m for m, _ in picks], jnp.int32)
    side = jnp.array([s for _, s in picks], jnp.int32)
    block = pl.BlockSpec((rows, width), lambda i, r, s: (r[i], s[i]))

    def out(k):
        return pl.BlockSpec((rows, width), lambda i, r, s: (jnp.where(i > 2 * k, 1, 0), 0))

    return pl.pallas_call(
        role_sum_kernel,
        grid_spec=pltpu.PrefetchScalarGridSpec(
            num_scalar_prefetch=2,
            grid=(8,),
            in_specs=[block, block],
            out_specs=[out(k) for k in range(4)],
        ),
        out_shape=[jax.ShapeDtypeStruct((2 * rows, width), LOW)] * 4,
        compiler_params=limits(),
        cost_estimate=cost(0, 12 * rows * both),
        name="role_sums",
    )(row, side, left, right)


def cut_kernel(place_ref, gate_ref, up_ref, down_ref, *refs):
    outs, turned_ref = refs[:3], refs[3]
    turned_ref[...] = down_ref[...].T
    outs[0][...] = gate_ref[...]
    outs[1][...] = up_ref[...]
    rows = outs[2].shape[0]
    start = pl.multiple_of(place_ref[0] * rows, rows)
    outs[2][...] = turned_ref[pl.ds(start, rows), :]


def cut_ff(place, layer, gate, up, down):
    wide, ff = gate.shape[1:]
    rows = wide // lax.axis_size("dp")
    block = pl.BlockSpec((None, rows, ff), lambda i, p: (layer, p[0], 0))
    return pl.pallas_call(
        cut_kernel,
        grid_spec=pltpu.PrefetchScalarGridSpec(
            num_scalar_prefetch=1,
            grid=(1,),
            in_specs=[block, block, pl.BlockSpec((None, ff, wide), lambda i, p: (layer, 0, 0))],
            out_specs=[whole((rows, ff))] * 3,
            scratch_shapes=[pltpu.VMEM((wide, ff), LOW)],
        ),
        out_shape=[jax.ShapeDtypeStruct((rows, ff), LOW)] * 3,
        compiler_params=limits(),
        cost_estimate=cost(0, 4 * wide * ff),
        name="cut_ff",
    )(place, gate, up, down)


def cut_in_kernel(place_ref, q_ref, k_ref, v_ref, o_ref, out_ref):
    rows, q_width = q_ref.shape
    kv_width = k_ref.shape[1]
    out_ref[:rows, :q_width] = q_ref[...]
    out_ref[:rows, q_width : q_width + kv_width] = k_ref[...]
    out_ref[:rows, q_width + kv_width :] = v_ref[...]
    out_ref[rows:, :] = o_ref[...]


def cut_in(place, layer, query, key, value, out):
    count = lax.axis_size("dp")
    blocks = [(v.shape[1] // count, v.shape[2]) for v in (query, key, value, out)]
    shape = (blocks[0][0] + blocks[3][0], blocks[3][1])
    return pl.pallas_call(
        cut_in_kernel,
        grid_spec=pltpu.PrefetchScalarGridSpec(
            num_scalar_prefetch=1,
            grid=(1,),
            in_specs=[pl.BlockSpec((None,) + b, lambda i, p: (layer, p[0], 0)) for b in blocks],
            out_specs=whole(shape),
        ),
        out_shape=jax.ShapeDtypeStruct(shape, LOW),
        compiler_params=limits(),
        cost_estimate=cost(0, 4 * shape[0] * shape[1]),
        name="cut_in",
    )(place, query, key, value, out)


def pick_kernel(hi_ref, block_ref, mine_ref, other_ref):
    first, second = block_ref[:, 0, :], block_ref[:, 1, :]
    mine_ref[...] = jnp.where(hi_ref[0] == 0, first, second)
    other_ref[...] = jnp.where(hi_ref[0] == 0, second, first)


def pick(hi, block):
    rows, _, width = block.shape
    return pl.pallas_call(
        pick_kernel,
        grid_spec=pltpu.PrefetchScalarGridSpec(
            num_scalar_prefetch=1,
            grid=(1,),
            in_specs=[whole(block.shape)],
            out_specs=[whole((rows, width))] * 2,
        ),
        out_shape=[jax.ShapeDtypeStruct((rows, width), LOW)] * 2,
        compiler_params=limits(),
        cost_estimate=cost(0, 8 * rows * width),
        name="pick",
    )(hi.astype(jnp.int32).reshape(1), block)


def spread_ff_kernel(spots, place_ref, *refs):
    count = len(spots)
    gate_refs, up_refs, down_refs = [refs[i * count : (i + 1) * count] for i in range(3)]
    outs, held_ref = refs[-4:-1], refs[-1]
    put_parts(place_ref, gate_refs, spots, outs[0].at[0])
    put_parts(place_ref, up_refs, spots, outs[1].at[0])
    put_parts(place_ref, down_refs, spots, held_ref)
    outs[2][0] = held_ref[...].T


def flatten(pieces):
    parts, spots = [], []
    for m, piece in enumerate(pieces):
        piece = piece if isinstance(piece, tuple) else (piece,)
        for i, part in enumerate(piece):
            if not isinstance(part, tuple):
                part = (part, 0, part.shape[0])
            parts.append((part[0], part[1] // part[2], part[2]))
            spots.append((m, i, len(piece)))
    return (parts, spots)


def put_parts(place_ref, refs, spots, out_ref):
    for ref, (m, i, count) in zip(refs, spots):
        rows = ref.shape[0]
        start = 0
        if len(spots) > 1:
            start = pl.multiple_of((place_ref[0] ^ m) * (rows * count) + i * rows, rows)
        out_ref[pl.ds(start, rows), :] = ref[...].astype(FULL)


def spread_ff(place, pieces, layer, earlier):
    pieces, spots = flatten(pieces)
    count = len(pieces)
    rows, wide = pieces[0][2], pieces[0][0].shape[1]
    ff = wide // 3
    step = min(256, ff)
    steps = ff // step
    tall = rows * count

    def block(k, at):
        return pl.BlockSpec((rows, step), lambda j, p: (at, j + k * steps))

    in_specs = [block(k, at) for k in range(3) for _, at, _ in pieces]
    operands = [array for array, _, _ in pieces] * 3
    aliases = {}
    if earlier is not None:
        aliases = {1 + len(operands) + i: i for i in range(3)}
        in_specs += [pl.BlockSpec(memory_space=pl.ANY)] * 3
        operands += list(earlier)

    def kernel(place_ref, *refs):
        refs = refs[: 3 * count] + refs[len(operands) :]
        spread_ff_kernel(spots, place_ref, *refs)

    tall_out = pl.BlockSpec((1, tall, step), lambda j, p: (layer, 0, j))
    flat_out = pl.BlockSpec((1, step, tall), lambda j, p: (layer, j, 0))
    return pl.pallas_call(
        kernel,
        grid_spec=pltpu.PrefetchScalarGridSpec(
            num_scalar_prefetch=1,
            grid=(steps,),
            in_specs=in_specs,
            out_specs=[tall_out, tall_out, flat_out],
            scratch_shapes=[pltpu.VMEM((tall, step), FULL)],
        ),
        out_shape=[
            jax.ShapeDtypeStruct((LAYERS, tall, ff), FULL),
            jax.ShapeDtypeStruct((LAYERS, tall, ff), FULL),
            jax.ShapeDtypeStruct((LAYERS, ff, tall), FULL),
        ],
        input_output_aliases=aliases,
        compiler_params=limits(),
        cost_estimate=cost(0, 18 * tall * ff),
        name="spread_ff",
    )(place, *operands)


def spread_in(place, pieces, layer, earlier, q_width):
    pieces, spots = flatten(pieces)
    count = len(pieces)
    rows, width = pieces[0][2], pieces[0][0].shape[1]
    tall = rows * count
    kv_width = q_width // 2
    operands = [array for array, _, _ in pieces]
    in_specs = [pl.BlockSpec((rows, width), lambda j, p, at=at: (at, 0)) for _, at, _ in pieces]
    aliases = {}
    if earlier is not None:
        aliases = {1 + count + i: i for i in range(4)}
        in_specs = in_specs + [pl.BlockSpec(memory_space=pl.ANY)] * 4
        operands += list(earlier)

    def kernel(place_ref, *refs):
        piece_refs, (q_ref, k_ref, v_ref, o_ref, held_ref) = refs[:count], refs[len(operands) :]
        put_parts(place_ref, piece_refs, spots, held_ref)
        at = 0
        for out_ref, size in ((q_ref, q_width), (k_ref, kv_width), (v_ref, kv_width)):
            out_ref[0] = held_ref[:, at : at + size]
            at += size
        o_ref[0] = held_ref[:, at:].T

    sizes = [(tall, q_width), (tall, kv_width), (tall, kv_width), (q_width, tall)]
    return pl.pallas_call(
        kernel,
        grid_spec=pltpu.PrefetchScalarGridSpec(
            num_scalar_prefetch=1,
            grid=(1,),
            in_specs=in_specs,
            out_specs=[pl.BlockSpec((1,) + s, lambda j, p: (layer, 0, 0)) for s in sizes],
            scratch_shapes=[pltpu.VMEM((tall, width), FULL)],
        ),
        out_shape=[jax.ShapeDtypeStruct((LAYERS,) + s, FULL) for s in sizes],
        input_output_aliases=aliases,
        compiler_params=limits(),
        cost_estimate=cost(0, 6 * tall * width),
        name="spread_in",
    )(place, *operands)


def gather_kernel(count, tops, place_ref, *refs):
    piece_refs, out_ref = refs[:count], refs[count]
    for m, ref in enumerate(piece_refs):
        row, part_row = 0, 0
        for size in tops:
            part = size // count
            start = pl.multiple_of(row + (place_ref[0] ^ m) * part, part)
            out_ref[pl.ds(start, part), :] = ref[part_row : part_row + part, :]
            row += size
            part_row += part


def gather_pieces(place, pieces, tops):
    count = len(pieces)
    shape = (sum(tops), pieces[0].shape[1])
    return pl.pallas_call(
        functools.partial(gather_kernel, count, tops),
        grid_spec=pltpu.PrefetchScalarGridSpec(
            num_scalar_prefetch=1,
            grid=(1,),
            in_specs=[whole(p.shape) for p in pieces],
            out_specs=whole(shape),
        ),
        out_shape=jax.ShapeDtypeStruct(shape, LOW),
        compiler_params=limits(),
        cost_estimate=cost(0, 4 * shape[0] * shape[1]),
        name="gather_pieces",
    )(place, *pieces)


def cut(weight, layer, place):
    rows = weight.shape[1] // lax.axis_size("dp")
    start = (jnp.int32(layer), place * rows, jnp.int32(0))
    return lax.dynamic_slice(weight, start, (1, rows, weight.shape[2]))[0]


class Group:
    def __init__(self, piece, tops, place):
        self.piece, self.tops, self.place = piece, tops, place
        self.count = lax.axis_size("dp")
        self.even = all(size // self.count % 16 == 0 for size in tops)

    def fetch(self, order):
        self.piece = flip_hi(order.after(self.piece))

    def gather(self, order):
        order.join(self.piece)
        piece = order.after(self.piece)
        if len(self.tops) == 1:
            self.first = lax.all_gather(piece, "dp", axis=0, tiled=True)
            return
        pieces = lax.all_gather(piece, "dp", axis=0)
        at, rows = 0, []
        for size in self.tops:
            part = size // self.count
            rows.append(pieces[:, at : at + part].reshape(size, -1))
            at += part
        self.first = jnp.concatenate(rows, axis=0)

    def cross(self, order, gated=False):
        first = order.after(self.first) if gated else self.first
        self.halves = (first, flip_core(first))

    def spread(self, order, near=(1, 2)):
        order.join(self.piece)
        if self.even:
            piece = order.after(self.piece)
            self.pieces = [piece] + [hop(piece, "dp", m) for m in near]
        else:
            self.gather(order)

    def spread_on(self, order):
        if self.even:
            order.join(*self.pieces[1:])
            piece = order.after(self.pieces[0])
            self.pieces += [hop(piece, "dp", m) for m in range(len(self.pieces), self.count)]

    def collect(self, order):
        if self.even:
            spot = self.place.astype(jnp.int32).reshape(1)
            order.join(*self.pieces[1:])
            pieces = [order.after(self.pieces[0])] + self.pieces[1:]
            self.first = gather_pieces(spot, pieces, self.tops)
        order.mark(self.first)
        self.halves = (self.first, flip_core(self.first))

    def done(self, order):
        order.join(self.halves[1])


def in_groups(layer, w_query, w_key, w_value, w_out, place):
    wide, q_width = w_query.shape[1:]
    width = q_width + 2 * w_key.shape[2]
    count = lax.axis_size("dp")
    if width == w_out.shape[2] and q_width // count % 16 == 0:
        spot = place.astype(jnp.int32).reshape(1)
        piece = cut_in(spot, layer, w_query, w_key, w_value, w_out)
        return [Group(piece, (wide, q_width), place)]
    piece = jnp.concatenate([cut(v, layer, place) for v in (w_query, w_key, w_value)], axis=1)
    return [Group(piece, (wide,), place), Group(cut(w_out, layer, place), (q_width,), place)]


ROLES = (((1, 0), (3, 0)), ((2, 1), (3, 1)), ((2, 0), (1, 1)), ((0, 0), (0, 1)))


class Sum:
    def __init__(self, parts, place, by_hops):
        self.first, self.last = parts
        self.place = place
        self.even = by_hops and lax.axis_size("dp") == 4

    def flip(self, order):
        self.came = flip_core(order.after(self.last))

    def start(self, order):
        order.join(self.came)
        if not self.even:
            total = order.mark(add_low(order.after(self.first), self.came))
            self.both = lax.psum_scatter(total, "dp", scatter_dimension=0, tiled=True)
            return
        spot = self.place.astype(jnp.int32).reshape(1)
        roles = role_sums(spot, order.after(self.first), self.came)
        to_x, to_y, self.on, self.keep = order.mark(roles)
        self.from_x, self.from_y = hop(to_x, "dp", 1), hop(to_y, "dp", 2)

    def second(self, order):
        if not self.even:
            return
        rows = self.on.shape[0] // 2
        on, keep, from_x, from_y = order.after((self.on, self.keep, self.from_x, self.from_y))
        to_y = add_low(on[:rows], from_x[rows:])
        to_x = add_low(on[rows:], from_y[rows:])
        self.own = add_low(keep[:rows], from_x[:rows])
        self.other = add_low(keep[rows:], from_y[:rows])
        order.mark((to_x, to_y))
        self.to_own, self.to_other = hop(to_y, "dp", 2), hop(to_x, "dp", 1)

    def third(self, order):
        if not self.even:
            both = order.after(self.both)
            width = both.shape[1] // 2
            self.own, self.other = order.mark((both[:, :width], both[:, width:]))
            return
        order.join(self.to_own)
        other, came = order.after((self.other, self.to_other))
        self.other = order.mark(add_low(other, came))

    def across(self, order):
        self.far = flip_hi(order.after(self.other))

    def fourth(self, order):
        own, far = order.after((self.own, self.far))
        total = own.astype(FULL) + far.astype(FULL)
        if self.even:
            total = total + order.after(self.to_own).astype(FULL)
        self.total = order.mark(total.astype(LOW))

    def gather(self, order):
        total = order.after(self.total)
        self.pieces = [lax.all_gather(total, "dp", axis=0, tiled=True)]

    def straight(self, order):
        total = order.after(self.total)
        self.pieces = [total] + [hop(total, "dp", m) for m in range(1, lax.axis_size("dp"))]

    def near(self, order):
        if not self.even:
            self.gather(order)
            return
        total = order.after(self.total)
        rows = total.shape[0] // 2
        self.mine = (total[:rows], total[rows:])
        self.beside = [hop(self.mine[0], "dp", 1), hop(self.mine[1], "dp", 2)]

    def fifth(self, order):
        if not self.even:
            return
        top, bottom = self.mine
        order.join(*self.beside)
        near_x, near_y = order.after(tuple(self.beside))
        tops = order.mark(jnp.concatenate([top, near_x], axis=0))
        bottoms = order.mark(jnp.concatenate([bottom, near_y], axis=0))
        tops, bottoms = hop(tops, "dp", 2), hop(bottoms, "dp", 1)
        rows = top.shape[0]
        self.pieces = [
            (top, bottom),
            (near_x, (bottoms, 0, rows)),
            ((tops, 0, rows), near_y),
            ((tops, rows, rows), (bottoms, rows, rows)),
        ]

    def done(self, order):
        order.join(*(part for piece in self.pieces if isinstance(piece, tuple) for part in piece))


def rope_tables(positions, width):
    indices = jnp.arange(HEAD // 2, dtype=FULL)
    inverse = ROPE_BASE ** (-2.0 * indices / HEAD)
    angles = positions.astype(FULL)[:, None] * inverse[None, :]
    cosine, sine = jnp.cos(angles), jnp.sin(angles)
    heads = width // HEAD
    return (
        jnp.concatenate([cosine, cosine] * heads, axis=1),
        jnp.concatenate([-sine, sine] * heads, axis=1),
    )


def finish_back(grad, left, right, hidden, factor, gain):
    unit = hidden * factor
    grad_normed = left.astype(FULL) + right.astype(FULL)
    grad_unit = grad_normed * gain
    inner = jnp.mean(grad_unit * unit, axis=-1, keepdims=True)
    return (
        grad + factor * (grad_unit - unit * inner),
        jnp.sum(grad_normed * unit, axis=0, keepdims=True),
    )


class Arrival:
    def __init__(self, block, hi, lo, core):
        self.block, self.hi, self.lo, self.core = block, hi, lo, core

    def pick(self, order):
        self.mine, self.other = order.mark(pick(self.hi, order.after(self.block)))

    def fetch_on(self, order):
        self.far = flip_hi(order.after(self.other))

    def fetch(self, order):
        self.pick(order)
        self.fetch_on(order)

    def share(self, order):
        order.join(self.far)
        mine, far = order.after((self.mine, self.far))
        self.parts = [jnp.where(self.hi == j, mine, far) for j in range(CHUNKS)]
        order.mark(tuple(self.parts))
        self.halves = [None] * CHUNKS
        self.near = [None] * CHUNKS

    def send(self, order, j):
        self.near[j] = hop(order.after(self.parts[j]), "cols", 1)

    def cross(self, order, j):
        lo, core = self.lo, self.core
        order.join(self.near[j])
        part, near = order.after((self.parts[j], self.near[j]))
        if len(low_bits()) == 1:
            at_home = lo == core
            first = jnp.where(at_home, part, near)
            second = jnp.where(at_home, near, part)
        else:
            for bit in low_bits():
                far = near if bit == 1 else hop(part, "cols", bit)
                part = jnp.where(
                    (lo & bit) == 0,
                    jnp.concatenate([part, far], axis=0),
                    jnp.concatenate([far, part], axis=0),
                )
            half = part.shape[0] // 2
            first = lax.dynamic_slice_in_dim(part, core * half, half, 0)
            second = lax.dynamic_slice_in_dim(part, (1 - core) * half, half, 0)
        first, second = order.mark((first, second))
        self.halves[j] = (first, flip_core(second))

    def chunk(self, order, j):
        order.join(self.halves[j][1])
        return order.mark(jnp.concatenate(order.after(self.halves[j]), axis=-1))


class Departure:
    def __init__(self, results, hi, lo, core, rows):
        self.results, self.hi, self.lo, self.core, self.rows = results, hi, lo, core, rows

    def cross(self, order):
        flat = order.after([chunk for chunks in self.results for chunk in chunks])
        half = flat[0].shape[1] // 2
        self.firsts = [chunk[:, :half] for chunk in flat]
        send = jnp.concatenate([chunk[:, half:].astype(LOW) for chunk in flat], axis=0)
        self.came = flip_core(order.mark(send))

    def away(self, order):
        came = order.after(self.came)
        size = self.firsts[0].shape[0]
        parts = []
        for i, first in enumerate(self.firsts):
            second = came[i * size : (i + 1) * size].astype(FULL)
            both = jnp.where(
                self.core == 0,
                jnp.concatenate([first, second], axis=0),
                jnp.concatenate([second, first], axis=0),
            )
            parts.append(lax.dynamic_slice_in_dim(both, self.lo * self.rows, self.rows, 0))
        pairs = list(zip(parts[0::2], parts[1::2]))
        self.mine = [jnp.where(self.hi == 0, a, b) for a, b in pairs]
        others = [jnp.where(self.hi == 0, b, a).astype(LOW) for a, b in pairs]
        self.mine, send = order.mark((self.mine, jnp.concatenate(others, axis=0)))
        self.far = flip_hi(send)

    def done(self, order):
        far = order.after(self.far)
        out = []
        for i, mine in enumerate(self.mine):
            other = far[i * self.rows : (i + 1) * self.rows].astype(FULL)
            out.append(
                jnp.where(
                    self.hi == 0, jnp.stack([mine, other], axis=1), jnp.stack([other, mine], axis=1)
                )
            )
        return out


def shards(
    block_input, block_cotangent, w_query, w_key, w_value, w_out, w_gate, w_up, w_down, norm_gains
):
    low_count = lax.axis_size("cols") // 2
    core, col, place = lax.axis_index("rows"), lax.axis_index("cols"), lax.axis_index("dp")
    hi, lo = col // low_count, col % low_count
    core_ref = core.astype(jnp.int32).reshape(1)
    block_rows = block_input.shape[0]
    rows = block_rows * low_count
    q_width = w_query.shape[2]
    half = rows // 2
    tables = [
        rope_tables(jnp.arange(half, dtype=jnp.int32) + j * rows + core * half, q_width)
        for j in range(CHUNKS)
    ]
    spot = place.astype(jnp.int32).reshape(1)
    order = Order()
    w_in = jnp.concatenate([w_query, w_key, w_value], axis=2)
    wide = w_in.shape[1]
    ff = w_gate.shape[2]
    arrival = Arrival(block_input, hi, lo, core)
    arrival.fetch(order)
    a_groups = [in_groups(0, order.after(w_query), w_key, w_value, w_out, place), None]
    order.mark([group.piece for group in a_groups[0]])
    for group in a_groups[0]:
        group.fetch(order)
    in_own, out_own, gates, ups, own_downs = [
        (v, flip_core(v)) for v in (w_in, w_out, w_gate, w_up, w_down)
    ]
    gains = jnp.concatenate([norm_gains, flip_core(norm_gains)], axis=-1)
    f_groups = []
    for l in range(LAYERS):
        pieces = order.mark(cut_ff(spot, l, order.after(w_gate), w_up, w_down))
        f_groups.append([Group(piece, (wide,), place) for piece in pieces])
        order.join(*((in_own[1], gains) if not l else (out_own[1],)))
    a_groups[1] = in_groups(1, order.after(w_query), w_key, w_value, w_out, place)
    order.mark([group.piece for group in a_groups[1]])
    order.join(gates[1], ups[1])
    cotangent = Arrival(block_cotangent, hi, lo, core)
    cotangent.pick(order)
    arrival.share(order)
    for group in a_groups[0]:
        group.spread(order)
    arrival.send(order, 0)
    f_groups[0][0].fetch(order)
    for group in a_groups[0]:
        group.spread_on(order)
    arrival.cross(order, 0)
    f_groups[0][0].gather(order)
    f_groups[0][1].fetch(order)
    for group in a_groups[0]:
        group.collect(order)
    hidden = [arrival.chunk(order, 0)]
    order.join(own_downs[1])
    arrival.send(order, 1)
    f_groups[0][1].gather(order)
    for group in a_groups[0]:
        group.done(order)

    stash = [[None] * CHUNKS for _ in range(LAYERS)]
    weights = [None] * LAYERS
    pairs = [None] * CHUNKS

    def front(l, j):
        block, factor_a, normed_a, query, mine = order.mark(
            project(order.after(hidden[j]), pairs[j], gains[l, 0:1], ins, *tables[j])
        )
        kvs.extend([mine, flip_core(mine)])
        return (block, factor_a, normed_a, query)

    def middle(l, j, kept):
        order.join(kvs[2 * j + 1])
        attended, lse, part = order.mark(
            attend(core_ref, order.after(kept[3]), kvs[: 2 * j + 2], outs)
        )
        pairs[j] = group_pair(part)
        return (*kept, kvs[: 2 * j + 2], lse, attended)

    def rear(l, j, kept):
        order.join(pairs[j])
        mixed, factor_b, normed_b, gate, up, inner, part = order.mark(
            feed_forward(order.after(kept[0]), pairs[j], gains[l, 1:2], pair_parts, down_parts)
        )
        hidden[j] = mixed
        pairs[j] = group_pair(part) if l + 1 < LAYERS else part
        stash[l][j] = kept + (mixed, factor_b, normed_b, gate, up, inner)

    for l in range(LAYERS):
        more = l + 1 < LAYERS
        halves = [group.halves for group in a_groups[l]]
        if len(halves) == 1:
            ins = [Part(v, None, 0, wide) for v in halves[0]]
            outs = [Part(v, None, wide, w_out.shape[1]) for v in halves[0]]
        else:
            ins, outs = [[Part(v) for v in pair] for pair in halves]
        ins = [Part(v, l) for v in in_own] + ins
        outs = [Part(v, l) for v in out_own] + outs
        kvs, kept = [], [None] * CHUNKS
        first, second, third = f_groups[l]
        if not l:
            third.fetch(order)
            kept[0] = front(l, 0)
            arrival.cross(order, 1)
            hidden.append(arrival.chunk(order, 1))
            kept[1] = front(l, 1)
            kept[0] = middle(l, 0, kept[0])
            kept[1] = middle(l, 1, kept[1])
            third.spread(order, range(1, lax.axis_size("dp")))
            order.join(pairs[0])
            for group in a_groups[1]:
                group.fetch(order)
            order.join(pairs[1])
            first.cross(order)
            for group in a_groups[1]:
                order.join(group.piece)
            third.collect(order)
            for group in a_groups[1]:
                group.gather(order)
            f_groups[1][0].fetch(order)
            second.cross(order)
            first.done(order)
        else:
            order.join(pairs[0])
            kept[0] = front(l, 0)
            second.gather(order)
            third.fetch(order)
            order.join(pairs[1])
            kept[1] = front(l, 1)
            kept[0] = middle(l, 0, kept[0])
            third.spread(order, range(1, lax.axis_size("dp")))
            cotangent.fetch_on(order)
            kept[1] = middle(l, 1, kept[1])
            order.join(pairs[0], cotangent.far)
            first.cross(order, True)
            third.collect(order)
            second.cross(order)
            first.done(order)
        second.done(order)
        third.done(order)
        packs = [group.halves for group in f_groups[l]]
        pair_parts = [Part(v, l) for v in (*gates, *ups)] + [
            Part(v) for pack in packs[:2] for v in pack
        ]
        down_parts = [Part(v, l) for v in own_downs] + [Part(v) for v in packs[2]]
        weights[l] = (ins, outs, pair_parts, down_parts)
        rear(l, 0, kept[0])
        if not more:
            cotangent.share(order)
            cotangent.send(order, 1)
            cotangent.send(order, 0)
        order.join(pairs[1])
        rear(l, 1, kept[1])
        if not more:
            cotangent.cross(order, 1)
        if more:
            f_groups[1][0].gather(order)
            f_groups[1][1].fetch(order)
            order.join(pairs[0])
            for group in a_groups[1]:
                group.cross(order, True)
                group.done(order)
    grads = [None] * CHUNKS
    grads[1] = (cotangent.chunk(order, 1),)

    gain_a, gain_b = [0.0] * LAYERS, [0.0] * LAYERS
    sums = {}

    def ff_step(l, j):
        pair_parts, down_parts = weights[l][2:]
        gate, up, inner = stash[l][j][-3:]
        if len(grads[j]) == 1:
            branch_b = order.after(grads[j][0])
            grad_hidden = branch_b.astype(FULL)
            pair_grad, part = order.mark(feed_back((branch_b,), gate, up, pair_parts, down_parts))
        else:
            order.join(*grads[j][1:3])
            grad_hidden, branch_b, gain_part, pair_grad, part = order.mark(
                feed_back(
                    (order.after(grads[j][0]), *grads[j][1:]), gate, up, pair_parts, down_parts
                )
            )
            gain_a[l + 1] = gain_a[l + 1] + gain_part
        mixed, factor_b, normed_b = stash[l][j][7:10]
        grads[j] = (grad_hidden, *group_pair(part), mixed, factor_b, gains[l, 1:2])
        return (normed_b, branch_b, pair_grad, inner)

    def ff_grad(l, kept):
        columns = list(zip(*kept))
        columns[0] = order.after(columns[0])
        sums["ff", l] = Sum(order.mark(ff_weights(*columns)), place, l == 0)

    def attend_step(l, j, held):
        block, factor_a, normed_a, query, kvs, lse, attended = stash[l][j][:7]
        order.join(*grads[j][1:3])
        grad_mixed, branch_a, gain_part, dq, *dkvs = order.mark(
            attend_back(
                core_ref,
                (order.after(grads[j][0]), *grads[j][1:]),
                query,
                lse,
                kvs,
                held,
                weights[l][1],
            )
        )
        gain_b[l] = gain_b[l] + gain_part
        grads[j] = (grad_mixed, None, None, block, factor_a, gains[l, 0:1])
        middle = (dq, dkvs[-2], flip_core(dkvs[-1]))
        return (dkvs[:2], middle, (normed_a, branch_a, None, attended))

    def project_step(l, j, middle, kept):
        dq, mine, came = middle
        order.join(came)
        proj_grad, part = order.mark(
            project_back(order.after(dq), mine, came, *tables[j], weights[l][0])
        )
        pair = group_pair(part) if l else last_pair(part)
        grads[j] = (grads[j][0], *pair, *grads[j][3:])
        return kept[:2] + (proj_grad,) + kept[3:]

    def in_grad(l, kept):
        columns = list(zip(*kept))
        columns[0] = order.after(columns[0])
        sums["in", l] = Sum(order.mark(in_weights(*columns)), place, l == 0)

    l = LAYERS - 1
    kept, mids = [None] * CHUNKS, [None] * CHUNKS
    kept[1] = ff_step(l, 1)
    cotangent.cross(order, 0)
    grads[0] = (cotangent.chunk(order, 0),)
    kept[0] = ff_step(l, 0)
    ff_grad(l, kept)
    sums["ff", l].flip(order)
    held, mids[1], kept[1] = attend_step(l, 1, None)
    sums["ff", l].start(order)
    order.join(mids[1][2])
    _, mids[0], kept[0] = attend_step(l, 0, held)
    kept[1] = project_step(l, 1, mids[1], kept[1])
    kept[0] = project_step(l, 0, mids[0], kept[0])
    in_grad(l, kept)
    l = 0
    kept, mids = [None] * CHUNKS, [None] * CHUNKS
    kept[1] = ff_step(l, 1)
    kept[0] = ff_step(l, 0)
    sums["in", 1].flip(order)
    ff_grad(l, kept)
    sums["ff", 1].third(order)
    sums["ff", 1].across(order)
    sums["in", 1].start(order)
    sums["ff", 0].flip(order)
    held, mids[1], kept[1] = attend_step(l, 1, None)
    sums["ff", 0].start(order)
    _, mids[0], kept[0] = attend_step(l, 0, held)
    kept[1] = project_step(l, 1, mids[1], kept[1])
    kept[0] = project_step(l, 0, mids[0], kept[0])
    sums["in", 1].third(order)
    in_grad(l, kept)
    sums["ff", 1].fourth(order)
    sums["ff", 1].gather(order)
    for g in reversed(grads):
        order.join(*g[1:3])
    ends = [finish_back(order.after(g[0]), *g[1:]) for g in grads]
    order.mark(tuple(g for g, _ in ends))
    gain_a[0] = sum(part for _, part in ends)
    if len(low_bits()) == 1:
        gain_a[0] = jnp.where(lo == core, gain_a[0], 0.0)
        gain_a[0] = gain_a[0] + hop(gain_a[0], "cols", 1)
    gain_grads = [jnp.concatenate([gain_a[l], gain_b[l]], axis=0) for l in range(LAYERS)]
    grad_gains = order.after(jnp.stack(gain_grads))
    width = grad_gains.shape[-1] // 2
    gains_came = flip_core(grad_gains[..., width:])
    sums["ff", 0].second(order)
    sums["in", 0].flip(order)
    sums["in", 1].across(order)
    grad_gains = order.mark(grad_gains[..., :width] + order.after(gains_came))
    gains_came = flip_hi(grad_gains)
    sums["in", 0].start(order)
    sums["in", 1].fourth(order)
    grad_gains = order.mark(grad_gains + order.after(gains_came))
    sums["ff", 0].third(order)
    sums["ff", 0].across(order)
    tops = [last_pair(part) for part in order.after(pairs)]
    sums["in", 1].gather(order)
    sums["in", 0].second(order)
    order.join(tops)
    hidden = [
        h + left.astype(FULL) + right.astype(FULL)
        for h, (left, right) in order.after(list(zip(hidden, tops)))
    ]
    results = Departure((hidden, [g for g, _ in ends]), hi, lo, core, block_rows)
    results.cross(order)
    gains_came = hop(order.after(grad_gains), "dp", 1)
    sums["ff", 0].fourth(order)
    sums["ff", 0].near(order)
    sums["in", 0].third(order)
    sums["in", 0].across(order)
    ff_out = order.mark(spread_ff(order.after(spot), sums["ff", 1].pieces, 1, None))
    bit = 1
    while 2 * bit < lax.axis_size("dp"):
        grad_gains = order.mark(grad_gains + order.after(gains_came))
        bit *= 2
        gains_came = hop(grad_gains, "dp", bit)
        if bit == 2:
            sums["ff", 0].fifth(order)
    sums["in", 0].fourth(order)
    sums["in", 0].straight(order)
    results.away(order)
    in_out = order.mark(spread_in(order.after(spot), sums["in", 1].pieces, 1, None, q_width))
    sums["ff", 0].done(order)
    ff_out = order.mark(spread_ff(order.after(spot), sums["ff", 0].pieces, 0, ff_out))
    in_out = order.mark(spread_in(order.after(spot), sums["in", 0].pieces, 0, in_out, q_width))
    grad_gains = grad_gains + order.after(gains_came)
    activations, input_grad = results.done(order)
    return (activations, input_grad, *in_out, *ff_out, grad_gains)


def solution(mesh):
    data = P("cols", "dp", "rows")
    tall = P(None, "rows", "cols")
    flat = P(None, "cols", "rows")
    gains = P(None, None, "rows")
    in_specs = (data, data, tall, tall, tall, flat, tall, tall, flat, gains)
    out_specs = (data, data, tall, tall, tall, flat, tall, tall, flat, gains)
    return jax.shard_map(
        shards, mesh=mesh, in_specs=in_specs, out_specs=out_specs, check_vma=False
    )
```
